32 devices in a mesh: dp: 16 (over z, y, x), mp: 2 (over core).
Axes of the slice: x: 2, y: 2, z: 4, core: 2. Of those that a mesh axis runs over, the one named last changes fastest.
Arguments:
- tokens: bfloat16 [8192, 768], P('dp'), may hold values from -6 to 6
- cell_ids: int32 [16, 512], P('dp'), may hold values from 0 to 7, never falling along the last dimension, each value on 1 to 256 neighbouring positions
- gene_range: int32 [8192, 1], P('dp'), may hold values from 0 to 15; in each aligned block of 512 rows (0 to 511, 512 to 1023, ...) at most 64 rows name the same one
- gene_offset: int32 [8192], P('dp'), may hold values from 0 to 151
- gain1: float32 [768], replicated, may hold values from 0.1 to 1.9
- shift1: float32 [768], replicated, may hold values from -4 to 4
- w_qkv: bfloat16 [3, 768, 768], P(None, None, 'mp'), may hold values from -0.21875 to 0.21875
- w_out: bfloat16 [768, 768], P('mp'), may hold values from -2.5 to 2.5
- out_bias: float32 [768], replicated, may hold values from -4 to 4
- gain2: float32 [768], replicated, may hold values from 0.1 to 1.9
- shift2: float32 [768], replicated, may hold values from -4 to 4
- w_up: bfloat16 [768, 3072], P(None, 'mp'), may hold values from -0.21875 to 0.21875
- up_bias: float32 [3072], P('mp'), may hold values from -6 to 6
- w_down: bfloat16 [3072, 768], P('mp'), may hold values from -0.109375 to 0.109375
- down_bias: float32 [768], replicated, may hold values from -4 to 4
- w_proj: bfloat16 [768, 512], P(None, 'mp'), may hold values from -0.21875 to 0.21875
- zero_embed: bfloat16 [2432, 512], P('dp', 'mp'), may hold values from -6 to 6
- dense_cot: bfloat16 [2432, 512], P('dp', 'mp'), may hold values from -6 to 6
Outputs:
- block_out: bfloat16 [8192, 768], P('dp')
- dense: float32 [2432, 512], P('dp', 'mp')
- grad_tokens: float32 [8192, 768], P('dp')
- grad_zero: float32 [2432, 512], P('dp', 'mp')
- grad_qkv: float32 [3, 768, 768], P(None, 'dp', 'mp')
- grad_wout: float32 [768, 768], P('mp', 'dp')
- grad_up: float32 [768, 3072], P('dp', 'mp')
- grad_down: float32 [3072, 768], P('mp', 'dp')
- grad_proj: float32 [768, 512], P('dp', 'mp')
- grad_gain1: float32 [768], replicated
- grad_shift1: float32 [768], replicated
- grad_out_bias: float32 [768], replicated
- grad_gain2: float32 [768], replicated
- grad_shift2: float32 [768], replicated
- grad_up_bias: float32 [3072], P('mp')
- grad_down_bias: float32 [768], replicated
The draws below stay inside these ranges and needn't reach their ends.
Inputs may be any that keep to these rules, and one draw needn't show every extreme that they name: `gene_range`: among the 512 rows of one device no owner appears more than 64 times. `cell_ids`: cell numbers never fall along a row; a cell spans at most 256 tokens.
All inputs are finite; a program needn't handle non-finite values.
Results may differ from the reference program's by a relative error of at most 0.012.
The reference program's roundings to bfloat16 on the way count: a program that leaves them out, or rounds other values in their place, can miss the bound.
Values may be sent and summed in bfloat16 or wider, within the bound.
No kernel may reach another device: no remote copies, remote signals or barrier semaphores. Data moves between devices by JAX's collectives and lax.ppermute only.
A program may use at most 128 MiB of HBM per device.

```python
import math
import jax
import jax.numpy as jnp
import numpy as np
from jax import lax

D = 768
HEADS = 12
HEAD_DIM = 64
FF = 3072
PD = 512
GENE_DEV = 152
TOK_DEV = 512
CELLS = 8
CELL_MOST = 256
TOKENS = 8192
GENES = 2432
CAP = 64
N_DP = 16


def set_ends(array, key, smallest, top_value):
    spot = [jax.random.randint(jax.random.fold_in(key, axis), (), 0, length) for axis, length in enumerate(array.shape)]
    longest = array.shape.index(max(array.shape))
    next_to = spot[:longest] + [(spot[longest] + 1) % array.shape[longest]] + spot[longest + 1:]
    return array.at[tuple(spot)].set(smallest).at[tuple(next_to)].set(top_value)


def block_scale(rng, shape, shards, low, high):
    level, own = 1.0, jax.random.fold_in(rng, 6)
    for position, shards_of in shards:
        steps = jnp.exp(jax.random.uniform(jax.random.fold_in(own, position), (shards_of,), jnp.float32, low / len(shards), high / len(shards)))
        level = level * jnp.repeat(steps, shape[position] // shards_of).reshape([-1 if axis == position else 1 for axis in range(len(shape))])
    return level


def length_profile(number_of, total, reach, lean):
    weights = [(1 << 20) // math.isqrt(rank ** lean) + 1 for rank in range(2, number_of + 1)]
    surplus, given = total - reach - (number_of - 1), [1] * (number_of - 1)
    while surplus > 0:
        candidates = [i for i in range(number_of - 1) if given[i] < reach]
        pool, remaining = sum([weights[i] for i in candidates]), surplus
        for i in candidates:
            addition = min(reach - given[i], max(1, remaining * weights[i] // pool), surplus)
            given[i] = given[i] + addition
            surplus = surplus - addition
    return np.array([reach] + given)


def uneven(own_key, number_of, total, reach, skew):
    if number_of == 2:
        one = jax.random.randint(own_key, (), max(1, total - reach), min(reach, total - 1) + 1)
        return jnp.stack([one, total - one])
    sizes = jnp.asarray(length_profile(number_of, total, reach, skew), jnp.int32)
    pairs = (number_of - 1) // 2
    giver, receiver = sizes[1:1 + 2 * pairs:2], sizes[2:2 + 2 * pairs:2]
    slack = jnp.minimum(giver - 1, reach - receiver)
    shifted = jax.random.randint(jax.random.fold_in(own_key, 1), (pairs,), 0, 1 << 20) % (slack + 1)
    sizes = sizes.at[1:1 + 2 * pairs:2].set(giver - shifted).at[2:2 + 2 * pairs:2].set(receiver + shifted)
    return sizes[jax.random.permutation(jax.random.fold_in(own_key, 2), number_of)]


def deal_out(rng, own, number, rows, number_of, top, reach, slope):
    order = jax.random.permutation(rng, number_of)
    crowded, ordinary = shares(number_of, rows * top, reach, slope, True), shares(number_of, rows * top, reach, slope, False)
    places = jnp.arange(number_of)

    def named(tallies, rotation):
        used = int((tallies > 0).sum())
        fixed = max(1, used // 4)
        passed = fixed + (places - fixed + rotation * (used - fixed)) % max(1, number_of - fixed)
        return jnp.zeros((number_of,), jnp.int32).at[order[jnp.where(places < fixed, places, passed)]].set(jnp.asarray(tallies, jnp.int32))

    tallies = jnp.where(number % 4 == 0, named(crowded, number // 4), named(ordinary, number - number // 4 - 1))
    mixed = jax.random.permutation(jax.random.fold_in(own, 3), number_of)
    source_of, receiver = mixed[0:number_of // 2 * 2:2], mixed[1:number_of // 2 * 2:2]
    slack = jnp.minimum(tallies[source_of] - 1, reach - tallies[receiver]) // 2
    slack = jnp.where((source_of == order[0]) | (receiver == order[0]) | (tallies[receiver] == 0), 0, jnp.maximum(slack, 0))
    passed = jax.random.randint(jax.random.fold_in(own, 4), (number_of // 2,), 0, 1 << 20) % (slack + 1)
    tallies = tallies.at[source_of].add(-passed).at[receiver].add(passed)
    items = jnp.searchsorted(jnp.cumsum(tallies), jnp.arange(rows * top), side="right").astype(jnp.int32)
    grid = items.reshape(top, rows).T
    grid = grid[jax.random.permutation(jax.random.fold_in(own, 1), rows)]
    rotation = jax.random.randint(jax.random.fold_in(own, 2), (rows, 1), 0, top)
    return jnp.take_along_axis(grid, (jnp.arange(top)[None, :] + rotation) % top, axis=1)


def shares(number_of, total, limit, slope, full):
    portions = [(1 << 20) // math.isqrt(standing ** slope) + 1 for standing in range(1, number_of + 1)]
    largest = limit if full else min(limit, max(-(-total // number_of), total * portions[0] // sum(portions)))
    least = 1 if total - largest >= number_of - 1 else 0
    holding, spare = [largest] + [least] * (number_of - 1), total - largest - least * (number_of - 1)
    while spare > 0:
        free = [i for i in range(1, number_of) if holding[i] < largest] or [i for i in range(1, number_of) if holding[i] < limit]
        mass, left = sum([portions[i] for i in free]), spare
        for i in free:
            extra = min(limit - holding[i], max(1, left * portions[i] // mass), spare)
            holding[i] = holding[i] + extra
            spare = spare - extra
    return np.array(holding)


def gaussian(key, extent, scale, limit, shards=(), dtype=jnp.bfloat16):
    values = jax.random.normal(key, extent, jnp.float32) * scale
    if len(shards) > 0:
        values = block_scale(key, extent, shards, -0.22, 0.18) * values
    return jnp.clip(values, min=-limit, max=limit).astype(dtype)


def setup_inputs(seed: int = 0) -> dict:
    arg_keys = jax.random.split(jax.random.key(seed), 19)
    tokens = gaussian(arg_keys[0], (TOKENS, D), 1.0, 6.0, ((0, 16),))
    cell_ids = jax.vmap(lambda own: jnp.searchsorted(jnp.cumsum(uneven(own, CELLS, TOK_DEV, CELL_MOST, 2)), jnp.arange(TOK_DEV), side="right"))(jax.random.split(arg_keys[1], N_DP)).reshape((N_DP, TOK_DEV)).astype(jnp.int32)
    gene_range_keys = jax.random.split(jax.random.fold_in(arg_keys[2], 1), TOKENS // TOK_DEV)
    gene_range_turns = jax.random.permutation(jax.random.fold_in(arg_keys[2], 3), TOKENS // TOK_DEV)
    gene_range = jax.vmap(lambda own, number: deal_out(jax.random.fold_in(arg_keys[2], 2), own, number, TOK_DEV, N_DP, 1, CAP, 2))(gene_range_keys, gene_range_turns).reshape((TOKENS, 1))
    gene_offset = set_ends(jax.random.randint(arg_keys[3], (TOKENS,), 0, GENE_DEV), jax.random.fold_in(arg_keys[3], 1), 0, GENE_DEV - 1).astype(jnp.int32)
    gain1 = jnp.clip(1.0 + 0.18 * jax.random.normal(arg_keys[4], (D,), jnp.float32), 0.1, 1.9)
    shift1 = gaussian(arg_keys[5], (D,), 0.3, 4.0, (), jnp.float32)
    w_qkv = gaussian(arg_keys[6], (3, D, D), D ** -0.5, 0.21875, ((2, 2),))
    w_out = gaussian(arg_keys[7], (D, D), (D // 128) ** -0.5, 2.5, ((0, 2),))
    out_bias = gaussian(arg_keys[8], (D,), 0.3, 4.0, (), jnp.float32)
    gain2 = jnp.clip(1.0 + 0.18 * jax.random.normal(arg_keys[9], (D,), jnp.float32), 0.1, 1.9)
    shift2 = gaussian(arg_keys[10], (D,), 0.3, 4.0, (), jnp.float32)
    w_up = gaussian(arg_keys[11], (D, FF), D ** -0.5, 0.21875, ((1, 2),))
    up_bias = gaussian(arg_keys[12], (FF,), 0.5, 6.0, ((0, 2),), jnp.float32)
    w_down = gaussian(arg_keys[13], (FF, D), FF ** -0.5, 0.109375, ((0, 2),))
    down_bias = gaussian(arg_keys[14], (D,), 0.3, 4.0, (), jnp.float32)
    w_proj = gaussian(arg_keys[15], (D, PD), D ** -0.5, 0.21875, ((1, 2),))
    zero_embed = gaussian(arg_keys[16], (GENES, PD), 1.0, 6.0, ((0, 16), (1, 2)))
    dense_cot = gaussian(arg_keys[17], (GENES, PD), 1.0, 6.0, ((0, 16), (1, 2)))
    return dict(tokens=tokens, cell_ids=cell_ids, gene_range=gene_range, gene_offset=gene_offset, gain1=gain1, shift1=shift1, w_qkv=w_qkv, w_out=w_out, out_bias=out_bias, gain2=gain2, shift2=shift2, w_up=w_up, up_bias=up_bias, w_down=w_down, down_bias=down_bias, w_proj=w_proj, zero_embed=zero_embed, dense_cot=dense_cot)


@jax.custom_vjp
def low(v):
    return lax.optimization_barrier(v.astype(jnp.bfloat16)).astype(jnp.float32)

@jax.custom_vjp
def low_back(v):
    return v

def low_keep(v):
    return (low(v), None)

def low_pass(kept, grad):
    return (grad,)

def back_keep(v):
    return (v, None)

def back_low(kept, grad):
    return (low(grad),)
low.defvjp(low_keep, low_pass)
low_back.defvjp(back_keep, back_low)
EPSILON = 1e-05
NEG_LARGE = -1e+30
HIGHEST = lax.Precision.HIGHEST

def layer_norm(values, gain, shift):
    centered = values - lax.optimization_barrier(jnp.mean(values, -1, keepdims=True))
    inverse = lax.rsqrt(lax.optimization_barrier(jnp.mean(centered * centered, -1, keepdims=True)) + EPSILON)
    return centered * inverse * gain + shift

def block_row(params, row_in, row_cells):
    gain1, shift1, w_qkv, w_out, out_bias, gain2, shift2, w_up, up_bias, w_down, down_bias, w_proj = params
    tok_count = row_in.shape[0]
    normed1 = low(layer_norm(row_in, gain1, shift1))
    qkv_all = low_back(low(jnp.einsum('td,jdc->jtc', normed1, w_qkv, precision=HIGHEST)))
    queries = qkv_all[0].reshape(tok_count, HEADS, HEAD_DIM)
    keys = qkv_all[1].reshape(tok_count, HEADS, HEAD_DIM)
    values = qkv_all[2].reshape(tok_count, HEADS, HEAD_DIM)
    scores = jnp.einsum('qhd,khd->hqk', queries, keys, precision=HIGHEST) * HEAD_DIM ** (-0.5)
    is_same = (row_cells[:, None] == row_cells[None, :])[None]
    scores = low_back(jnp.where(is_same, scores, NEG_LARGE))
    log_total = jax.nn.logsumexp(scores, axis=-1, keepdims=True)
    probs = low(jnp.exp(scores - log_total))
    mixed = low_back(low(jnp.einsum('hqk,khd->qhd', probs, values, precision=HIGHEST))).reshape(tok_count, D)
    attended = low_back(jnp.dot(mixed, w_out, precision=HIGHEST))
    middle = row_in + attended + out_bias
    normed2 = low(layer_norm(middle, gain2, shift2))
    hidden = low_back(jnp.dot(normed2, w_up, precision=HIGHEST) + up_bias)
    activ = low(jax.nn.gelu(hidden))
    result = middle + jnp.dot(activ, w_down, precision=HIGHEST) + down_bias
    result_low = low(low_back(result))
    projected = low_back(low(jnp.dot(result_low, w_proj, precision=HIGHEST)))
    return (result, projected)

def reference(tokens, cell_ids, gene_range, gene_offset, gain1, shift1, w_qkv, w_out, out_bias, gain2, shift2, w_up, up_bias, w_down, down_bias, w_proj, zero_embed, dense_cot):
    params = tuple((item.astype(jnp.float32) for item in (gain1, shift1, w_qkv, w_out, out_bias, gain2, shift2, w_up, up_bias, w_down, down_bias, w_proj)))
    tok_float = tokens.astype(jnp.float32)
    zero_float = zero_embed.astype(jnp.float32)
    genes = (gene_range[:, 0] * GENE_DEV + gene_offset).astype(jnp.int32)
    counts = jax.ops.segment_sum(jnp.ones(genes.shape, jnp.float32), genes, num_segments=GENES)
    divisor = (1.0 + counts)[:, None]
    checked = jax.checkpoint(block_row)

    def forward(tok_in, weights, zero_in):

        def step(carry, items):
            row_out, row_sent = checked(weights, items[0], items[1])
            return (carry, (row_out, row_sent))
        _, (outputs, sents) = lax.scan(step, jnp.zeros((), jnp.float32), (tok_in.reshape(N_DP, TOK_DEV, D), cell_ids))
        summed = jax.ops.segment_sum(sents.reshape(TOKENS, PD), genes, num_segments=GENES)
        return (outputs.reshape(TOKENS, D), (zero_in + summed) / divisor)
    (block, dense), pull = jax.vjp(forward, tok_float, params, zero_float)
    grad_tok, grads, grad_zero = pull((jnp.zeros_like(block), dense_cot.astype(jnp.float32)))
    return (block.astype(jnp.bfloat16), dense, grad_tok, grad_zero, grads[2], grads[3], grads[7], grads[9], grads[11], grads[0], grads[1], grads[4], grads[5], grads[6], grads[8], grads[10])
```

```python
import jax
import jax.numpy as jnp
from jax import lax
from jax.sharding import PartitionSpec as P

HEAD_DIM = 64
EPSILON = 1e-05
NEG_LARGE = -1e30
BF = jnp.bfloat16
F32 = jnp.float32


def layer_stats(values):
    centered = values - jnp.mean(values, -1, keepdims=True)
    inverse = lax.rsqrt(jnp.mean(centered * centered, -1, keepdims=True) + EPSILON)
    return (centered * inverse, inverse)


def layer_back(grad_normed, normal, inverse, gain):
    scaled = grad_normed * gain
    return inverse * (
        scaled
        - jnp.mean(scaled, -1, keepdims=True)
        - normal * jnp.mean(scaled * normal, -1, keepdims=True)
    )


def masked_scores(queries, keys, is_same, factor):
    scores = jnp.einsum("qhd,khd->hqk", queries, keys, preferred_element_type=jnp.float32) * factor
    return jnp.where(is_same, scores, NEG_LARGE)


def dp_swap(value, bit):
    size = lax.axis_size("dp")
    return lax.ppermute(value, "dp", [(i, i ^ (1 << bit)) for i in range(size)])


def mp_swap(value):
    return lax.ppermute(value, "mp", [(0, 1), (1, 0)])


def bit_order(turn):
    bits = lax.axis_size("dp").bit_length() - 1
    low = list(range(bits - 1))
    turn = turn % len(low)
    return low[turn:] + low[:turn] + [bits - 1]


def slot_offsets(order):
    bits = len(order)
    return [
        sum(((s >> (bits - 1 - place)) & 1) << bit for place, bit in enumerate(order))
        for s in range(1 << bits)
    ]


def chunks_of(grad, order):
    size = lax.axis_size("dp")
    chosen = jnp.asarray(slot_offsets(order), jnp.int32) ^ lax.axis_index("dp")
    return jnp.take(grad.astype(BF).reshape(size, -1, grad.shape[1]), chosen, axis=0)


def reduce_scatter(slots, order):
    for bit in order:
        half = slots.shape[0] // 2
        arrived = dp_swap(slots[half:], bit)
        slots = slots[:half] + arrived
    return slots[0]


def all_reduce(value):
    for bit in range(lax.axis_size("dp").bit_length() - 1):
        value = value + dp_swap(value, bit)
    return value


def all_gather(value):
    bits = lax.axis_size("dp").bit_length() - 1
    held = value[None]
    for bit in reversed(range(bits)):
        held = jnp.stack([held, dp_swap(held, bit)], 1).reshape((-1,) + value.shape)
    return held


def per_device(
    tokens,
    cell_ids,
    gene_range,
    gene_offset,
    gain1,
    shift1,
    w_qkv,
    w_out,
    out_bias,
    gain2,
    shift2,
    w_up,
    up_bias,
    w_down,
    down_bias,
    w_proj,
    zero_embed,
    dense_cot,
):
    tok_count = tokens.shape[0]
    owners = lax.axis_size("dp")
    me = lax.axis_index("dp")
    core = lax.axis_index("mp")
    local_width = w_qkv.shape[2]
    local_heads = local_width // HEAD_DIM
    factor = HEAD_DIM ** (-0.5)
    gene_local = zero_embed.shape[0]

    offset_hits = (gene_offset[None, :] == jnp.arange(gene_local)[:, None]).astype(BF)
    owner_hits = (gene_range == jnp.arange(owners)[None, :]).astype(BF)
    hist = jnp.dot(offset_hits, owner_hits, preferred_element_type=F32)
    gathered = all_gather(jnp.concatenate([dense_cot, hist.astype(BF)], 1))
    proj_width = dense_cot.shape[1]
    cots = gathered[:, :, :proj_width].astype(F32)
    counts = jnp.sum(gathered[:, :, proj_width:].astype(F32), 0)
    slot_owner = jnp.arange(owners) ^ me
    divisors = 1.0 + jnp.take(counts.T, slot_owner, axis=0)[:, :, None]
    grad_zero_all = cots / divisors
    grad_zero = grad_zero_all[0]
    divisor = divisors[0]
    slot_gene = ((gene_range[:, 0] ^ me) * gene_local + gene_offset)[:, None]
    gene_hits = (slot_gene == jnp.arange(owners * gene_local)[None, :]).astype(BF)
    grad_sent = jnp.dot(
        gene_hits,
        grad_zero_all.astype(BF).reshape(owners * gene_local, proj_width),
        preferred_element_type=F32,
    ).astype(BF)
    sent_other = mp_swap(grad_sent)
    proj_other = mp_swap(w_proj)
    grad_result = (
        jnp.einsum("tp,dp->td", grad_sent, w_proj, preferred_element_type=F32)
        + jnp.einsum("tp,dp->td", sent_other, proj_other, preferred_element_type=F32)
    ).astype(BF)

    row_cells = cell_ids[0]
    is_same = (row_cells[:, None] == row_cells[None, :])[None]
    x_float = tokens.astype(jnp.float32)
    normal1, inverse1 = layer_stats(x_float)
    normed1 = (normal1 * gain1 + shift1).astype(jnp.bfloat16)
    qkv_all = jnp.einsum("td,jdc->jtc", normed1, w_qkv, preferred_element_type=jnp.float32).astype(
        jnp.bfloat16
    )
    queries = qkv_all[0].reshape(tok_count, local_heads, HEAD_DIM)
    keys = qkv_all[1].reshape(tok_count, local_heads, HEAD_DIM)
    values = qkv_all[2].reshape(tok_count, local_heads, HEAD_DIM)
    scores = masked_scores(queries, keys, is_same, factor)
    top_score = jnp.max(scores, -1, keepdims=True)
    log_total = top_score + jnp.log(jnp.sum(jnp.exp(scores - top_score), -1, keepdims=True))
    probs = jnp.exp(scores - log_total).astype(jnp.bfloat16)
    mixed = (
        jnp.einsum("hqk,khd->qhd", probs, values, preferred_element_type=jnp.float32)
        .astype(jnp.bfloat16)
        .reshape(tok_count, local_width)
    )
    mixed_other = mp_swap(mixed)
    out_other = mp_swap(w_out)
    attended = jnp.dot(mixed, w_out, preferred_element_type=F32) + jnp.dot(
        mixed_other, out_other, preferred_element_type=F32
    )
    middle = x_float + attended + out_bias
    normal2, inverse2 = layer_stats(middle)
    normed2 = (normal2 * gain2 + shift2).astype(jnp.bfloat16)
    hidden = jnp.dot(normed2, w_up, preferred_element_type=jnp.float32) + up_bias
    activ = jax.nn.gelu(hidden).astype(jnp.bfloat16)
    feed_part = jnp.dot(activ, w_down, preferred_element_type=jnp.float32).astype(jnp.bfloat16)
    feed = feed_part.astype(F32) + mp_swap(feed_part).astype(F32)
    result = middle + feed + down_bias
    block_out = result.astype(jnp.bfloat16)
    sent = jnp.dot(block_out, w_proj, preferred_element_type=jnp.float32).astype(jnp.bfloat16)

    grad_result_float = grad_result.astype(jnp.float32)
    grad_down_bias = jnp.sum(grad_result_float, 0)
    grad_activ = jnp.einsum("td,cd->tc", grad_result, w_down, preferred_element_type=jnp.float32)
    _, gelu_pull = jax.vjp(jax.nn.gelu, hidden)
    grad_hidden = gelu_pull(grad_activ)[0].astype(jnp.bfloat16)
    grad_up_bias = jnp.sum(grad_hidden.astype(jnp.float32), 0)
    part2 = jnp.einsum("tc,dc->td", grad_hidden, w_up, preferred_element_type=jnp.float32)
    grad_normed2 = part2 + mp_swap(part2)

    orders = [bit_order(0), bit_order(1), bit_order(2)]
    grad_down = jnp.einsum("td,tc->dc", grad_result, activ, preferred_element_type=jnp.float32)
    share_down = reduce_scatter(chunks_of(grad_down, orders[0]), orders[0])
    grad_up = jnp.einsum("td,tc->dc", normed2, grad_hidden, preferred_element_type=jnp.float32)
    share_up = reduce_scatter(chunks_of(grad_up, orders[1]), orders[1])

    grad_gain2 = jnp.sum(grad_normed2 * normal2, 0)
    grad_shift2 = jnp.sum(grad_normed2, 0)
    grad_middle = grad_result_float + layer_back(grad_normed2, normal2, inverse2, gain2)
    grad_out_bias = jnp.sum(grad_middle, 0)
    grad_middle_low = grad_middle.astype(jnp.bfloat16)
    grad_wout = jnp.einsum("td,tc->dc", grad_middle_low, mixed, preferred_element_type=jnp.float32)
    grad_proj = jnp.einsum("td,tp->dp", block_out, grad_sent, preferred_element_type=jnp.float32)
    small_grads = jnp.concatenate([grad_wout, grad_proj], 1)
    share_small = reduce_scatter(chunks_of(small_grads, orders[2]), orders[2])
    share_wout = share_small[:, : grad_wout.shape[1]]
    share_proj = share_small[:, grad_wout.shape[1] :]

    partial_dense = jnp.einsum("tg,tp->gp", gene_hits, sent, preferred_element_type=F32)
    dense_order = list(range(owners.bit_length() - 1))[::-1]
    summed = reduce_scatter(
        partial_dense.astype(BF).reshape(owners, gene_local, proj_width), dense_order
    ).astype(F32)
    dense = (zero_embed.astype(jnp.float32) + summed) / divisor

    grad_mixed = (
        jnp.einsum("td,cd->tc", grad_middle_low, w_out, preferred_element_type=jnp.float32)
        .astype(jnp.bfloat16)
        .reshape(tok_count, local_heads, HEAD_DIM)
    )
    again = masked_scores(queries, keys, is_same, factor)
    probs_full = jnp.exp(again - log_total)
    grad_values = jnp.einsum(
        "hqk,qhd->khd",
        probs_full.astype(jnp.bfloat16),
        grad_mixed,
        preferred_element_type=jnp.float32,
    ).astype(jnp.bfloat16)
    grad_probs = jnp.einsum("qhd,khd->hqk", grad_mixed, values, preferred_element_type=jnp.float32)
    grad_scores = (
        probs_full * (grad_probs - jnp.sum(probs_full * grad_probs, -1, keepdims=True))
    ).astype(jnp.bfloat16)
    grad_queries = (
        jnp.einsum("hqk,khd->qhd", grad_scores, keys, preferred_element_type=jnp.float32) * factor
    ).astype(jnp.bfloat16)
    grad_keys = (
        jnp.einsum("hqk,qhd->khd", grad_scores, queries, preferred_element_type=jnp.float32)
        * factor
    ).astype(jnp.bfloat16)
    grad_stack = jnp.concatenate(
        [
            grad_queries.reshape(tok_count, local_width),
            grad_keys.reshape(tok_count, local_width),
            grad_values.reshape(tok_count, local_width),
        ],
        1,
    )
    grad_wqkv = jnp.einsum("td,tc->dc", normed1, grad_stack, preferred_element_type=jnp.float32)
    share_qkv = jnp.concatenate(
        [
            reduce_scatter(
                chunks_of(grad_wqkv[:, j * local_width : (j + 1) * local_width], orders[j]),
                orders[j],
            )[None]
            for j in range(3)
        ],
        0,
    )
    part1 = sum(
        jnp.einsum(
            "tc,dc->td",
            grad_stack[:, j * local_width : (j + 1) * local_width],
            w_qkv[j],
            preferred_element_type=jnp.float32,
        )
        for j in range(3)
    ).astype(BF)
    grad_normed1 = part1.astype(F32) + mp_swap(part1).astype(F32)
    grad_gain1 = jnp.sum(grad_normed1 * normal1, 0)
    grad_shift1 = jnp.sum(grad_normed1, 0)
    grad_tokens = grad_middle + layer_back(grad_normed1, normal1, inverse1, gain1)
    pieces = [
        grad_gain1,
        grad_shift1,
        grad_out_bias,
        grad_gain2,
        grad_shift2,
        grad_up_bias,
        grad_down_bias,
    ]
    total = all_reduce(jnp.concatenate(pieces))
    small_sums, at = [], 0
    for piece in pieces:
        small_sums.append(total[at : at + piece.shape[0]])
        at += piece.shape[0]
    return (
        block_out,
        dense,
        grad_tokens,
        grad_zero,
        share_qkv.astype(F32),
        share_wout.astype(F32).T,
        share_up.astype(F32),
        share_down.astype(F32).T,
        share_proj.astype(F32),
    ) + tuple(small_sums)


def solution(mesh):
    in_specs = (
        P("dp", None),
        P("dp", None),
        P("dp", None),
        P("dp"),
        P(),
        P(),
        P(None, None, "mp"),
        P("mp", None),
        P(),
        P(),
        P(),
        P(None, "mp"),
        P("mp"),
        P("mp", None),
        P(),
        P(None, "mp"),
        P("dp", "mp"),
        P("dp", "mp"),
    )
    out_specs = (
        P("dp", None),
        P("dp", "mp"),
        P("dp", None),
        P("dp", "mp"),
        P(None, "dp", "mp"),
        P("mp", "dp"),
        P("dp", "mp"),
        P("mp", "dp"),
        P("dp", "mp"),
        P(),
        P(),
        P(),
        P(),
        P(),
        P("mp"),
        P(),
    )
    return jax.shard_map(
        per_device, mesh=mesh, in_specs=in_specs, out_specs=out_specs, check_vma=False
    )
```

```python
import functools
import jax
import jax.numpy as jnp
from jax import lax
from jax.experimental import pallas as pl
from jax.experimental.pallas import tpu as pltpu
from jax.sharding import PartitionSpec as P

HEAD_DIM = 64
EPSILON = 1e-05
BIG = 1e30
BF = jnp.bfloat16
F32 = jnp.float32
MIB = 1 << 20

NT = (((1,), (1,)), ((), ()))


def dot(left, right):
    return jnp.dot(left, right, preferred_element_type=F32)


def dot_nt(left, right):
    return lax.dot_general(left, right, NT, preferred_element_type=F32)


def whole(shape):
    return pl.BlockSpec(shape, lambda *_: (0,) * len(shape))


VM = pl.BlockSpec(memory_space=pltpu.VMEM)
SM = pl.BlockSpec(memory_space=pltpu.SMEM)


def pick(place_ref, offsets, slot):
    first, second = offsets[0][slot], offsets[1][slot]
    if first == second:
        return first
    return first + place_ref[1] * (second - first)


def slot_of(place_ref, orders, owner):
    other = place_ref[0] ^ owner
    slots = []
    for order in orders:
        bits = len(order)
        slots.append(sum(((other >> bit) & 1) << (bits - 1 - spot) for spot, bit in enumerate(order)))
    return jnp.where(place_ref[1] == 0, slots[0], slots[1])


def params(mib=20):
    return pltpu.CompilerParams(vmem_limit_bytes=mib * MIB)


def cost(flops, moved):
    return pl.CostEstimate(flops=int(flops), bytes_accessed=int(moved), transcendentals=0)


def norm_stats(values):
    centered = values - jnp.mean(values, -1, keepdims=True)
    inverse = lax.rsqrt(jnp.mean(centered * centered, -1, keepdims=True) + EPSILON)
    return centered * inverse, inverse


def norm_back(grad, normal, inverse, gain):
    scaled = grad * gain
    return inverse * (
        scaled
        - jnp.mean(scaled, -1, keepdims=True)
        - normal * jnp.mean(scaled * normal, -1, keepdims=True)
    )


def gene_rows(genes, owners):
    owners_pad = -(-owners // 16) * 16
    return -(-genes // owners_pad) * owners_pad, owners_pad


def payload_kernel(owners_pad, range_hbm, offset_hbm, cot_hbm, out_ref, range_ref, offset_ref, cot_ref, sems):
    copies = [
        pltpu.make_async_copy(source, target, sems.at[i])
        for i, (source, target) in enumerate(
            ((range_hbm, range_ref), (offset_hbm, offset_ref), (cot_hbm, cot_ref))
        )
    ]
    for copy in copies:
        copy.start()
    for copy in copies:
        copy.wait()
    genes, width = cot_ref.shape
    tok = range_ref.shape[1]
    rows = out_ref.shape[0] - owners_pad
    cot = cot_ref[...].astype(F32)
    if rows > genes:
        cot = jnp.concatenate([cot, jnp.zeros((rows - genes, width), F32)], 0)
    out_ref[:rows, :] = cot.astype(BF)
    owner_hits = jnp.where(
        lax.broadcasted_iota(jnp.int32, (owners_pad, tok), 0) == range_ref[...], 1.0, 0.0
    ).astype(BF)
    offset_hits = jnp.where(
        lax.broadcasted_iota(jnp.int32, (width, tok), 0) == offset_ref[...], 1.0, 0.0
    ).astype(BF)
    out_ref[rows:, :] = dot_nt(owner_hits, offset_hits).astype(BF)


def make_payload(gene_range, gene_offset, cot, owners):
    genes, width = cot.shape
    tok = gene_offset.shape[1]
    rows, owners_pad = gene_rows(genes, owners)
    hbm = pl.BlockSpec(memory_space=pltpu.HBM)
    return pl.pallas_call(
        functools.partial(payload_kernel, owners_pad),
        in_specs=[hbm] * 3,
        out_shape=jax.ShapeDtypeStruct((rows + owners_pad, width), BF),
        scratch_shapes=[
            pltpu.VMEM((1, tok), jnp.int32),
            pltpu.VMEM((1, tok), jnp.int32),
            pltpu.VMEM((genes, width), BF),
            pltpu.SemaphoreType.DMA((3,)),
        ],
        compiler_params=params(),
        cost_estimate=cost(2 * tok * 16 * 256, 300000),
        name="payload",
    )(*(pltpu.with_memory_space_constraint(item, pltpu.HBM) for item in (gene_range, gene_offset, cot)))


def sent_kernel(
    genes, orders, place_ref, range_ref, offset_ref, hist_ref, hist_far_ref, held_ref, far_ref,
    sent_ref, zero_ref, div_ref, total, by_gene, low,
):
    batch, rows, width = held_ref.shape
    half, owners_pad, _ = hist_ref.shape
    step = pl.program_id(0)
    me = place_ref[0]
    tok = range_ref.shape[1]

    @pl.when(step == 0)
    def _():
        counts = jnp.zeros((owners_pad, width), F32)
        for ref in (hist_ref, hist_far_ref):
            for slot in range(half):
                counts += ref[slot].astype(F32)
        if owners_pad < 128:
            counts = jnp.concatenate([counts, jnp.zeros((128 - owners_pad, width), F32)], 0)
        by_gene[...] = 1.0 + counts.T[:rows]
        total[...] = jnp.zeros_like(total)

    spread = by_gene[...]
    owner_lane = lax.broadcasted_iota(jnp.int32, spread.shape, 1)
    other = range_ref[...] ^ me
    slots = [
        sum(((other >> bit) & 1) << spot for spot, bit in enumerate(order)) for order in orders
    ]
    slots = jnp.where(place_ref[1] == 0, slots[0], slots[1])
    top = 2 * half // 2
    far_side = slots // top
    near = slots - far_side * top
    index = (far_side * batch + near - step * batch) * rows + offset_ref[...]
    index = jnp.where((near >= step * batch) & (near < (step + 1) * batch), index, -1)
    columns = jnp.broadcast_to(index, (128, tok)).T
    for side, ref in enumerate((held_ref, far_ref)):
        for place in range(batch):
            slot = side * half + step * batch + place
            offset = jnp.int32(0)
            for core, order in enumerate(orders):
                one = sum(((slot >> spot) & 1) << bit for spot, bit in enumerate(order))
                offset = jnp.where(place_ref[1] == core, one, offset)
            divisor = jnp.sum(jnp.where(owner_lane == (me ^ offset), spread, 0.0), 1, keepdims=True)
            grad = ref[place].astype(F32) * (1.0 / divisor)
            if place == 0 and side == 0:

                @pl.when(step == 0)
                def _():
                    zero_ref[...] = grad[:genes]
                    div_ref[...] = jnp.broadcast_to(divisor[:genes], (genes, width))

            at = (side * batch + place) * rows
            low[at : at + rows, :] = grad.astype(BF)
    lane = lax.broadcasted_iota(jnp.int32, (tok, 128), 1)
    hits = jnp.concatenate(
        [
            jnp.where(columns == lane + at, 1.0, 0.0).astype(BF)
            for at in range(0, 2 * batch * rows, 128)
        ],
        1,
    )
    total[...] += dot(hits, low[...])

    @pl.when(step == pl.num_programs(0) - 1)
    def _():
        sent_ref[...] = total[...].astype(BF)


def make_sent(place, gene_range, gene_offset, held, far, genes, orders):
    half, height, width = held.shape
    owners = 2 * half
    rows, owners_pad = gene_rows(genes, owners)
    batch = min(half, 8)
    tok = gene_offset.shape[1]
    hist = pl.BlockSpec((half, owners_pad, width), lambda i: (0, rows // owners_pad, 0))
    cots = pl.BlockSpec((batch, rows, width), lambda i: (i, 0, 0))
    return pl.pallas_call(
        functools.partial(sent_kernel, genes, orders),
        grid=(half // batch,),
        in_specs=[SM, whole((1, tok)), whole((1, tok)), hist, hist, cots, cots],
        out_specs=(whole((tok, width)), whole((genes, width)), whole((genes, width))),
        out_shape=(
            jax.ShapeDtypeStruct((tok, width), BF),
            jax.ShapeDtypeStruct((genes, width), F32),
            jax.ShapeDtypeStruct((genes, width), F32),
        ),
        scratch_shapes=[
            pltpu.VMEM((tok, width), F32),
            pltpu.VMEM((rows, 128 * -(-owners // 128)), F32),
            pltpu.VMEM((2 * batch * rows, width), BF),
        ],
        compiler_params=params(20 if owners <= 16 else 48),
        cost_estimate=cost(2 * tok * owners * 160 * width, 2 * held.size),
        name="grad_sent",
    )(place, gene_range, gene_offset, held, far, held, far)


def qkv_kernel(x_ref, affine_ref, w_ref, normed_ref, q_ref, k_ref, v_ref):
    normal, _ = norm_stats(x_ref[...].astype(F32))
    normed = (normal * affine_ref[0:1] + affine_ref[1:2]).astype(BF)
    normed_ref[...] = normed
    for j, out in enumerate((q_ref, k_ref, v_ref)):
        out[...] = dot(normed, w_ref[j]).astype(BF)


def make_qkv(tokens, affine, w_qkv):
    tok, width = tokens.shape
    local = w_qkv.shape[2]
    one = jax.ShapeDtypeStruct((tok, local), BF)
    return pl.pallas_call(
        qkv_kernel,
        in_specs=[pl.BlockSpec(memory_space=pltpu.VMEM)] * 3,
        out_shape=(jax.ShapeDtypeStruct((tok, width), BF), one, one, one),
        compiler_params=params(),
        cost_estimate=cost(2 * tok * w_qkv.size, 2 * (tokens.size * 2 + w_qkv.size * 2)),
        name="qkv",
    )(tokens, affine, w_qkv)


def masked_pair(q_pair, k_pair, cells, half, cell_count=8):
    lane = lax.broadcasted_iota(jnp.int32, q_pair.shape, 1)
    own = (lane // HEAD_DIM) == half
    place = lane % HEAD_DIM
    same = place == cells
    q_mask = jnp.where((place < cell_count) & jnp.logical_not(same), -BIG, 0.0)
    k_mask = jnp.where(same, 1.0, 0.0)
    scaled = q_pair.astype(F32) * (HEAD_DIM**-0.5)
    q_head = jnp.where(own, scaled, q_mask).astype(BF)
    k_head = jnp.where(own, k_pair.astype(F32), k_mask).astype(BF)
    return q_head, k_head


def attend_kernel(cells_ref, q_ref, k_ref, v_ref, mixed_ref, lse_ref):
    tok, local = q_ref.shape
    cells = jnp.broadcast_to(cells_ref[...], (128, tok)).T
    lane = lax.broadcasted_iota(jnp.int32, (tok, 128), 1)
    logs = jnp.zeros((tok, 128), F32)
    for pair in range(local // 128):
        cut = slice(pair * 128, pair * 128 + 128)
        q_pair, k_pair, v_pair = q_ref[:, cut], k_ref[:, cut], v_ref[:, cut]
        heads = []
        for half in range(2):
            q_head, k_head = masked_pair(q_pair, k_pair, cells, half)
            scores = dot_nt(q_head, k_head)
            top = jnp.max(scores, 1, keepdims=True)
            powers = jnp.exp(scores - top)
            total = jnp.sum(powers, 1, keepdims=True)
            probs = (powers * (1.0 / total)).astype(BF)
            logs = jnp.where(lane == 2 * pair + half, top + jnp.log(total), logs)
            heads.append(dot(probs, v_pair))
        mixed_ref[:, cut] = jnp.where(lane < HEAD_DIM, heads[0], heads[1]).astype(BF)
    lse_ref[...] = logs.T[: lse_ref.shape[0]]

def make_attend(cell_ids, q, k, v):
    tok, local = q.shape
    heads = -(-local // HEAD_DIM // 8) * 8
    return pl.pallas_call(
        attend_kernel,
        in_specs=[VM] * 4,
        out_shape=(jax.ShapeDtypeStruct((tok, local), BF), jax.ShapeDtypeStruct((heads, tok), F32)),
        compiler_params=params(), cost_estimate=cost(4 * tok * tok * local, 8 * tok * local), name="attend",
    )(cell_ids, q, k, v)

def pair_back(cells, q_pair, k_pair, v_pair, gm_pair, lse, lane):
    factor = HEAD_DIM**-0.5
    k_turned = k_pair.astype(F32).T.astype(BF)
    gq_halves = []
    gk = gv = None
    for half in range(2):
        own = (lane // HEAD_DIM) == half
        q_head, k_head = masked_pair(q_pair, k_pair, cells, half)
        v_head = jnp.where(own, v_pair.astype(F32), 0.0).astype(BF)
        probs = jnp.exp(dot_nt(k_head, q_head) - lse[half : half + 1])
        part = dot(probs.astype(BF), gm_pair)
        gv = part if half == 0 else jnp.where(own, part, gv)
        grad_probs = dot_nt(v_head, gm_pair)
        spread = jnp.sum(probs * grad_probs, 0, keepdims=True)
        grad_scores = (probs * (grad_probs - spread)).astype(BF)
        part = dot(grad_scores, q_pair)
        gk = part if half == 0 else jnp.where(own, part, gk)
        gq_halves.append(dot(k_turned[half * HEAD_DIM : (half + 1) * HEAD_DIM], grad_scores))
    gq = (jnp.concatenate(gq_halves, 0).T * factor).astype(BF)
    return gq, (gk * factor).astype(BF), gv.astype(BF)


GELU_A = 0.7978845608028654
GELU_B = 0.044715


def middle_kernel(
    chunk, x_ref, mixed_ref, other_ref, wo_ref, wo_other_ref, bias_ref, gain_ref, shift_ref, up_ref, up_bias_ref,
    middle_ref, normed_ref, act_ref, slope_ref,
):
    attended = dot(mixed_ref[...], wo_ref[...]) + dot(other_ref[...], wo_other_ref[...])
    middle = x_ref[...].astype(F32) + attended + bias_ref[...]
    middle_ref[...] = middle
    normal, _ = norm_stats(middle)
    normed = (normal * gain_ref[...] + shift_ref[...]).astype(BF)
    normed_ref[...] = normed
    for at in range(0, up_ref.shape[1], chunk):
        cut = slice(at, at + chunk)
        hidden = dot(normed, up_ref[:, cut]) + up_bias_ref[:, cut]
        square = hidden * hidden
        curve = jnp.tanh(hidden * (GELU_A + (GELU_A * GELU_B) * square))
        half = 0.5 * hidden
        act_ref[:, cut] = (half + half * curve).astype(BF)
        slope = (0.5 + 0.5 * curve) + half * (1.0 - curve * curve) * (
            GELU_A + (3 * GELU_A * GELU_B) * square
        )
        slope_ref[:, cut] = slope.astype(BF)


def make_middle(
    tokens, mixed, mixed_other, w_out, out_other, out_bias, gain, shift, w_up, up_bias, chunk=768
):
    tok, width = tokens.shape
    units = w_up.shape[1]
    return pl.pallas_call(
        functools.partial(middle_kernel, chunk),
        in_specs=[VM] * 10,
        out_shape=(
            jax.ShapeDtypeStruct((tok, width), F32),
            jax.ShapeDtypeStruct((tok, width), BF),
            jax.ShapeDtypeStruct((tok, units), BF),
            jax.ShapeDtypeStruct((tok, units), BF),
        ),
        compiler_params=params(24),
        cost_estimate=cost(4 * tok * mixed.shape[1] * width + 2 * tok * units * width, 12000000),
        name="middle",
    )(
        tokens, mixed, mixed_other, w_out, out_other, out_bias.reshape(1, -1), gain.reshape(1, -1),
        shift.reshape(1, -1), w_up, up_bias.reshape(1, -1),
    )


def feed_kernel(act_ref, down_ref, feed_ref):
    feed_ref[...] = dot(act_ref[...], down_ref[...]).astype(BF)


def make_feed(act, w_down):
    tok, units = act.shape
    width = w_down.shape[1]
    return pl.pallas_call(
        feed_kernel,
        in_specs=[VM] * 2,
        out_shape=jax.ShapeDtypeStruct((tok, width), BF),
        compiler_params=params(),
        cost_estimate=cost(2 * tok * units * width, 5000000),
        name="feed",
    )(act, w_down)


def feed_back_kernel(chunk, sent_ref, other_ref, wp_ref, wp_other_ref, slope_ref, down_ref, up_ref,
    result_ref, hidden_ref, normed_ref, down_bias_ref, up_bias_ref):
    result = dot_nt(sent_ref[...], wp_ref[...]) + dot_nt(other_ref[...], wp_other_ref[...])
    low = result.astype(BF)
    result_ref[...] = low
    down_bias_ref[...] = jnp.sum(low.astype(F32), 0, keepdims=True)
    for at in range(0, up_ref.shape[1], chunk):
        cut = slice(at, at + chunk)
        grad = (dot_nt(low, down_ref[cut]) * slope_ref[:, cut].astype(F32)).astype(BF)
        hidden_ref[:, cut] = grad
        up_bias_ref[:, cut] = jnp.sum(grad.astype(F32), 0, keepdims=True)
    normed_ref[...] = dot_nt(hidden_ref[...], up_ref[...]).astype(normed_ref.dtype)

def make_feed_back(sent, sent_other, w_proj, proj_other, slope, w_down, w_up, chunk=768):
    tok = sent.shape[0]
    width, units = w_up.shape
    return pl.pallas_call(
        functools.partial(feed_back_kernel, chunk),
        in_specs=[VM] * 7,
        out_shape=(
            jax.ShapeDtypeStruct((tok, width), BF),
            jax.ShapeDtypeStruct((tok, units), BF),
            jax.ShapeDtypeStruct((tok, width), BF),
            jax.ShapeDtypeStruct((1, width), F32),
            jax.ShapeDtypeStruct((1, units), F32),
        ),
        compiler_params=params(24),
        cost_estimate=cost(4 * tok * units * width, 12000000),
        name="feed_back",
    )(sent, sent_other, w_proj, proj_other, slope, w_down, w_up)


def weight_kernel(orders, groups, place_ref, *refs):
    ins = refs[: -2 - len(groups)]
    keep_ref, send_ref = refs[len(ins) : len(ins) + 2]
    size, chunk, tok = refs[-1].shape
    half = size // 2 * chunk
    at = place = 0
    for count, chosen in zip(groups, refs[len(ins) + 2 :]):
        turned = ins[place][...].astype(F32).T.astype(BF).reshape(chosen.shape)
        for owner in range(size):
            chosen[slot_of(place_ref, orders, owner)] = turned[owner]
        for right_ref in ins[place + 1 : place + 1 + count]:
            right = right_ref[...]
            cut = slice(at, at + right.shape[1])
            out = (size // 2, chunk, right.shape[1])
            keep_ref[:, :, cut] = dot(chosen[: size // 2].reshape(half, tok), right).astype(BF).reshape(out)
            send_ref[:, :, cut] = dot(chosen[size // 2 :].reshape(half, tok), right).astype(BF).reshape(out)
            at += right.shape[1]
        place += 1 + count


def make_weight(index, pairs, orders):
    tok, width = pairs[0][0].shape
    columns = sum(right.shape[1] for _, rights in pairs for right in rights)
    size = 1 << len(orders[0])
    chunk = width // size
    if chunk % 16:
        parts = [chunks_of(left, right, orders) for left, rights in pairs for right in rights]
        return tuple(jnp.concatenate(side, 2) for side in zip(*parts))
    out = jax.ShapeDtypeStruct((size // 2, chunk, columns), BF)
    flat = [item for left, rights in pairs for item in (left, *rights)]
    return pl.pallas_call(
        functools.partial(weight_kernel, orders, [len(rights) for _, rights in pairs]),
        in_specs=[SM] + [VM] * len(flat),
        out_shape=(out, out),
        scratch_shapes=[pltpu.VMEM((size, chunk, tok), BF) for _ in pairs],
        compiler_params=params(),
        cost_estimate=cost(2 * tok * width * columns, 2 * (tok * width + tok * columns + width * columns)),
        name="weight_grad",
    )(index, *flat)


def back_kernel(first, *refs):
    if first == 0:
        (
            cells_ref, result_ref, part_ref, other_ref, middle_ref, gain_ref, wo_ref, q_ref, k_ref, v_ref, lse_ref, w_ref,
            grad_middle_ref, low_ref, gain_sum_ref, shift_sum_ref, bias_sum_ref, gq_ref, gk_ref, gv_ref, normed_ref,
        ) = refs
        grad = part_ref[...].astype(F32) + other_ref[...].astype(F32)
        normal, inverse = norm_stats(middle_ref[...])
        gain_sum_ref[...] = jnp.sum(grad * normal, 0, keepdims=True)
        shift_sum_ref[...] = jnp.sum(grad, 0, keepdims=True)
        middle = result_ref[...].astype(F32) + norm_back(grad, normal, inverse, gain_ref[...])
        bias_sum_ref[...] = jnp.sum(middle, 0, keepdims=True)
        grad_middle_ref[...] = middle
        low = middle.astype(BF)
        low_ref[...] = low
    else:
        (
            cells_ref, low_ref, part_ref, wo_ref, q_ref, k_ref, v_ref, lse_ref, w_ref,
            gq_ref, gk_ref, gv_ref, normed_ref,
        ) = refs
        low = low_ref[...]
    tok = q_ref.shape[0]
    cells = jnp.broadcast_to(cells_ref[...], (128, tok)).T
    lane = lax.broadcasted_iota(jnp.int32, (tok, 128), 1)
    span = slice(first * 128, first * 128 + gq_ref.shape[1])
    gm = dot_nt(low, wo_ref[span]).astype(BF)
    for pair in range(gq_ref.shape[1] // 128):
        cut = slice(pair * 128, pair * 128 + 128)
        at = (first + pair) * 128
        own = slice(at, at + 128)
        head = 2 * (first + pair)
        out = pair_back(
            cells, q_ref[:, own], k_ref[:, own], v_ref[:, own], gm[:, cut], lse_ref[head : head + 2], lane
        )
        for ref, value in zip((gq_ref, gk_ref, gv_ref), out):
            ref[:, cut] = value
    total = (
        dot_nt(gq_ref[...], w_ref[0, :, span])
        + dot_nt(gk_ref[...], w_ref[1, :, span])
        + dot_nt(gv_ref[...], w_ref[2, :, span])
    )
    if first:
        total += part_ref[...]
    normed_ref[...] = total.astype(normed_ref.dtype)


def make_back_first(cell_ids, result, part, other, middle, gain, w_out, q, k, v, lse, w_qkv):
    tok, local = q.shape
    width = middle.shape[1]
    one = jax.ShapeDtypeStruct((tok, 128), BF)
    small = jax.ShapeDtypeStruct((1, width), F32)
    full = jax.ShapeDtypeStruct((tok, width), F32)
    return pl.pallas_call(
        functools.partial(back_kernel, 0),
        in_specs=[VM] * 12,
        out_shape=(full, jax.ShapeDtypeStruct((tok, width), BF), small, small, small, one, one, one, full),
        compiler_params=params(),
        cost_estimate=cost(10 * tok * tok * 128 + 8 * tok * width * 128, 15000000),
        name="back_first",
    )(cell_ids, result, part, other, middle, gain.reshape(1, -1), w_out, q, k, v, lse, w_qkv)


def make_back_rest(cell_ids, low, part, w_out, q, k, v, lse, w_qkv):
    tok, local = q.shape
    width = low.shape[1]
    one = jax.ShapeDtypeStruct((tok, local - 128), BF)
    return pl.pallas_call(
        functools.partial(back_kernel, 1),
        in_specs=[VM] * 9,
        out_shape=(one, one, one, jax.ShapeDtypeStruct((tok, width), BF)),
        compiler_params=params(),
        cost_estimate=cost(10 * tok * tok * (local - 128) + 8 * tok * width * local, 10000000),
        name="back_rest",
    )(cell_ids, low, part, w_out, q, k, v, lse, w_qkv)


def last_kernel(x_ref, part_ref, other_ref, middle_ref, gain_ref, out_ref, gain_sum_ref, shift_sum_ref):
    grad = part_ref[...].astype(F32) + other_ref[...].astype(F32)
    normal, inverse = norm_stats(x_ref[...].astype(F32))
    gain_sum_ref[...] = jnp.sum(grad * normal, 0, keepdims=True)
    shift_sum_ref[...] = jnp.sum(grad, 0, keepdims=True)
    out_ref[...] = middle_ref[...] + norm_back(grad, normal, inverse, gain_ref[...])


def make_last(tokens, part, other, grad_middle, gain):
    tok, width = tokens.shape
    small = jax.ShapeDtypeStruct((1, width), F32)
    return pl.pallas_call(
        last_kernel,
        out_shape=(jax.ShapeDtypeStruct((tok, width), F32), small, small),
        compiler_params=params(),
        cost_estimate=cost(20 * tok * width, 16 * tok * width),
        name="last",
    )(tokens, part, other, grad_middle, gain.reshape(1, -1))


def output_kernel(
    orders, place_ref, range_ref, offset_ref, middle_ref, part_ref, other_ref, bias_ref, wp_ref,
    out_ref, keep_ref, send_ref,
):
    result = middle_ref[...] + (part_ref[...].astype(F32) + other_ref[...].astype(F32)) + bias_ref[...]
    low = result.astype(BF)
    out_ref[...] = low
    sent = dot(low, wp_ref[...]).astype(BF)
    half, rows, width = keep_ref.shape
    tok = range_ref.shape[1]
    index = slot_of(place_ref, orders, range_ref[...]) * rows + offset_ref[...]
    gene = lax.broadcasted_iota(jnp.int32, (rows, tok), 0)
    for side, ref in enumerate((keep_ref, send_ref)):
        for at in range(0, half, 8):
            hits = jnp.concatenate(
                [
                    jnp.where(gene + (side * half + slot) * rows == index, 1.0, 0.0).astype(BF)
                    for slot in range(at, min(half, at + 8))
                ],
                0,
            )
            ref[at : at + 8] = dot(hits, sent).astype(BF).reshape((-1, rows, width))


def make_output(place, gene_range, gene_offset, middle, part, other, bias, w_proj, orders, genes):
    tok, width = middle.shape
    proj = w_proj.shape[1]
    owners = 1 << len(orders[0])
    rows = -(-genes // 16) * 16
    half = jax.ShapeDtypeStruct((owners // 2, rows, proj), BF)
    return pl.pallas_call(
        functools.partial(output_kernel, orders),
        in_specs=[SM] + [VM] * 7,
        out_shape=(jax.ShapeDtypeStruct((tok, width), BF), half, half),
        compiler_params=params(20 if owners <= 16 else 48),
        cost_estimate=cost(2 * tok * owners * genes * proj, 8000000),
        name="output",
    )(place, gene_range, gene_offset, middle, part, other, bias.reshape(1, -1), w_proj)


def fold_kernel(keep_ref, far_ref, token_ref, *outs):
    total = keep_ref[...].astype(F32) + far_ref[...].astype(F32)
    if len(outs) == 1:
        outs[0][...] = total
    else:
        half = total.shape[0] // 2
        outs[0][...] = total[:half].astype(BF)
        outs[1][...] = total[half:].astype(BF)


def fold(keep, far, token):
    slots, rows, columns = keep.shape
    if slots == 1:
        out = (jax.ShapeDtypeStruct((1, rows, columns), F32),)
    else:
        out = (jax.ShapeDtypeStruct((slots // 2, rows, columns), BF),) * 2
    return pl.pallas_call(
        fold_kernel,
        in_specs=[VM, VM, pl.BlockSpec(memory_space=pl.ANY)],
        out_shape=out,
        compiler_params=params(16 if slots <= 8 else 48),
        cost_estimate=cost(keep.size, 6 * keep.size),
        name="fold",
    )(keep, far, token)
ORDERS = {
    "dense": ("zyxw", "xzyw"),
    "down": ("yzwx", "xywz"),
    "up": ("xzyw", "zxyw"),
    "early": ("zyxw", "yxzw"),
    "late": ("yzxw", "xzyw"),
}
ADDS = {
    "output": [],
    "sent": [],
    "feed_back": [],
    "down": [],
    "up": [],
    "back_first": ["dense"],
    "early": [],
    "back_rest": ["down"],
    "late": [],
    "last": [
        "up", "early", "dense", "small", "down", "late", "up", "early", "small", "dense", "up", "down",
        "late", "early", "late", "up", "down", "small", "early", "dense", "late", "small",
    ],
}


def dp_swap(value, bits):
    size = lax.axis_size("dp")
    pairs = [(2 * i + core, 2 * (i ^ (1 << bits[core])) + core) for i in range(size) for core in range(2)]
    return lax.ppermute(value, ("dp", "mp"), pairs)


def mp_swap(value):
    return lax.ppermute(value, "mp", [(0, 1), (1, 0)])


def slot_offsets(order):
    bits = len(order)
    return [
        sum(((s >> (bits - 1 - place)) & 1) << bit for place, bit in enumerate(order))
        for s in range(1 << bits)
    ]


def chunks_of(left, right, orders):
    offsets = [slot_offsets(order) for order in orders]
    size = len(offsets[0])
    grad = lax.dot_general(left, right, (((0,), (0,)), ((), ())), preferred_element_type=F32)
    chosen = jnp.asarray(offsets, jnp.int32)[lax.axis_index("mp")] ^ lax.axis_index("dp")
    slots = jnp.take(grad.astype(BF).reshape(size, -1, grad.shape[1]), chosen, axis=0)
    return slots[: size // 2], slots[size // 2 :]


def tie(value, *others):
    return lax.optimization_barrier((value,) + others)[0]


class Scatter:
    def __init__(self, orders):
        self.orders = orders
        self.step = 0

    def send(self, keep, send):
        self.keep = keep
        self.flight = dp_swap(send, [order[self.step] for order in self.orders])

    def add(self, token):
        self.step += 1
        out = fold(self.keep, self.flight, token)
        if len(out) == 2:
            self.send(*out)
        else:
            self.result = out[0][0]
        return out[0]


class Total:
    def __init__(self, bits):
        self.bits = list(range(bits))

    def send(self, value):
        self.result = value
        if self.bits:
            bit = self.bits.pop()
            self.flight = dp_swap(value, [bit, bit])

    def add(self, token):
        self.send(tie(self.result, token) + self.flight)
        return self.result


def scatter_plan(bits):
    if bits == 4:
        orders, adds = ORDERS, ADDS
        return {name: [["xyzw".index(axis) for axis in one] for one in pair] for name, pair in orders.items()}, adds
    one = list(range(bits))
    adds = {name: [] for name in ADDS}
    adds["last"] = [name for _ in one for name in list(ORDERS) + ["small"]]
    return {name: [one, one[1:-1] + [0, bits - 1]] for name in ORDERS}, adds


def per_device(
    tokens,
    cell_ids,
    gene_range,
    gene_offset,
    gain1,
    shift1,
    w_qkv,
    w_out,
    out_bias,
    gain2,
    shift2,
    w_up,
    up_bias,
    w_down,
    down_bias,
    w_proj,
    zero_embed,
    dense_cot,
):
    owners = lax.axis_size("dp")
    bits = owners.bit_length() - 1
    place = jnp.stack([lax.axis_index("dp"), lax.axis_index("mp")])
    genes = zero_embed.shape[0]
    orders, adds = scatter_plan(bits)
    parts = {name: Scatter(pair) for name, pair in orders.items()}
    parts["small"] = Total(bits)
    gene_range, gene_offset = gene_range.reshape(1, -1), gene_offset.reshape(1, -1)

    def service(event, token):
        for name in adds[event]:
            token = parts[name].add(token)
        return token

    spread = list(range(bits))[::-1]
    gather = [spread, spread[:-2] + [spread[-1], spread[-2]]]
    payload = make_payload(gene_range, gene_offset, dense_cot, owners)[None]
    steps = [[order[step] for order in gather] for step in range(bits)]
    far = dp_swap(payload, steps[0])
    out_other = mp_swap(w_out)
    proj_other = mp_swap(w_proj)
    normed1, q, k, v = make_qkv(tie(tokens, payload), jnp.stack([gain1, shift1]), w_qkv)
    held = jnp.concatenate([payload, tie(far, q)])
    for step in range(1, bits - 2):
        far = dp_swap(held, steps[step])
        if step < bits - 3:
            held = jnp.concatenate([held, far])
    mixed, lse = make_attend(cell_ids, tie(q, held), k, v)
    mixed_other = mp_swap(mixed)
    held = jnp.concatenate([held, tie(far, mixed)])
    far = dp_swap(held, steps[-2])
    middle, normed2, act, slope = make_middle(
        tie(tokens, held), mixed, mixed_other, w_out, out_other, out_bias, gain2, shift2, w_up, up_bias
    )
    held = jnp.concatenate([held, tie(far, normed2)])
    far = dp_swap(held, steps[-1])
    feed_part = make_feed(tie(act, held), w_down)
    feed_other = mp_swap(feed_part)
    dense_part = parts["dense"]
    block_out, dense_keep, dense_send = make_output(
        place, gene_range, gene_offset, middle, feed_part, feed_other, down_bias, w_proj, dense_part.orders, genes
    )
    dense_part.send(dense_keep, dense_send)
    token = service("output", block_out)
    grad_sent, grad_zero, divisor = make_sent(
        place, gene_range, gene_offset, held, tie(far, token), genes, gather
    )
    sent_other = mp_swap(grad_sent)
    token = service("sent", grad_sent)
    grad_result, grad_hidden, part2, grad_down_bias, grad_up_bias = make_feed_back(
        tie(grad_sent, token), sent_other, w_proj, proj_other, slope, w_down, w_up
    )
    other2 = mp_swap(part2)
    token = service("feed_back", part2)
    down = make_weight(place, [(tie(grad_result, token), (act,))], parts["down"].orders)
    parts["down"].send(*down)
    token = service("down", down[0])
    up = make_weight(place, [(normed2, (tie(grad_hidden, token),))], parts["up"].orders)
    parts["up"].send(*up)
    token = service("up", up[0])
    (
        grad_middle, low, grad_gain2, grad_shift2, grad_out_bias, gq, gk, gv, part1,
    ) = make_back_first(
        cell_ids, grad_result, tie(part2, token), other2, middle, gain2, w_out, q, k, v, lse, w_qkv
    )
    token = service("back_first", low)
    early = make_weight(
        place, [(normed1, (gq, gk, gv)), (tie(low, token), (mixed,)), (block_out, (grad_sent,))], parts["early"].orders
    )
    parts["early"].send(*early)
    token = service("early", early[0])
    gq2, gk2, gv2, part1 = make_back_rest(cell_ids, tie(low, token), part1, w_out, q, k, v, lse, w_qkv)
    other1 = mp_swap(part1)
    token = service("back_rest", gq2)
    late = make_weight(place, [(normed1, (tie(gq2, token), gk2, gv2))], parts["late"].orders)
    parts["late"].send(*late)
    token = service("late", late[0])
    grad_tokens, grad_gain1, grad_shift1 = make_last(tokens, tie(part1, token), other1, grad_middle, gain1)
    pieces = [
        grad_gain1,
        grad_shift1,
        grad_out_bias,
        grad_gain2,
        grad_shift2,
        grad_up_bias,
        grad_down_bias,
    ]
    parts["small"].send(jnp.concatenate(pieces, 1))
    token = service("last", grad_tokens)
    total = parts["small"].result

    pair, local = gq.shape[1], mixed.shape[1]
    early, late = parts["early"].result, parts["late"].result
    shares = [
        jnp.concatenate(
            [early[:, j * pair : (j + 1) * pair], late[:, j * (local - pair) : (j + 1) * (local - pair)]], 1
        )
        for j in range(3)
    ]
    share_wout = early[:, 3 * pair : 3 * pair + local]
    share_proj = early[:, 3 * pair + local :]
    share_up, share_down = parts["up"].result, parts["down"].result
    dense = (zero_embed.astype(F32) + dense_part.result[:genes]) / divisor
    small_sums, at = [], 0
    for piece in pieces:
        small_sums.append(total[0, at : at + piece.shape[1]])
        at += piece.shape[1]
    return (
        block_out,
        dense,
        grad_tokens,
        grad_zero,
        jnp.stack(shares),
        share_wout.T,
        share_up,
        share_down.T,
        share_proj,
    ) + tuple(small_sums)


def solution(mesh):
    in_specs = (
        P("dp", None),
        P("dp", None),
        P("dp", None),
        P("dp"),
        P(),
        P(),
        P(None, None, "mp"),
        P("mp", None),
        P(),
        P(),
        P(),
        P(None, "mp"),
        P("mp"),
        P("mp", None),
        P(),
        P(None, "mp"),
        P("dp", "mp"),
        P("dp", "mp"),
    )
    out_specs = (
        P("dp", None),
        P("dp", "mp"),
        P("dp", None),
        P("dp", "mp"),
        P(None, "dp", "mp"),
        P("mp", "dp"),
        P("dp", "mp"),
        P("mp", "dp"),
        P("dp", "mp"),
        P(),
        P(),
        P(),
        P(),
        P(),
        P("mp"),
        P(),
    )
    return jax.shard_map(
        per_device, mesh=mesh, in_specs=in_specs, out_specs=out_specs, check_vma=False
    )
```

```python
import functools
import jax
import jax.numpy as jnp
from jax import lax
from jax.experimental import pallas as pl
from jax.experimental.pallas import tpu as pltpu
from jax.sharding import PartitionSpec as P

HEAD_DIM = 64
EPSILON = 1e-05
BIG = 1e30
BF = jnp.bfloat16
F32 = jnp.float32
MIB = 1 << 20
SLOW, FAST = 1e8, 1e8

NT = (((1,), (1,)), ((), ()))


def dot(left, right):
    return jnp.dot(left, right, preferred_element_type=F32)


def dot_nt(left, right):
    return lax.dot_general(left, right, NT, preferred_element_type=F32)


def whole(shape):
    return pl.BlockSpec(shape, lambda *_: (0,) * len(shape))


VM = pl.BlockSpec(memory_space=pltpu.VMEM)
SM = pl.BlockSpec(memory_space=pltpu.SMEM)


def pick(place_ref, offsets, slot):
    first, second = offsets[0][slot], offsets[1][slot]
    if first == second:
        return first
    return first + place_ref[1] * (second - first)


def slot_of(place_ref, orders, owner):
    other = place_ref[0] ^ owner
    slots = []
    for order in orders:
        bits = len(order)
        slots.append(sum(((other >> bit) & 1) << (bits - 1 - spot) for spot, bit in enumerate(order)))
    return jnp.where(place_ref[1] == 0, slots[0], slots[1])


def params(mib=20):
    return pltpu.CompilerParams(vmem_limit_bytes=mib * MIB)


def cost(micros, rate=FAST):
    return pl.CostEstimate(flops=int(micros * rate), bytes_accessed=1, transcendentals=0)


def near(item):
    return pltpu.with_memory_space_constraint(item, pltpu.HBM)


HBM = pl.BlockSpec(memory_space=pltpu.HBM)


def fetch(pairs, sems):
    copies = [
        pltpu.make_async_copy(source, target, sems.at[i]) for i, (source, target) in enumerate(pairs)
    ]
    for copy in copies:
        copy.start()
    return copies


def line(ref):
    return ref[...].reshape(1, -1)


def norm_stats(values):
    centered = values - jnp.mean(values, -1, keepdims=True)
    inverse = lax.rsqrt(jnp.mean(centered * centered, -1, keepdims=True) + EPSILON)
    return centered * inverse, inverse


def norm_back(grad, normal, inverse, gain):
    scaled = grad * gain
    return inverse * (
        scaled
        - jnp.mean(scaled, -1, keepdims=True)
        - normal * jnp.mean(scaled * normal, -1, keepdims=True)
    )


def gene_rows(genes, owners):
    owners_pad = -(-owners // 16) * 16
    return -(-genes // owners_pad) * owners_pad, owners_pad


def payload_kernel(
    owners_pad, range_hbm, offset_hbm, cot_hbm, x_hbm, w_hbm, out_ref, x_ref, w_ref, range_ref, offset_ref, cot_ref, sems,
):
    copies = fetch(
        (
            (range_hbm, range_ref),
            (offset_hbm, offset_ref),
            (cot_hbm, cot_ref),
            (x_hbm, x_ref),
            (w_hbm, w_ref),
        ),
        sems,
    )
    for copy in copies[:3]:
        copy.wait()
    genes, width = cot_ref.shape
    tok = range_ref.shape[1]
    rows = out_ref.shape[0] - owners_pad
    cot = cot_ref[...].astype(F32)
    if rows > genes:
        cot = jnp.concatenate([cot, jnp.zeros((rows - genes, width), F32)], 0)
    out_ref[:rows, :] = cot.astype(BF)
    owner_hits = jnp.where(
        lax.broadcasted_iota(jnp.int32, (owners_pad, tok), 0) == range_ref[...], 1.0, 0.0
    ).astype(BF)
    offset_hits = jnp.where(
        lax.broadcasted_iota(jnp.int32, (width, tok), 0) == offset_ref[...], 1.0, 0.0
    ).astype(BF)
    out_ref[rows:, :] = dot_nt(owner_hits, offset_hits).astype(BF)
    for copy in copies[3:]:
        copy.wait()


def make_payload(gene_range, gene_offset, cot, tokens, w_qkv, owners):
    genes, width = cot.shape
    tok = gene_offset.shape[1]
    rows, owners_pad = gene_rows(genes, owners)
    operands = (gene_range, gene_offset, cot, tokens, w_qkv)
    return pl.pallas_call(
        functools.partial(payload_kernel, owners_pad),
        in_specs=[HBM] * 5,
        out_specs=[VM] * 3,
        out_shape=(
            jax.ShapeDtypeStruct((rows + owners_pad, width), BF),
            jax.ShapeDtypeStruct(tokens.shape, BF),
            jax.ShapeDtypeStruct(w_qkv.shape, BF),
        ),
        scratch_shapes=[
            pltpu.VMEM((1, tok), jnp.int32),
            pltpu.VMEM((1, tok), jnp.int32),
            pltpu.VMEM((genes, width), BF),
            pltpu.SemaphoreType.DMA((5,)),
        ],
        compiler_params=params(),
        cost_estimate=cost(1.8, SLOW),
        name="payload",
    )(*map(near, operands))


def join_kernel(near_ref, far_ref, out_ref):
    half = near_ref.shape[0]
    out_ref[:half] = near_ref[...]
    out_ref[half:] = far_ref[...]


def join(near, far):
    return pl.pallas_call(
        join_kernel,
        in_specs=[VM, VM],
        out_shape=jax.ShapeDtypeStruct((2 * near.shape[0],) + near.shape[1:], near.dtype),
        compiler_params=params(16 if near.shape[0] < 8 else 32),
        cost_estimate=cost(0.4, SLOW),
        name="join",
    )(near, far)


def sent_kernel(genes, orders, count, place_ref, range_hbm, offset_hbm, *refs):
    range_ref, offset_ref, sems = refs[-3:]
    refs = refs[:-3]
    hist_refs, held_refs = refs[:count], refs[count : 2 * count]
    sent_ref, zero_ref, div_ref, total, by_gene, low = refs[2 * count :]
    batch, rows, width = held_refs[0].shape
    size, owners_pad, _ = hist_refs[0].shape
    step = pl.program_id(0)
    me = place_ref[0]
    tok = range_ref.shape[1]

    @pl.when(step == 0)
    def _():
        copies = fetch(((range_hbm, range_ref), (offset_hbm, offset_ref)), sems)
        counts = jnp.zeros((owners_pad, width), F32)
        for ref in hist_refs:
            for slot in range(size):
                counts += ref[slot].astype(F32)
        if owners_pad < 128:
            counts = jnp.concatenate([counts, jnp.zeros((128 - owners_pad, width), F32)], 0)
        by_gene[...] = 1.0 + counts.T[:rows]
        total[...] = jnp.zeros_like(total)
        for copy in copies:
            copy.wait()

    spread = by_gene[...]
    owner_lane = lax.broadcasted_iota(jnp.int32, spread.shape, 1)
    other = range_ref[...] ^ me
    slots = [
        sum(((other >> bit) & 1) << spot for spot, bit in enumerate(order)) for order in orders
    ]
    slots = jnp.where(place_ref[1] == 0, slots[0], slots[1])
    side = slots // size
    near = slots - side * size - step * batch
    index = jnp.where((near >= 0) & (near < batch), (side * batch + near) * rows + offset_ref[...], -1)
    columns = jnp.broadcast_to(index, (128, tok)).T
    for side, ref in enumerate(held_refs):
        for spot in range(batch):
            slot = side * size + step * batch + spot
            offset = jnp.int32(0)
            for core, order in enumerate(orders):
                one = sum(((slot >> i) & 1) << bit for i, bit in enumerate(order))
                offset = jnp.where(place_ref[1] == core, one, offset)
            divisor = jnp.sum(jnp.where(owner_lane == (me ^ offset), spread, 0.0), 1, keepdims=True)
            grad = ref[spot].astype(F32) * (1.0 / divisor)
            if spot == 0 and side == 0:

                @pl.when(step == 0)
                def _():
                    zero_ref[...] = grad[:genes]
                    div_ref[...] = jnp.broadcast_to(divisor[:genes], (genes, width))

            at = (side * batch + spot) * rows
            low[at : at + rows, :] = grad.astype(BF)
    lane = lax.broadcasted_iota(jnp.int32, (tok, 128), 1)
    hits = jnp.concatenate(
        [
            jnp.where(columns == lane + at, 1.0, 0.0).astype(BF)
            for at in range(0, count * batch * rows, 128)
        ],
        1,
    )
    total[...] += dot(hits, low[...])

    @pl.when(step == pl.num_programs(0) - 1)
    def _():
        sent_ref[...] = total[...].astype(BF)


def make_sent(place, gene_range, gene_offset, held, genes, orders):
    size, height, width = held[0].shape
    count = len(held)
    owners = count * size
    rows, owners_pad = gene_rows(genes, owners)
    batch = min(size, 4)
    tok = gene_offset.shape[1]
    hist = pl.BlockSpec((size, owners_pad, width), lambda i: (0, rows // owners_pad, 0))
    cots = pl.BlockSpec((batch, rows, width), lambda i: (i, 0, 0))
    return pl.pallas_call(
        functools.partial(sent_kernel, genes, orders, count),
        grid=(size // batch,),
        in_specs=[SM, HBM, HBM] + [hist] * count + [cots] * count,
        out_specs=(whole((tok, width)), whole((genes, width)), whole((genes, width))),
        out_shape=(
            jax.ShapeDtypeStruct((tok, width), BF),
            jax.ShapeDtypeStruct((genes, width), F32),
            jax.ShapeDtypeStruct((genes, width), F32),
        ),
        scratch_shapes=[
            pltpu.VMEM((tok, width), F32),
            pltpu.VMEM((rows, 128 * -(-owners // 128)), F32),
            pltpu.VMEM((count * batch * rows, width), BF),
            pltpu.VMEM((1, tok), jnp.int32),
            pltpu.VMEM((1, tok), jnp.int32),
            pltpu.SemaphoreType.DMA((2,)),
        ],
        compiler_params=params(20 if owners <= 16 else 48),
        cost_estimate=cost(2.5, SLOW),
        name="grad_sent",
    )(place, near(gene_range), near(gene_offset), *held, *held)


def qkv_kernel(x_ref, gain_ref, shift_ref, w_ref, normed_ref, q_ref, k_ref, v_ref):
    normal, _ = norm_stats(x_ref[...].astype(F32))
    normed = (normal * line(gain_ref) + line(shift_ref)).astype(BF)
    normed_ref[...] = normed
    for j, out in enumerate((q_ref, k_ref, v_ref)):
        out[...] = dot(normed, w_ref[j]).astype(BF)


def make_qkv(tokens, gain, shift, w_qkv):
    tok, width = tokens.shape
    local = w_qkv.shape[2]
    one = jax.ShapeDtypeStruct((tok, local), BF)
    return pl.pallas_call(
        qkv_kernel,
        in_specs=[VM] * 4,
        out_shape=(jax.ShapeDtypeStruct((tok, width), BF), one, one, one),
        compiler_params=params(),
        cost_estimate=cost(1.7, SLOW),
        name="qkv",
    )(tokens, gain, shift, w_qkv)


def masked_pair(q_pair, k_pair, cells, half, cell_count=8):
    lane = lax.broadcasted_iota(jnp.int32, q_pair.shape, 1)
    own = (lane // HEAD_DIM) == half
    place = lane % HEAD_DIM
    same = place == cells
    q_mask = jnp.where((place < cell_count) & jnp.logical_not(same), -BIG, 0.0)
    k_mask = jnp.where(same, 1.0, 0.0)
    scaled = q_pair.astype(F32) * (HEAD_DIM**-0.5)
    q_head = jnp.where(own, scaled, q_mask).astype(BF)
    k_head = jnp.where(own, k_pair.astype(F32), k_mask).astype(BF)
    return q_head, k_head


def attend_kernel(
    cells_ref, q_ref, k_ref, v_ref, normed_ref, upper_ref, lower_ref, lse_ref, q_far, k_far, v_far, normed_far, sems,
):
    copies = fetch(((q_ref, q_far), (k_ref, k_far), (v_ref, v_far), (normed_ref, normed_far)), sems)
    tok, local = q_ref.shape
    half_tok = tok // 2
    cells = jnp.broadcast_to(cells_ref[...], (128, tok)).T
    lane = lax.broadcasted_iota(jnp.int32, (tok, 128), 1)
    logs = jnp.zeros((tok, 128), F32)
    for pair in range(local // 128):
        cut = slice(pair * 128, pair * 128 + 128)
        q_pair, k_pair, v_pair = q_ref[:, cut], k_ref[:, cut], v_ref[:, cut]
        heads = []
        for half in range(2):
            q_head, k_head = masked_pair(q_pair, k_pair, cells, half)
            scores = dot_nt(q_head, k_head)
            top = jnp.max(scores, 1, keepdims=True)
            powers = jnp.exp(scores - top)
            total = jnp.sum(powers, 1, keepdims=True)
            probs = (powers * (1.0 / total)).astype(BF)
            logs = jnp.where(lane == 2 * pair + half, top + jnp.log(total), logs)
            heads.append(dot(probs, v_pair))
        mixed = jnp.where(lane < HEAD_DIM, heads[0], heads[1]).astype(BF)
        upper_ref[:, cut] = mixed[:half_tok]
        lower_ref[:, cut] = mixed[half_tok:]
    lse_ref[...] = logs.T[: lse_ref.shape[0]]
    for copy in copies:
        copy.wait()


def make_attend(cell_ids, q, k, v, normed):
    tok, local = q.shape
    heads = -(-local // HEAD_DIM // 8) * 8
    half = jax.ShapeDtypeStruct((tok // 2, local), BF)
    return pl.pallas_call(
        attend_kernel,
        in_specs=[VM] * 5,
        out_specs=[VM] * 3 + [HBM] * 4,
        out_shape=(
            half,
            half,
            jax.ShapeDtypeStruct((heads, tok), F32),
            *(pltpu.HBM(item.shape, BF) for item in (q, k, v, normed)),
        ),
        scratch_shapes=[pltpu.SemaphoreType.DMA((4,))],
        compiler_params=params(),
        cost_estimate=cost(2.9, SLOW),
        name="attend",
    )(cell_ids, q, k, v, normed)


def pair_back(cells, q_pair, k_pair, v_pair, gm_pair, lse, lane):
    factor = HEAD_DIM**-0.5
    k_turned = k_pair.astype(F32).T.astype(BF)
    gq_halves = []
    gk = gv = None
    for half in range(2):
        own = (lane // HEAD_DIM) == half
        q_head, k_head = masked_pair(q_pair, k_pair, cells, half)
        v_head = jnp.where(own, v_pair.astype(F32), 0.0).astype(BF)
        probs = jnp.exp(dot_nt(k_head, q_head) - lse[half : half + 1])
        part = dot(probs.astype(BF), gm_pair)
        gv = part if half == 0 else jnp.where(own, part, gv)
        grad_probs = dot_nt(v_head, gm_pair)
        spread = jnp.sum(probs * grad_probs, 0, keepdims=True)
        grad_scores = (probs * (grad_probs - spread)).astype(BF)
        part = dot(grad_scores, q_pair)
        gk = part if half == 0 else jnp.where(own, part, gk)
        gq_halves.append(dot(k_turned[half * HEAD_DIM : (half + 1) * HEAD_DIM], grad_scores))
    gq = (jnp.concatenate(gq_halves, 0).T * factor).astype(BF)
    return gq, (gk * factor).astype(BF), gv.astype(BF)


GELU_A = 0.7978845608028654
GELU_B = 0.044715


def middle_kernel(
    x_ref, own_upper_ref, own_lower_ref, upper_ref, lower_ref, wo_ref, wo_other_ref, bias_ref, gain_ref, shift_ref,
    middle_ref, normed_ref,
):
    own = jnp.concatenate([own_upper_ref[...], own_lower_ref[...]], 0)
    other = jnp.concatenate([upper_ref[...], lower_ref[...]], 0)
    attended = dot(own, wo_ref[...]) + dot(other, wo_other_ref[...])
    middle = x_ref[...].astype(F32) + attended + line(bias_ref)
    middle_ref[...] = middle
    normal, _ = norm_stats(middle)
    normed_ref[...] = (normal * line(gain_ref) + line(shift_ref)).astype(BF)


def make_middle(tokens, mixed, mixed_other, w_out, out_other, out_bias, gain, shift):
    tok, width = tokens.shape
    return pl.pallas_call(
        middle_kernel,
        in_specs=[VM] * 10,
        out_shape=(jax.ShapeDtypeStruct((tok, width), F32), jax.ShapeDtypeStruct((tok, width), BF)),
        compiler_params=params(),
        cost_estimate=cost(1.4, SLOW),
        name="middle",
    )(tokens, *mixed, *mixed_other, w_out, out_other, out_bias, gain, shift)


def feed_kernel(
    chunk, normed_ref, middle_ref, up_ref, up_bias_ref, down_ref,
    *refs,
):
    quarters, (act_far, slope_far, middle_far, act_ref, slope_ref, sems) = refs[:4], refs[4:]
    copies = fetch(((middle_ref, middle_far),), sems)
    normed = normed_ref[...]
    up_bias = line(up_bias_ref)
    units = up_ref.shape[1]
    for place, at in enumerate(range(0, units, chunk)):
        cut = slice(at, at + chunk)
        hidden = dot(normed, up_ref[:, cut]) + up_bias[:, cut]
        square = hidden * hidden
        curve = jnp.tanh(hidden * (GELU_A + (GELU_A * GELU_B) * square))
        half = 0.5 * hidden
        act_ref[:, cut] = (half + half * curve).astype(BF)
        slope = (0.5 + 0.5 * curve) + half * (1.0 - curve * curve) * (
            GELU_A + (3 * GELU_A * GELU_B) * square
        )
        slope_ref[:, cut] = slope.astype(BF)
        copies += fetch(
            ((act_ref.at[:, cut], act_far.at[:, cut]), (slope_ref.at[:, cut], slope_far.at[:, cut])),
            sems.at[pl.ds(1 + 2 * place, 2)],
        )
    feed = dot(act_ref[...], down_ref[...]).astype(BF)
    for place, ref in enumerate(quarters):
        ref[...] = feed[place * ref.shape[0] : (place + 1) * ref.shape[0]]
    for copy in copies:
        copy.wait()


def make_feed(normed, middle, w_up, up_bias, w_down, chunk=768):
    tok, width = normed.shape
    units = w_up.shape[1]
    return pl.pallas_call(
        functools.partial(feed_kernel, chunk),
        in_specs=[VM] * 5,
        out_specs=[VM] * 4 + [HBM] * 3,
        out_shape=(
            *(jax.ShapeDtypeStruct((tok // 4, width), BF) for _ in range(4)),
            pltpu.HBM((tok, units), BF),
            pltpu.HBM((tok, units), BF),
            pltpu.HBM((tok, width), F32),
        ),
        scratch_shapes=[
            pltpu.VMEM((tok, units), BF),
            pltpu.VMEM((tok, units), BF),
            pltpu.SemaphoreType.DMA((1 + 2 * units // chunk,)),
        ],
        compiler_params=params(24),
        cost_estimate=cost(4.1, SLOW),
        name="feed",
    )(normed, middle, w_up, up_bias, w_down)


def result_kernel(
    orders, place_ref, sent_ref, other_ref, wp_ref, wp_other_ref, act_ref,
    result_ref, bias_ref, keep_ref, send_ref, chosen,
):
    size, chunk, tok = chosen.shape
    half = size // 2 * chunk
    result = dot_nt(sent_ref[...], wp_ref[...]) + dot_nt(other_ref[...], wp_other_ref[...])
    low = result.astype(BF)
    result_ref[...] = low
    bias_ref[...] = jnp.sum(low.astype(F32), 0, keepdims=True)
    turned = low.astype(F32).T.astype(BF).reshape(chosen.shape)
    for owner in range(size):
        chosen[slot_of(place_ref, orders, owner)] = turned[owner]
    for at in range(0, act_ref.shape[1], 512):
        cut = slice(at, at + 512)
        right = act_ref[:, cut]
        out = (size // 2, chunk, right.shape[1])
        keep_ref[:, :, cut] = dot(chosen[: size // 2].reshape(half, tok), right).astype(BF).reshape(out)
        send_ref[:, :, cut] = dot(chosen[size // 2 :].reshape(half, tok), right).astype(BF).reshape(out)


def plain_result_kernel(sent_ref, other_ref, wp_ref, wp_other_ref, result_ref, bias_ref):
    result = dot_nt(sent_ref[...], wp_ref[...]) + dot_nt(other_ref[...], wp_other_ref[...])
    low = result.astype(BF)
    result_ref[...] = low
    bias_ref[...] = jnp.sum(low.astype(F32), 0, keepdims=True)


def make_result(index, sent, sent_other, w_proj, proj_other, act, orders):
    tok = sent.shape[0]
    width = w_proj.shape[0]
    units = act.shape[1]
    size = 1 << len(orders[0])
    chunk = width // size
    outs = (jax.ShapeDtypeStruct((tok, width), BF), jax.ShapeDtypeStruct((1, width), F32))
    if chunk % 16:
        result, bias = pl.pallas_call(
            plain_result_kernel, in_specs=[VM] * 4, out_shape=outs, compiler_params=params(), name="result"
        )(sent, sent_other, w_proj, proj_other)
        return result, bias, make_weight(index, [(result, (act,))], orders)
    half = jax.ShapeDtypeStruct((size // 2, chunk, units), BF)
    result, bias, keep, send = pl.pallas_call(
        functools.partial(result_kernel, orders),
        in_specs=[SM] + [VM] * 5,
        out_shape=(*outs, half, half),
        scratch_shapes=[pltpu.VMEM((size, chunk, tok), BF)],
        compiler_params=params(),
        cost_estimate=cost(3.7, SLOW),
        name="result",
    )(index, sent, sent_other, w_proj, proj_other, act)
    return result, bias, (keep, send)


def feed_back_kernel(
    chunk, result_ref, slope_ref, down_ref, up_ref, hidden_ref, normed_ref, upper_ref, lower_ref, up_bias_ref
):
    low = result_ref[...]
    for at in range(0, up_ref.shape[1], chunk):
        cut = slice(at, at + chunk)
        grad = (dot_nt(low, down_ref[cut]) * slope_ref[:, cut].astype(F32)).astype(BF)
        hidden_ref[:, cut] = grad
        up_bias_ref[:, cut] = jnp.sum(grad.astype(F32), 0, keepdims=True)
    normed = dot_nt(hidden_ref[...], up_ref[...]).astype(BF)
    normed_ref[...] = normed
    half = upper_ref.shape[0]
    upper_ref[...] = normed[:half]
    lower_ref[...] = normed[half:]


def make_feed_back(result, slope, w_down, w_up, chunk=768):
    tok, width = result.shape
    units = w_up.shape[1]
    return pl.pallas_call(
        functools.partial(feed_back_kernel, chunk),
        in_specs=[VM] * 4,
        out_shape=(
            jax.ShapeDtypeStruct((tok, units), BF),
            jax.ShapeDtypeStruct((tok, width), BF),
            jax.ShapeDtypeStruct((tok // 2, width), BF),
            jax.ShapeDtypeStruct((tok // 2, width), BF),
            jax.ShapeDtypeStruct((1, units), F32),
        ),
        compiler_params=params(24),
        cost_estimate=cost(2.8),
        name="feed_back",
    )(result, slope, w_down, w_up)


def turn_kernel(orders, place_ref, left_ref, out_ref):
    turned = left_ref[...].astype(F32).T.astype(BF).reshape(out_ref.shape)
    for owner in range(out_ref.shape[0]):
        out_ref[slot_of(place_ref, orders, owner)] = turned[owner]


def make_turned(index, left, orders):
    tok, width = left.shape
    size = 1 << len(orders[0])
    if width // size % 16:
        return left
    return pl.pallas_call(
        functools.partial(turn_kernel, orders),
        in_specs=[SM, VM],
        out_shape=jax.ShapeDtypeStruct((size, width // size, tok), BF),
        compiler_params=params(),
        cost_estimate=cost(0.9, SLOW),
        name="turn",
    )(index, left)


def turned_kernel(chosen_ref, right_ref, keep_ref, send_ref):
    size, chunk, tok = chosen_ref.shape
    half = size // 2 * chunk
    for at in range(0, right_ref.shape[1], 512):
        cut = slice(at, at + 512)
        right = right_ref[:, cut]
        out = (size // 2, chunk, right.shape[1])
        keep_ref[:, :, cut] = dot(chosen_ref[: size // 2].reshape(half, tok), right).astype(BF).reshape(out)
        send_ref[:, :, cut] = dot(chosen_ref[size // 2 :].reshape(half, tok), right).astype(BF).reshape(out)


def make_turned_weight(index, left, right, orders):
    if left.ndim == 2:
        return make_weight(index, [(left, (right,))], orders)
    size, chunk, _ = left.shape
    out = jax.ShapeDtypeStruct((size // 2, chunk, right.shape[1]), BF)
    return pl.pallas_call(
        turned_kernel,
        in_specs=[VM, VM],
        out_shape=(out, out),
        compiler_params=params(),
        cost_estimate=cost(2.2),
        name="up_grad",
    )(left, right)


def weight_kernel(orders, groups, place_ref, *refs):
    ins = refs[: -2 - len(groups)]
    keep_ref, send_ref = refs[len(ins) : len(ins) + 2]
    size, chunk, tok = refs[-1].shape
    half = size // 2 * chunk
    at = place = 0
    for count, chosen in zip(groups, refs[len(ins) + 2 :]):
        turned = ins[place][...].astype(F32).T.astype(BF).reshape(chosen.shape)
        for owner in range(size):
            chosen[slot_of(place_ref, orders, owner)] = turned[owner]
        rights = [ref[...] for ref in ins[place + 1 : place + 1 + count]]
        if rights[0].shape[0] < tok:
            rights = [jnp.concatenate(rights, 0)]
        for right in rights:
            cut = slice(at, at + right.shape[1])
            out = (size // 2, chunk, right.shape[1])
            keep_ref[:, :, cut] = dot(chosen[: size // 2].reshape(half, tok), right).astype(BF).reshape(out)
            send_ref[:, :, cut] = dot(chosen[size // 2 :].reshape(half, tok), right).astype(BF).reshape(out)
            at += right.shape[1]
        place += 1 + count


def make_weight(index, pairs, orders):
    tok, width = pairs[0][0].shape
    columns = sum(right.shape[1] * right.shape[0] for _, rights in pairs for right in rights) // tok
    size = 1 << len(orders[0])
    chunk = width // size
    if chunk % 16:
        pairs = [
            (left, (jnp.concatenate(rights),) if rights[0].shape[0] < tok else rights) for left, rights in pairs
        ]
        parts = [chunks_of(left, right, orders) for left, rights in pairs for right in rights]
        return tuple(jnp.concatenate(side, 2) for side in zip(*parts))
    out = jax.ShapeDtypeStruct((size // 2, chunk, columns), BF)
    flat = [item for left, rights in pairs for item in (left, *rights)]
    return pl.pallas_call(
        functools.partial(weight_kernel, orders, [len(rights) for _, rights in pairs]),
        in_specs=[SM] + [VM] * len(flat),
        out_shape=(out, out),
        scratch_shapes=[pltpu.VMEM((size, chunk, tok), BF) for _ in pairs],
        compiler_params=params(),
        cost_estimate=cost(2.2),
        name="weight_grad",
    )(index, *flat)


def norm2_kernel(
    result_ref, part_ref, upper_ref, lower_ref, middle_ref, gain_ref,
    grad_middle_ref, low_ref, gain_sum_ref, shift_sum_ref, bias_sum_ref,
):
    other = jnp.concatenate([upper_ref[...], lower_ref[...]], 0)
    grad = part_ref[...].astype(F32) + other.astype(F32)
    normal, inverse = norm_stats(middle_ref[...])
    gain_sum_ref[...] = jnp.sum(grad * normal, 0, keepdims=True)
    shift_sum_ref[...] = jnp.sum(grad, 0, keepdims=True)
    middle = result_ref[...].astype(F32) + norm_back(grad, normal, inverse, line(gain_ref))
    grad_middle_ref[...] = middle
    bias_sum_ref[...] = jnp.sum(middle, 0, keepdims=True)
    low_ref[...] = middle.astype(BF)


def make_norm2(result, part, other, middle, gain):
    tok, width = middle.shape
    small = jax.ShapeDtypeStruct((1, width), F32)
    return pl.pallas_call(
        norm2_kernel,
        in_specs=[VM] * 6,
        out_shape=(
            jax.ShapeDtypeStruct((tok, width), F32), jax.ShapeDtypeStruct((tok, width), BF), small, small, small
        ),
        compiler_params=params(),
        cost_estimate=cost(2.4),
        name="norm2",
    )(result, part, *other, middle, gain)


def back_kernel(
    cells_ref, low_ref, x_ref, wo_ref, q_ref, k_ref, v_ref, lse_ref, w_ref, gq_ref, gk_ref, gv_ref, normed_ref, sums_ref,
):
    tok = q_ref.shape[0]
    cells = jnp.broadcast_to(cells_ref[...], (128, tok)).T
    lane = lax.broadcasted_iota(jnp.int32, (tok, 128), 1)
    gm = dot_nt(low_ref[...], wo_ref[...]).astype(BF)
    for pair in range(q_ref.shape[1] // 128):
        cut = slice(pair * 128, pair * 128 + 128)
        out = pair_back(
            cells, q_ref[:, cut], k_ref[:, cut], v_ref[:, cut], gm[:, cut], lse_ref[2 * pair : 2 * pair + 2], lane
        )
        for ref, value in zip((gq_ref, gk_ref, gv_ref), out):
            ref[:, cut] = value
    total = dot_nt(gq_ref[...], w_ref[0]) + dot_nt(gk_ref[...], w_ref[1]) + dot_nt(gv_ref[...], w_ref[2])
    normal, _ = norm_stats(x_ref[...].astype(F32))
    sums_ref[0:1] = jnp.sum(total * normal, 0, keepdims=True)
    sums_ref[1:2] = jnp.sum(total, 0, keepdims=True)
    normed_ref[...] = total.astype(BF)


def make_back(cell_ids, low, tokens, w_out, q, k, v, lse, w_qkv):
    tok, local = q.shape
    width = low.shape[1]
    one = jax.ShapeDtypeStruct((tok, local), BF)
    return pl.pallas_call(
        back_kernel,
        in_specs=[VM] * 9,
        out_shape=(
            one, one, one, jax.ShapeDtypeStruct((tok, width), BF), jax.ShapeDtypeStruct((2, width), F32)
        ),
        compiler_params=params(),
        cost_estimate=cost(6.4),
        name="back",
    )(cell_ids, low, tokens, w_out, q, k, v, lse, w_qkv)


def last_kernel(x_ref, part_ref, other_ref, middle_ref, gain_ref, out_hbm, out_ref, sems):
    half = x_ref.shape[0] // 2
    cuts = [pl.ds(place * half, half) for place in range(2)]
    out = []
    for place, cut in enumerate(cuts):
        grad = part_ref[cut].astype(F32) + other_ref[cut].astype(F32)
        normal, inverse = norm_stats(x_ref[cut].astype(F32))
        grad = norm_back(grad, normal, inverse, line(gain_ref))
        out_ref[cut] = middle_ref[cut] + grad
        out += fetch([(out_ref.at[cut], out_hbm.at[cut])], sems.at[pl.ds(place, 1)])
    for copy in out:
        copy.wait()


def make_last(tokens, part, other, grad_middle, gain):
    tok, width = tokens.shape
    return pl.pallas_call(
        last_kernel,
        in_specs=[VM] * 5,
        out_specs=HBM,
        out_shape=pltpu.HBM((tok, width), F32),
        scratch_shapes=[pltpu.VMEM((tok, width), F32), pltpu.SemaphoreType.DMA((2,))],
        compiler_params=params(),
        cost_estimate=cost(2.3),
        name="last",
    )(tokens, part, other, grad_middle, gain)


def output_kernel(orders, place_ref, range_hbm, offset_hbm, bias_hbm, middle_hbm, *refs):
    own, other = refs[:4], refs[4:8]
    wp_ref, out_ref, keep_ref, send_ref, range_ref, offset_ref, bias_ref, middle_ref, hits, sems = refs[8:]
    copies = fetch(
        ((range_hbm, range_ref), (offset_hbm, offset_ref), (bias_hbm, bias_ref), (middle_hbm, middle_ref)), sems
    )
    half, rows, width = keep_ref.shape
    tok = range_ref.shape[1]
    for copy in copies[:2]:
        copy.wait()
    index = slot_of(place_ref, orders, range_ref[...]) * rows + offset_ref[...]
    gene = lax.broadcasted_iota(jnp.int32, (rows, tok), 0)
    batch = hits.shape[0] // rows

    def find(first):
        for spot in range(batch):
            hits[spot * rows : (spot + 1) * rows, :] = jnp.where(
                gene + (first + spot) * rows == index, 1.0, 0.0
            ).astype(BF)

    find(0)
    for copy in copies[2:]:
        copy.wait()
    feed = jnp.concatenate([left[...].astype(F32) + right[...].astype(F32) for left, right in zip(own, other)], 0)
    low = (middle_ref[...] + feed + line(bias_ref)).astype(BF)
    out_ref[...] = low
    sent = dot(low, wp_ref[...]).astype(BF)
    for first in range(0, 2 * half, batch):
        if first:
            find(first)
        ref = keep_ref if first < half else send_ref
        at = first % half
        ref[at : at + batch] = dot(hits[...], sent).astype(BF).reshape((batch, rows, width))


def make_output(place, gene_range, gene_offset, bias, middle, own, other, w_proj, orders, genes):
    tok, width = middle.shape
    proj = w_proj.shape[1]
    owners = 1 << len(orders[0])
    rows = -(-genes // 16) * 16
    half = jax.ShapeDtypeStruct((owners // 2, rows, proj), BF)
    return pl.pallas_call(
        functools.partial(output_kernel, orders),
        in_specs=[SM] + [HBM] * 4 + [VM] * 9,
        out_shape=(jax.ShapeDtypeStruct((tok, width), BF), half, half),
        scratch_shapes=[
            pltpu.VMEM((1, tok), jnp.int32),
            pltpu.VMEM((1, tok), jnp.int32),
            pltpu.VMEM((width,), F32),
            pltpu.VMEM((tok, width), F32),
            pltpu.VMEM((min(owners // 2, 8) * rows, tok), BF),
            pltpu.SemaphoreType.DMA((4,)),
        ],
        compiler_params=params(20 if owners <= 16 else 48),
        cost_estimate=cost(2.8, SLOW),
        name="output",
    )(place, near(gene_range), near(gene_offset), near(bias), near(middle), *own, *other, w_proj)


def fold_kernel(keep_ref, far_ref, new_keep_ref, send_ref):
    total = keep_ref[...].astype(F32) + far_ref[...].astype(F32)
    half = total.shape[0] // 2
    new_keep_ref[...] = total[:half].astype(BF)
    send_ref[...] = total[half:].astype(BF)


def last_fold_kernel(keep_ref, far_ref, out_hbm, out_ref, sems):
    out_ref[...] = (keep_ref[...].astype(F32) + far_ref[...].astype(F32))[0]
    for copy in fetch(((out_ref, out_hbm),), sems):
        copy.wait()


def fold(keep, far):
    slots, rows, columns = keep.shape
    if slots == 1:
        return pl.pallas_call(
            last_fold_kernel,
            in_specs=[VM, VM],
            out_specs=HBM,
            out_shape=pltpu.HBM((rows, columns), F32),
            scratch_shapes=[pltpu.VMEM((rows, columns), F32), pltpu.SemaphoreType.DMA((1,))],
            compiler_params=params(16),
            cost_estimate=cost(0.4),
            name="last_fold",
        )(keep, far)
    return pl.pallas_call(
        fold_kernel,
        in_specs=[VM, VM],
        out_shape=(jax.ShapeDtypeStruct((slots // 2, rows, columns), BF),) * 2,
        compiler_params=params(16 if slots <= 8 else 48),
        cost_estimate=cost(0.4),
        name="fold",
    )(keep, far)


def parted(value):
    high = value.astype(BF).astype(F32)
    return jnp.concatenate([high, value - high], 0).astype(BF)


def tail_kernel(orders, groups, vectors, place_ref, own_ref, other_ref, *refs):
    keep_ref, small_ref, send_ref, rest_ref = refs[-4 - len(groups) : -len(groups)]
    size, chunk, tok = refs[-1].shape
    half = size // 2 * chunk
    quarter = send_ref.shape[0]
    at = place = 0
    for count, chosen in zip(groups, refs[-len(groups) :]):
        turned = refs[place][...].astype(F32).T.astype(BF).reshape(chosen.shape)
        for owner in range(size):
            chosen[slot_of(place_ref, orders, owner)] = turned[owner]
        rights = [ref[...] for ref in refs[place + 1 : place + 1 + count]]
        if rights[0].shape[0] < tok:
            rights = [jnp.concatenate(rights, 0)]
        for right in rights:
            cut = slice(at, at + right.shape[1])
            out = (size // 2, chunk, right.shape[1])
            keep_ref[:, :, cut] = dot(chosen[: size // 2].reshape(half, tok), right).astype(BF).reshape(out)
            sent = dot(chosen[size // 2 :].reshape(half, tok), right).astype(BF)
            send_ref[:, cut] = sent[:quarter]
            rest_ref[: half - quarter, cut] = sent[quarter:]
            at += right.shape[1]
        place += 1 + count
    sums = own_ref[...] + other_ref[...]
    vector = sums.shape[1]
    per_row = small_ref.shape[1] // vector
    pieces = [sums[0:1], sums[1:2]]
    for ref in refs[place : place + vectors]:
        pieces += [ref[:, start : start + vector] for start in range(0, ref.shape[1], vector)]
    small_ref[...] = jnp.zeros_like(small_ref)
    for spot, piece in enumerate(pieces):
        row, column = spot // per_row, spot % per_row * vector
        small_ref[row : row + 1, column : column + vector] = piece
    rest_ref[half - quarter :, :] = parted(small_ref[...])


def make_tail(index, pairs, own, other, sums, orders):
    tok, width = pairs[0][0].shape
    columns = sum(right.shape[1] * right.shape[0] for _, rights in pairs for right in rights) // tok
    size = 1 << len(orders[0])
    chunk = width // size
    flat = [item for left, rights in pairs for item in (left, *rights)]
    return pl.pallas_call(
        functools.partial(tail_kernel, orders, [len(rights) for _, rights in pairs], len(sums)),
        in_specs=[SM] + [VM] * (2 + len(flat) + len(sums)),
        out_shape=(
            jax.ShapeDtypeStruct((size // 2, chunk, columns), BF),
            jax.ShapeDtypeStruct((8, columns), F32),
            jax.ShapeDtypeStruct((size // 4 * chunk, columns), BF),
            jax.ShapeDtypeStruct((size // 4 * chunk + 16, columns), BF),
        ),
        scratch_shapes=[pltpu.VMEM((size, chunk, tok), BF) for _ in pairs],
        compiler_params=params(),
        cost_estimate=cost(2.9),
        name="tail_grad",
    )(index, own, other, *flat, *sums)


def late_sums(keep_ref, small_ref, far_refs):
    slots, chunk, columns = keep_ref.shape
    count = slots * chunk
    far = jnp.concatenate([ref[...] for ref in far_refs], 0)
    total = keep_ref[...].astype(F32) + far[:count].astype(F32).reshape(keep_ref.shape)
    extra = far[count:].astype(F32)
    return total, small_ref[...] + extra[:8] + extra[8:]


def late_fold_kernel(keep_ref, small_ref, *refs):
    far_refs, (new_keep_ref, new_small_ref, send_ref) = refs[:-3], refs[-3:]
    total, small = late_sums(keep_ref, small_ref, far_refs)
    half, chunk, columns = new_keep_ref.shape
    new_keep_ref[...] = total[:half].astype(BF)
    new_small_ref[...] = small
    send_ref[: half * chunk, :] = total[half:].reshape(half * chunk, columns).astype(BF)
    send_ref[half * chunk :, :] = parted(small)


def late_fold(keep, small, far):
    slots, chunk, columns = keep.shape
    half = slots // 2
    return pl.pallas_call(
        late_fold_kernel,
        in_specs=[VM, VM] + [VM] * len(far),
        out_shape=(
            jax.ShapeDtypeStruct((half, chunk, columns), BF),
            jax.ShapeDtypeStruct(small.shape, F32),
            jax.ShapeDtypeStruct((half * chunk + 16, columns), BF),
        ),
        compiler_params=params(),
        cost_estimate=cost(0.4),
        name="late_fold",
    )(keep, small, *far)


def finish_kernel(keep_ref, small_ref, far_ref, qkv_hbm, *refs):
    sums, (qkv_ref, sems) = refs[:-2], refs[-2:]
    total, small = late_sums(keep_ref, small_ref, (far_ref,))
    total = total[0]
    local = qkv_ref.shape[2]
    for j in range(3):
        qkv_ref[j] = total[:, j * local : (j + 1) * local]
    copies = fetch(((qkv_ref, qkv_hbm),), sems)
    vector = sums[0].shape[0]
    per_row = small.shape[1] // vector
    spot = 0
    for ref in sums:
        for start in range(0, ref.shape[0], vector):
            row, column = spot // per_row, spot % per_row * vector
            ref[start : start + vector] = small[row, column : column + vector]
            spot += 1
    for copy in copies:
        copy.wait()


def finish(keep, small, far, local, lengths):
    chunk = keep.shape[1]
    return pl.pallas_call(
        finish_kernel,
        in_specs=[VM] * 3,
        out_specs=[HBM] + [VM] * len(lengths),
        out_shape=(
            pltpu.HBM((3, chunk, local), F32),
            *(jax.ShapeDtypeStruct((length,), F32) for length in lengths),
        ),
        scratch_shapes=[pltpu.VMEM((3, chunk, local), F32), pltpu.SemaphoreType.DMA((1,))],
        compiler_params=params(),
        cost_estimate=cost(0.75),
        name="finish",
    )(keep, small, far)


def halves_kernel(keep_ref, far_ref, wout_hbm, proj_hbm, wout_ref, proj_ref, sems):
    total = (keep_ref[...].astype(F32) + far_ref[...].astype(F32))[0]
    local = wout_ref.shape[1]
    wout_ref[...] = total[:, :local]
    proj_ref[...] = total[:, local:]
    copies = fetch(((wout_ref, wout_hbm), (proj_ref, proj_hbm)), sems)
    for copy in copies:
        copy.wait()


def make_halves(keep, far, local, proj):
    chunk = keep.shape[1]
    return pl.pallas_call(
        halves_kernel,
        in_specs=[VM] * 2,
        out_specs=[HBM] * 2,
        out_shape=(pltpu.HBM((chunk, local), F32), pltpu.HBM((chunk, proj), F32)),
        scratch_shapes=[
            pltpu.VMEM((chunk, local), F32),
            pltpu.VMEM((chunk, proj), F32),
            pltpu.SemaphoreType.DMA((2,)),
        ],
        compiler_params=params(),
        cost_estimate=cost(0.4),
        name="halves",
    )(keep, far)


def dense_kernel(keep_ref, far_ref, zero_ref, divisor_ref, out_ref):
    genes = out_ref.shape[0]
    total = (keep_ref[...].astype(F32) + far_ref[...].astype(F32))[0]
    out_ref[...] = (zero_ref[...].astype(F32) + total[:genes]) / divisor_ref[...]


def make_dense(keep, far, zero_embed, divisor):
    return pl.pallas_call(
        dense_kernel,
        in_specs=[VM] * 4,
        out_shape=jax.ShapeDtypeStruct(zero_embed.shape, F32),
        compiler_params=params(),
        cost_estimate=cost(0.7),
        name="dense",
    )(keep, far, zero_embed, divisor)
ORDERS = {
    "dense": ("xzwy", "zxwy"),
    "down": ("yxwz", "xyzw"),
    "up": ("xzyw", "yxzw"),
    "A": ("wyxz", "zyxw"),
    "B": ("yxwz", "zywx"),
}
ADDS = {
    "output": [],
    "sent": [],
    "down": [],
    "feed_back": ["dense"],
    "up": [],
    "norm2": [],
    "A": [],
    "back": [],
    "B": ["down", "swap", "up", "dense", "A", "dense", "B", "down", "B", "up", "A", "down", "dense", "A", "last", "up", "down", "A", "B", "up"],
}


def dp_swap(value, bits):
    size = lax.axis_size("dp")
    pairs = [(2 * i + core, 2 * (i ^ (1 << bits[core])) + core) for i in range(size) for core in range(2)]
    return lax.ppermute(value, ("dp", "mp"), pairs)


def mp_swap(value):
    return lax.ppermute(value, "mp", [(0, 1), (1, 0)])


def slot_offsets(order):
    bits = len(order)
    return [
        sum(((s >> (bits - 1 - place)) & 1) << bit for place, bit in enumerate(order))
        for s in range(1 << bits)
    ]


def chunks_of(left, right, orders):
    offsets = [slot_offsets(order) for order in orders]
    size = len(offsets[0])
    grad = lax.dot_general(left, right, (((0,), (0,)), ((), ())), preferred_element_type=F32)
    chosen = jnp.asarray(offsets, jnp.int32)[lax.axis_index("mp")] ^ lax.axis_index("dp")
    slots = jnp.take(grad.astype(BF).reshape(size, -1, grad.shape[1]), chosen, axis=0)
    return slots[: size // 2], slots[size // 2 :]


def tie(value, *others):
    return lax.optimization_barrier((value,) + others)[0]


class Scatter:
    def __init__(self, orders):
        self.orders = orders
        self.step = 0

    def exchange(self, value):
        self.flight = dp_swap(value, [order[self.step] for order in self.orders])

    def send(self, keep, send):
        self.keep = keep
        self.exchange(send)

    @property
    def waiting(self):
        return self.step == len(self.orders[0]) - 1

    def add(self, token):
        out = fold(tie(self.keep, token), self.flight)
        self.step += 1
        if self.step == len(self.orders[0]):
            self.result = out
            return out
        self.send(*out)
        return out[0]


class LateScatter(Scatter):
    def send(self, keep, small, *pieces):
        self.keep, self.small = keep, small
        bits = [order[self.step] for order in self.orders]
        self.flight = [dp_swap(piece, bits) for piece in pieces]

    def add(self, token):
        self.step += 1
        self.send(*late_fold(tie(self.keep, token), self.small, self.flight))
        return self.keep


class Total:
    def __init__(self, bits):
        self.bits = list(range(bits))

    def send(self, value):
        self.result = value
        if self.bits:
            bit = self.bits.pop()
            self.flight = dp_swap(value, [bit, bit])

    def add(self, token):
        self.send(tie(self.result, token) + self.flight)
        return self.result


def scatter_plan(bits):
    if bits == 4:
        orders, adds = ORDERS, ADDS
        return {name: [["xyzw".index(axis) for axis in one] for one in pair] for name, pair in orders.items()}, adds
    one = list(range(bits))
    adds = {name: [] for name in ADDS}
    adds["B"] = ["swap", "last"] + [name for _ in one for name in list(ORDERS) + ["small"]]
    return {name: [one, one[1:-1] + [0, bits - 1]] for name in ORDERS}, adds


def per_device(
    tokens,
    cell_ids,
    gene_range,
    gene_offset,
    gain1,
    shift1,
    w_qkv,
    w_out,
    out_bias,
    gain2,
    shift2,
    w_up,
    up_bias,
    w_down,
    down_bias,
    w_proj,
    zero_embed,
    dense_cot,
):
    owners = lax.axis_size("dp")
    bits = owners.bit_length() - 1
    divisor = None
    place = jnp.stack([lax.axis_index("dp"), lax.axis_index("mp")])
    genes = zero_embed.shape[0]
    orders, adds = scatter_plan(bits)
    parts = {name: Scatter(pair) for name, pair in orders.items()}
    riding = tokens.shape[1] // owners % 16 == 0
    if riding:
        parts["B"] = LateScatter(orders["B"])
    else:
        parts["small"] = Total(bits)
    gene_range, gene_offset = gene_range.reshape(1, -1), gene_offset.reshape(1, -1)

    finals = {}
    local = w_out.shape[0]

    def service(event, token):
        for name in adds[event]:
            if name == "swap":
                finals["other"] = mp_swap(tie(finals["part"], token))
                continue
            if name == "last":
                token = finals["tokens"] = make_last(tokens, tie(finals["part"], token), finals["other"], grad_middle, gain1)
                continue
            part = parts[name]
            if name == "A" and part.waiting:
                part.result = make_halves(tie(part.keep, token), part.flight, local, w_proj.shape[1])
                token = part.result[0]
            elif name == "dense" and part.waiting:
                part.result = make_dense(tie(part.keep, token), part.flight, zero_embed, divisor)
                token = part.result
            else:
                token = part.add(token)
        return token

    spread = list(range(bits))[::-1]
    gather = [spread, spread[:1] + spread[-1:] + spread[1:-1]]
    payload, tokens, w_near = make_payload(gene_range, gene_offset, dense_cot, tokens, w_qkv, owners)
    payload = payload[None]
    steps = [[order[step] for order in gather] for step in range(bits)]
    far = dp_swap(payload, steps[0])
    out_other = mp_swap(w_out)
    proj_other = mp_swap(w_proj)
    normed1, q, k, v = make_qkv(tokens, gain1, shift1, w_near)
    *mixed, lse, q, k, v, normed1 = make_attend(cell_ids, q, k, v, normed1)
    mixed_other = [mp_swap(half) for half in mixed]
    held = join(payload, tie(far, lse))
    for step in range(1, bits - 2):
        far = dp_swap(held, steps[step])
        if step < bits - 3:
            held = join(held, far)
    middle, normed2 = make_middle(
        tie(tokens, held), mixed, mixed_other, w_out, out_other, out_bias, gain2, shift2
    )
    turned2 = make_turned(place, normed2, orders["up"])
    held = join(held, tie(far, turned2))
    far = dp_swap(held, steps[-2])
    far_first = dp_swap(held, steps[-1])
    *feed_part, act, slope, middle = make_feed(tie(normed2, held), middle, w_up, up_bias, w_down)
    feed_other = [mp_swap(half) for half in feed_part]
    far, far_first = lax.optimization_barrier((far, far_first, act))[:2]
    far_second = dp_swap(far, steps[-1])
    dense_part = parts["dense"]
    block_out, dense_keep, dense_send = make_output(
        place, gene_range, gene_offset, down_bias, middle, feed_part, feed_other, w_proj, dense_part.orders, genes
    )
    dense_part.send(dense_keep, dense_send)
    token = service("output", block_out)
    grad_sent, grad_zero, divisor = make_sent(
        place, gene_range, gene_offset, (held, far, far_first, tie(far_second, token)), genes, gather
    )
    sent_other = mp_swap(grad_sent)
    token = service("sent", grad_sent)
    grad_result, grad_down_bias, down = make_result(
        place, tie(grad_sent, token), sent_other, w_proj, proj_other, act, parts["down"].orders
    )
    parts["down"].send(*down)
    token = service("down", down[0])
    grad_hidden, part2, *halves, grad_up_bias = make_feed_back(tie(grad_result, token), slope, w_down, w_up)
    other2 = [mp_swap(half) for half in halves]
    token = service("feed_back", part2)
    up = make_turned_weight(place, turned2, tie(grad_hidden, token), orders["up"])
    parts["up"].send(*up)
    token = service("up", up[0])
    grad_middle, low, grad_gain2, grad_shift2, grad_out_bias = make_norm2(
        grad_result, tie(part2, token), other2, middle, gain2
    )
    token = service("norm2", low)
    parts["A"].send(*make_weight(place, [(tie(low, token), mixed), (block_out, (grad_sent,))], orders["A"]))
    token = service("A", parts["A"].keep)
    gq, gk, gv, part1, sums1 = make_back(cell_ids, tie(low, token), tokens, w_out, q, k, v, lse, w_qkv)
    sums_other = mp_swap(sums1)
    finals["part"] = part1
    token = service("back", gq)
    sums = [grad_out_bias, grad_gain2, grad_shift2, grad_down_bias, grad_up_bias]
    pairs = [(normed1, (tie(gq, token), gk, gv))]
    last = parts["B"]
    lengths = [item.shape[-1] for item in (sums1, sums1, *sums)]
    if riding:
        last.send(*make_tail(place, pairs, sums1, sums_other, sums, orders["B"]))
        token = service("B", last.keep)
        share_qkv, *small_sums = finish(tie(last.keep, token), last.small, last.flight[0], local, lengths)
    else:
        last.send(*make_weight(place, pairs, orders["B"]))
        sums1 = sums1 + sums_other
        parts["small"].send(jnp.concatenate([sums1[:1], sums1[1:]] + sums, 1))
        token = service("B", last.keep)
        share_qkv = jnp.stack([last.result[:, j * local : (j + 1) * local] for j in range(3)])
        small_sums, at = [], 0
        for length in lengths:
            small_sums.append(parts["small"].result[0, at : at + length])
            at += length
    share_wout, share_proj = parts["A"].result
    small_sums = small_sums[:5] + [small_sums[6], small_sums[5]]
    share_up, share_down, dense = parts["up"].result, parts["down"].result, dense_part.result
    return (
        block_out,
        dense,
        finals["tokens"],
        grad_zero,
        share_qkv,
        share_wout.T,
        share_up,
        share_down.T,
        share_proj,
    ) + tuple(small_sums)


def solution(mesh):
    in_specs = (
        P("dp", None),
        P("dp", None),
        P("dp", None),
        P("dp"),
        P(),
        P(),
        P(None, None, "mp"),
        P("mp", None),
        P(),
        P(),
        P(),
        P(None, "mp"),
        P("mp"),
        P("mp", None),
        P(),
        P(None, "mp"),
        P("dp", "mp"),
        P("dp", "mp"),
    )
    out_specs = (
        P("dp", None),
        P("dp", "mp"),
        P("dp", None),
        P("dp", "mp"),
        P(None, "dp", "mp"),
        P("mp", "dp"),
        P("dp", "mp"),
        P("mp", "dp"),
        P("dp", "mp"),
        P(),
        P(),
        P(),
        P(),
        P(),
        P("mp"),
        P(),
    )
    return jax.shard_map(
        per_device, mesh=mesh, in_specs=in_specs, out_specs=out_specs, check_vma=False
    )
```

```python
import functools
import jax
import jax.numpy as jnp
from jax import lax
from jax.experimental import pallas as pl
from jax.experimental.pallas import tpu as pltpu
from jax.sharding import PartitionSpec as P

HEAD_DIM = 64
EPSILON = 1e-05
BIG = 1e30
BF = jnp.bfloat16
F32 = jnp.float32
MIB = 1 << 20
SLOW, FAST = 1e8, 1e8

NT = (((1,), (1,)), ((), ()))


def dot(left, right):
    return jnp.dot(left, right, preferred_element_type=F32)


def dot_nt(left, right):
    return lax.dot_general(left, right, NT, preferred_element_type=F32)


def whole(shape):
    return pl.BlockSpec(shape, lambda *_: (0,) * len(shape))


VM = pl.BlockSpec(memory_space=pltpu.VMEM)
SM = pl.BlockSpec(memory_space=pltpu.SMEM)


def pick(place_ref, offsets, slot):
    first, second = offsets[0][slot], offsets[1][slot]
    if first == second:
        return first
    return first + place_ref[1] * (second - first)


def slot_of(place_ref, orders, owner):
    other = place_ref[0] ^ owner
    slots = []
    for order in orders:
        bits = len(order)
        slots.append(sum(((other >> bit) & 1) << (bits - 1 - spot) for spot, bit in enumerate(order)))
    return jnp.where(place_ref[1] == 0, slots[0], slots[1])


def params(mib=20):
    return pltpu.CompilerParams(vmem_limit_bytes=mib * MIB)


def cost(micros, rate=FAST):
    return pl.CostEstimate(flops=int(micros * rate), bytes_accessed=1, transcendentals=0)


def near(item):
    return pltpu.with_memory_space_constraint(item, pltpu.HBM)


HBM = pl.BlockSpec(memory_space=pltpu.HBM)


def fetch(pairs, sems):
    copies = [
        pltpu.make_async_copy(source, target, sems.at[i]) for i, (source, target) in enumerate(pairs)
    ]
    for copy in copies:
        copy.start()
    return copies


def line(ref):
    return ref[...].reshape(1, -1)


def norm_stats(values):
    centered = values - jnp.mean(values, -1, keepdims=True)
    inverse = lax.rsqrt(jnp.mean(centered * centered, -1, keepdims=True) + EPSILON)
    return centered * inverse, inverse


def norm_back(grad, normal, inverse, gain):
    scaled = grad * gain
    return inverse * (
        scaled
        - jnp.mean(scaled, -1, keepdims=True)
        - normal * jnp.mean(scaled * normal, -1, keepdims=True)
    )


def gene_rows(genes, owners):
    owners_pad = -(-owners // 16) * 16
    return -(-genes // owners_pad) * owners_pad, owners_pad


def payload_kernel(
    owners_pad, range_hbm, offset_hbm, cot_hbm, x_hbm, w_hbm, out_ref, x_ref, w_ref, range_ref, offset_ref, cot_ref, sems,
):
    copies = fetch(
        (
            (range_hbm, range_ref),
            (offset_hbm, offset_ref),
            (cot_hbm, cot_ref),
            (x_hbm, x_ref),
            (w_hbm, w_ref),
        ),
        sems,
    )
    for copy in copies[:3]:
        copy.wait()
    genes, width = cot_ref.shape
    tok = range_ref.shape[1]
    rows = out_ref.shape[0] - owners_pad
    cot = cot_ref[...].astype(F32)
    if rows > genes:
        cot = jnp.concatenate([cot, jnp.zeros((rows - genes, width), F32)], 0)
    out_ref[:rows, :] = cot.astype(BF)
    owner_hits = jnp.where(
        lax.broadcasted_iota(jnp.int32, (owners_pad, tok), 0) == range_ref[...], 1.0, 0.0
    ).astype(BF)
    offset_hits = jnp.where(
        lax.broadcasted_iota(jnp.int32, (width, tok), 0) == offset_ref[...], 1.0, 0.0
    ).astype(BF)
    out_ref[rows:, :] = dot_nt(owner_hits, offset_hits).astype(BF)
    for copy in copies[3:]:
        copy.wait()


def make_payload(gene_range, gene_offset, cot, tokens, w_qkv, owners):
    genes, width = cot.shape
    tok = gene_offset.shape[1]
    rows, owners_pad = gene_rows(genes, owners)
    operands = (gene_range, gene_offset, cot, tokens, w_qkv)
    return pl.pallas_call(
        functools.partial(payload_kernel, owners_pad),
        in_specs=[HBM] * 5,
        out_specs=[VM] * 3,
        out_shape=(
            jax.ShapeDtypeStruct((rows + owners_pad, width), BF),
            jax.ShapeDtypeStruct(tokens.shape, BF),
            jax.ShapeDtypeStruct(w_qkv.shape, BF),
        ),
        scratch_shapes=[
            pltpu.VMEM((1, tok), jnp.int32),
            pltpu.VMEM((1, tok), jnp.int32),
            pltpu.VMEM((genes, width), BF),
            pltpu.SemaphoreType.DMA((5,)),
        ],
        compiler_params=params(),
        cost_estimate=cost(1.8, SLOW),
        name="payload",
    )(*map(near, operands))


def join_kernel(near_ref, far_ref, out_ref):
    half = near_ref.shape[0]
    out_ref[:half] = near_ref[...]
    out_ref[half:] = far_ref[...]


def join(near, far):
    return pl.pallas_call(
        join_kernel,
        in_specs=[VM, VM],
        out_shape=jax.ShapeDtypeStruct((2 * near.shape[0],) + near.shape[1:], near.dtype),
        compiler_params=params(16 if near.shape[0] < 8 else 32),
        cost_estimate=cost(0.4, SLOW),
        name="join",
    )(near, far)


def sent_kernel(genes, orders, count, place_ref, range_hbm, offset_hbm, *refs):
    range_ref, offset_ref, sems = refs[-3:]
    refs = refs[:-3]
    hist_refs, held_refs = refs[:count], refs[count : 2 * count]
    sent_ref, zero_ref, div_ref, total, by_gene, low = refs[2 * count :]
    batch, rows, width = held_refs[0].shape
    size, owners_pad, _ = hist_refs[0].shape
    step = pl.program_id(0)
    me = place_ref[0]
    tok = range_ref.shape[1]

    @pl.when(step == 0)
    def _():
        copies = fetch(((range_hbm, range_ref), (offset_hbm, offset_ref)), sems)
        counts = jnp.zeros((owners_pad, width), F32)
        for ref in hist_refs:
            for slot in range(size):
                counts += ref[slot].astype(F32)
        if owners_pad < 128:
            counts = jnp.concatenate([counts, jnp.zeros((128 - owners_pad, width), F32)], 0)
        by_gene[...] = 1.0 + counts.T[:rows]
        total[...] = jnp.zeros_like(total)
        for copy in copies:
            copy.wait()

    spread = by_gene[...]
    owner_lane = lax.broadcasted_iota(jnp.int32, spread.shape, 1)
    other = range_ref[...] ^ me
    slots = [
        sum(((other >> bit) & 1) << spot for spot, bit in enumerate(order)) for order in orders
    ]
    slots = jnp.where(place_ref[1] == 0, slots[0], slots[1])
    side = slots // size
    near = slots - side * size - step * batch
    index = jnp.where((near >= 0) & (near < batch), (side * batch + near) * rows + offset_ref[...], -1)
    columns = jnp.broadcast_to(index, (128, tok)).T
    for side, ref in enumerate(held_refs):
        for spot in range(batch):
            slot = side * size + step * batch + spot
            offset = jnp.int32(0)
            for core, order in enumerate(orders):
                one = sum(((slot >> i) & 1) << bit for i, bit in enumerate(order))
                offset = jnp.where(place_ref[1] == core, one, offset)
            divisor = jnp.sum(jnp.where(owner_lane == (me ^ offset), spread, 0.0), 1, keepdims=True)
            grad = ref[spot].astype(F32) * (1.0 / divisor)
            if spot == 0 and side == 0:

                @pl.when(step == 0)
                def _():
                    zero_ref[...] = grad[:genes]
                    div_ref[...] = jnp.broadcast_to(divisor[:genes], (genes, width))

            at = (side * batch + spot) * rows
            low[at : at + rows, :] = grad.astype(BF)
    lane = lax.broadcasted_iota(jnp.int32, (tok, 128), 1)
    hits = jnp.concatenate(
        [
            jnp.where(columns == lane + at, 1.0, 0.0).astype(BF)
            for at in range(0, count * batch * rows, 128)
        ],
        1,
    )
    total[...] += dot(hits, low[...])

    @pl.when(step == pl.num_programs(0) - 1)
    def _():
        sent_ref[...] = total[...].astype(BF)


def make_sent(place, gene_range, gene_offset, held, genes, orders):
    size, height, width = held[0].shape
    count = len(held)
    owners = count * size
    rows, owners_pad = gene_rows(genes, owners)
    batch = min(size, 4)
    tok = gene_offset.shape[1]
    hist = pl.BlockSpec((size, owners_pad, width), lambda i: (0, rows // owners_pad, 0))
    cots = pl.BlockSpec((batch, rows, width), lambda i: (i, 0, 0))
    return pl.pallas_call(
        functools.partial(sent_kernel, genes, orders, count),
        grid=(size // batch,),
        in_specs=[SM, HBM, HBM] + [hist] * count + [cots] * count,
        out_specs=(whole((tok, width)), whole((genes, width)), whole((genes, width))),
        out_shape=(
            jax.ShapeDtypeStruct((tok, width), BF),
            jax.ShapeDtypeStruct((genes, width), F32),
            jax.ShapeDtypeStruct((genes, width), F32),
        ),
        scratch_shapes=[
            pltpu.VMEM((tok, width), F32),
            pltpu.VMEM((rows, 128 * -(-owners // 128)), F32),
            pltpu.VMEM((count * batch * rows, width), BF),
            pltpu.VMEM((1, tok), jnp.int32),
            pltpu.VMEM((1, tok), jnp.int32),
            pltpu.SemaphoreType.DMA((2,)),
        ],
        compiler_params=params(20 if owners <= 16 else 48),
        cost_estimate=cost(2.5, SLOW),
        name="grad_sent",
    )(place, near(gene_range), near(gene_offset), *held, *held)


def qkv_kernel(x_ref, gain_ref, shift_ref, w_ref, normed_ref, q_ref, k_ref, v_ref):
    normal, _ = norm_stats(x_ref[...].astype(F32))
    normed = (normal * line(gain_ref) + line(shift_ref)).astype(BF)
    normed_ref[...] = normed
    for j, out in enumerate((q_ref, k_ref, v_ref)):
        out[...] = dot(normed, w_ref[j]).astype(BF)


def make_qkv(tokens, gain, shift, w_qkv):
    tok, width = tokens.shape
    local = w_qkv.shape[2]
    one = jax.ShapeDtypeStruct((tok, local), BF)
    return pl.pallas_call(
        qkv_kernel,
        in_specs=[VM] * 4,
        out_shape=(jax.ShapeDtypeStruct((tok, width), BF), one, one, one),
        compiler_params=params(),
        cost_estimate=cost(1.7, SLOW),
        name="qkv",
    )(tokens, gain, shift, w_qkv)


def masked_pair(q_pair, k_pair, cells, half, cell_count=8):
    lane = lax.broadcasted_iota(jnp.int32, q_pair.shape, 1)
    own = (lane // HEAD_DIM) == half
    place = lane % HEAD_DIM
    same = place == cells
    q_mask = jnp.where((place < cell_count) & jnp.logical_not(same), -BIG, 0.0)
    k_mask = jnp.where(same, 1.0, 0.0)
    scaled = q_pair.astype(F32) * (HEAD_DIM**-0.5)
    q_head = jnp.where(own, scaled, q_mask).astype(BF)
    k_head = jnp.where(own, k_pair.astype(F32), k_mask).astype(BF)
    return q_head, k_head


def attend_kernel(
    cells_ref, q_ref, k_ref, v_ref, normed_ref, upper_ref, lower_ref, lse_ref, q_far, k_far, v_far, normed_far, sems,
):
    copies = fetch(((q_ref, q_far), (k_ref, k_far), (v_ref, v_far), (normed_ref, normed_far)), sems)
    tok, local = q_ref.shape
    half_tok = tok // 2
    cells = jnp.broadcast_to(cells_ref[...], (128, tok)).T
    lane = lax.broadcasted_iota(jnp.int32, (tok, 128), 1)
    logs = jnp.zeros((tok, 128), F32)
    for pair in range(local // 128):
        cut = slice(pair * 128, pair * 128 + 128)
        q_pair, k_pair, v_pair = q_ref[:, cut], k_ref[:, cut], v_ref[:, cut]
        heads = []
        for half in range(2):
            q_head, k_head = masked_pair(q_pair, k_pair, cells, half)
            scores = dot_nt(q_head, k_head)
            top = jnp.max(scores, 1, keepdims=True)
            powers = jnp.exp(scores - top)
            total = jnp.sum(powers, 1, keepdims=True)
            probs = (powers * (1.0 / total)).astype(BF)
            logs = jnp.where(lane == 2 * pair + half, top + jnp.log(total), logs)
            heads.append(dot(probs, v_pair))
        mixed = jnp.where(lane < HEAD_DIM, heads[0], heads[1]).astype(BF)
        upper_ref[:, cut] = mixed[:half_tok]
        lower_ref[:, cut] = mixed[half_tok:]
    lse_ref[...] = logs.T[: lse_ref.shape[0]]
    for copy in copies:
        copy.wait()


def make_attend(cell_ids, q, k, v, normed):
    tok, local = q.shape
    heads = -(-local // HEAD_DIM // 8) * 8
    half = jax.ShapeDtypeStruct((tok // 2, local), BF)
    return pl.pallas_call(
        attend_kernel,
        in_specs=[VM] * 5,
        out_specs=[VM] * 3 + [HBM] * 4,
        out_shape=(
            half,
            half,
            jax.ShapeDtypeStruct((heads, tok), F32),
            *(pltpu.HBM(item.shape, BF) for item in (q, k, v, normed)),
        ),
        scratch_shapes=[pltpu.SemaphoreType.DMA((4,))],
        compiler_params=params(),
        cost_estimate=cost(2.9, SLOW),
        name="attend",
    )(cell_ids, q, k, v, normed)


def pair_back(cells, q_pair, k_pair, v_pair, gm_pair, lse, lane):
    factor = HEAD_DIM**-0.5
    k_turned = k_pair.astype(F32).T.astype(BF)
    gq_halves = []
    gk = gv = None
    for half in range(2):
        own = (lane // HEAD_DIM) == half
        q_head, k_head = masked_pair(q_pair, k_pair, cells, half)
        v_head = jnp.where(own, v_pair.astype(F32), 0.0).astype(BF)
        probs = jnp.exp(dot_nt(k_head, q_head) - lse[half : half + 1])
        part = dot(probs.astype(BF), gm_pair)
        gv = part if half == 0 else jnp.where(own, part, gv)
        grad_probs = dot_nt(v_head, gm_pair)
        spread = jnp.sum(probs * grad_probs, 0, keepdims=True)
        grad_scores = (probs * (grad_probs - spread)).astype(BF)
        part = dot(grad_scores, q_pair)
        gk = part if half == 0 else jnp.where(own, part, gk)
        gq_halves.append(dot(k_turned[half * HEAD_DIM : (half + 1) * HEAD_DIM], grad_scores))
    gq = (jnp.concatenate(gq_halves, 0).T * factor).astype(BF)
    return gq, (gk * factor).astype(BF), gv.astype(BF)


GELU_A = 0.7978845608028654
GELU_B = 0.044715


def middle_kernel(
    x_ref, own_upper_ref, own_lower_ref, upper_ref, lower_ref, wo_ref, wo_other_ref, bias_ref, gain_ref, shift_ref,
    middle_ref, normed_ref,
):
    own = jnp.concatenate([own_upper_ref[...], own_lower_ref[...]], 0)
    other = jnp.concatenate([upper_ref[...], lower_ref[...]], 0)
    attended = dot(own, wo_ref[...]) + dot(other, wo_other_ref[...])
    middle = x_ref[...].astype(F32) + attended + line(bias_ref)
    middle_ref[...] = middle
    normal, _ = norm_stats(middle)
    normed_ref[...] = (normal * line(gain_ref) + line(shift_ref)).astype(BF)


def make_middle(tokens, mixed, mixed_other, w_out, out_other, out_bias, gain, shift):
    tok, width = tokens.shape
    return pl.pallas_call(
        middle_kernel,
        in_specs=[VM] * 10,
        out_shape=(jax.ShapeDtypeStruct((tok, width), F32), jax.ShapeDtypeStruct((tok, width), BF)),
        compiler_params=params(),
        cost_estimate=cost(1.4, SLOW),
        name="middle",
    )(tokens, *mixed, *mixed_other, w_out, out_other, out_bias, gain, shift)


def feed_kernel(
    chunk, normed_ref, middle_ref, up_ref, up_bias_ref, down_ref,
    *refs,
):
    quarters, (act_far, slope_far, middle_far, act_ref, slope_ref, sems) = refs[:4], refs[4:]
    copies = fetch(((middle_ref, middle_far),), sems)
    normed = normed_ref[...]
    up_bias = line(up_bias_ref)
    units = up_ref.shape[1]
    for place, at in enumerate(range(0, units, chunk)):
        cut = slice(at, at + chunk)
        hidden = dot(normed, up_ref[:, cut]) + up_bias[:, cut]
        square = hidden * hidden
        curve = jnp.tanh(hidden * (GELU_A + (GELU_A * GELU_B) * square))
        half = 0.5 * hidden
        act_ref[:, cut] = (half + half * curve).astype(BF)
        slope = (0.5 + 0.5 * curve) + half * (1.0 - curve * curve) * (
            GELU_A + (3 * GELU_A * GELU_B) * square
        )
        slope_ref[:, cut] = slope.astype(BF)
        copies += fetch(
            ((act_ref.at[:, cut], act_far.at[:, cut]), (slope_ref.at[:, cut], slope_far.at[:, cut])),
            sems.at[pl.ds(1 + 2 * place, 2)],
        )
    feed = dot(act_ref[...], down_ref[...]).astype(BF)
    for place, ref in enumerate(quarters):
        ref[...] = feed[place * ref.shape[0] : (place + 1) * ref.shape[0]]
    for copy in copies:
        copy.wait()


def make_feed(normed, middle, w_up, up_bias, w_down, chunk=768):
    tok, width = normed.shape
    units = w_up.shape[1]
    return pl.pallas_call(
        functools.partial(feed_kernel, chunk),
        in_specs=[VM] * 5,
        out_specs=[VM] * 4 + [HBM] * 3,
        out_shape=(
            *(jax.ShapeDtypeStruct((tok // 4, width), BF) for _ in range(4)),
            pltpu.HBM((tok, units), BF),
            pltpu.HBM((tok, units), BF),
            pltpu.HBM((tok, width), F32),
        ),
        scratch_shapes=[
            pltpu.VMEM((tok, units), BF),
            pltpu.VMEM((tok, units), BF),
            pltpu.SemaphoreType.DMA((1 + 2 * units // chunk,)),
        ],
        compiler_params=params(24),
        cost_estimate=cost(4.1, SLOW),
        name="feed",
    )(normed, middle, w_up, up_bias, w_down)


def result_kernel(
    orders, place_ref, sent_ref, other_ref, wp_ref, wp_other_ref, act_ref,
    result_ref, bias_ref, keep_ref, send_ref, chosen,
):
    size, chunk, tok = chosen.shape
    half = size // 2 * chunk
    result = dot_nt(sent_ref[...], wp_ref[...]) + dot_nt(other_ref[...], wp_other_ref[...])
    low = result.astype(BF)
    result_ref[...] = low
    bias_ref[...] = jnp.sum(low.astype(F32), 0, keepdims=True)
    turned = low.astype(F32).T.astype(BF).reshape(chosen.shape)
    for owner in range(size):
        chosen[slot_of(place_ref, orders, owner)] = turned[owner]
    for at in range(0, act_ref.shape[1], 512):
        cut = slice(at, at + 512)
        right = act_ref[:, cut]
        out = (size // 2, chunk, right.shape[1])
        keep_ref[:, :, cut] = dot(chosen[: size // 2].reshape(half, tok), right).astype(BF).reshape(out)
        send_ref[:, :, cut] = dot(chosen[size // 2 :].reshape(half, tok), right).astype(BF).reshape(out)


def plain_result_kernel(sent_ref, other_ref, wp_ref, wp_other_ref, result_ref, bias_ref):
    result = dot_nt(sent_ref[...], wp_ref[...]) + dot_nt(other_ref[...], wp_other_ref[...])
    low = result.astype(BF)
    result_ref[...] = low
    bias_ref[...] = jnp.sum(low.astype(F32), 0, keepdims=True)


def make_result(index, sent, sent_other, w_proj, proj_other, act, orders):
    tok = sent.shape[0]
    width = w_proj.shape[0]
    units = act.shape[1]
    size = 1 << len(orders[0])
    chunk = width // size
    outs = (jax.ShapeDtypeStruct((tok, width), BF), jax.ShapeDtypeStruct((1, width), F32))
    if chunk % 16:
        result, bias = pl.pallas_call(
            plain_result_kernel, in_specs=[VM] * 4, out_shape=outs, compiler_params=params(), name="result"
        )(sent, sent_other, w_proj, proj_other)
        return result, bias, make_weight(index, [(result, (act,))], orders)
    half = jax.ShapeDtypeStruct((size // 2, chunk, units), BF)
    result, bias, keep, send = pl.pallas_call(
        functools.partial(result_kernel, orders),
        in_specs=[SM] + [VM] * 5,
        out_shape=(*outs, half, half),
        scratch_shapes=[pltpu.VMEM((size, chunk, tok), BF)],
        compiler_params=params(),
        cost_estimate=cost(3.7, SLOW),
        name="result",
    )(index, sent, sent_other, w_proj, proj_other, act)
    return result, bias, (keep, send)


def feed_back_kernel(
    chunk, result_ref, slope_ref, down_ref, up_ref, hidden_ref, normed_ref, upper_ref, lower_ref, up_bias_ref
):
    low = result_ref[...]
    for at in range(0, up_ref.shape[1], chunk):
        cut = slice(at, at + chunk)
        grad = (dot_nt(low, down_ref[cut]) * slope_ref[:, cut].astype(F32)).astype(BF)
        hidden_ref[:, cut] = grad
        up_bias_ref[:, cut] = jnp.sum(grad.astype(F32), 0, keepdims=True)
    normed = dot_nt(hidden_ref[...], up_ref[...]).astype(BF)
    normed_ref[...] = normed
    half = upper_ref.shape[0]
    upper_ref[...] = normed[:half]
    lower_ref[...] = normed[half:]


def make_feed_back(result, slope, w_down, w_up, chunk=768):
    tok, width = result.shape
    units = w_up.shape[1]
    return pl.pallas_call(
        functools.partial(feed_back_kernel, chunk),
        in_specs=[VM] * 4,
        out_shape=(
            jax.ShapeDtypeStruct((tok, units), BF),
            jax.ShapeDtypeStruct((tok, width), BF),
            jax.ShapeDtypeStruct((tok // 2, width), BF),
            jax.ShapeDtypeStruct((tok // 2, width), BF),
            jax.ShapeDtypeStruct((1, units), F32),
        ),
        compiler_params=params(24),
        cost_estimate=cost(2.8),
        name="feed_back",
    )(result, slope, w_down, w_up)


def turn_kernel(orders, place_ref, left_ref, out_ref):
    turned = left_ref[...].astype(F32).T.astype(BF).reshape(out_ref.shape)
    for owner in range(out_ref.shape[0]):
        out_ref[slot_of(place_ref, orders, owner)] = turned[owner]


def make_turned(index, left, orders):
    tok, width = left.shape
    size = 1 << len(orders[0])
    if width // size % 16:
        return left
    return pl.pallas_call(
        functools.partial(turn_kernel, orders),
        in_specs=[SM, VM],
        out_shape=jax.ShapeDtypeStruct((size, width // size, tok), BF),
        compiler_params=params(),
        cost_estimate=cost(0.9, SLOW),
        name="turn",
    )(index, left)


def turned_kernel(chosen_ref, right_ref, keep_ref, send_ref):
    size, chunk, tok = chosen_ref.shape
    half = size // 2 * chunk
    for at in range(0, right_ref.shape[1], 512):
        cut = slice(at, at + 512)
        right = right_ref[:, cut]
        out = (size // 2, chunk, right.shape[1])
        keep_ref[:, :, cut] = dot(chosen_ref[: size // 2].reshape(half, tok), right).astype(BF).reshape(out)
        send_ref[:, :, cut] = dot(chosen_ref[size // 2 :].reshape(half, tok), right).astype(BF).reshape(out)


def make_turned_weight(index, left, right, orders):
    if left.ndim == 2:
        return make_weight(index, [(left, (right,))], orders)
    size, chunk, _ = left.shape
    out = jax.ShapeDtypeStruct((size // 2, chunk, right.shape[1]), BF)
    return pl.pallas_call(
        turned_kernel,
        in_specs=[VM, VM],
        out_shape=(out, out),
        compiler_params=params(),
        cost_estimate=cost(2.2),
        name="up_grad",
    )(left, right)


def weight_kernel(orders, groups, place_ref, *refs):
    ins = refs[: -2 - len(groups)]
    keep_ref, send_ref = refs[len(ins) : len(ins) + 2]
    size, chunk, tok = refs[-1].shape
    half = size // 2 * chunk
    at = place = 0
    for count, chosen in zip(groups, refs[len(ins) + 2 :]):
        turned = ins[place][...].astype(F32).T.astype(BF).reshape(chosen.shape)
        for owner in range(size):
            chosen[slot_of(place_ref, orders, owner)] = turned[owner]
        rights = [ref[...] for ref in ins[place + 1 : place + 1 + count]]
        if rights[0].shape[0] < tok:
            rights = [jnp.concatenate(rights, 0)]
        for right in rights:
            cut = slice(at, at + right.shape[1])
            out = (size // 2, chunk, right.shape[1])
            keep_ref[:, :, cut] = dot(chosen[: size // 2].reshape(half, tok), right).astype(BF).reshape(out)
            send_ref[:, :, cut] = dot(chosen[size // 2 :].reshape(half, tok), right).astype(BF).reshape(out)
            at += right.shape[1]
        place += 1 + count


def make_weight(index, pairs, orders):
    tok, width = pairs[0][0].shape
    columns = sum(right.shape[1] * right.shape[0] for _, rights in pairs for right in rights) // tok
    size = 1 << len(orders[0])
    chunk = width // size
    if chunk % 16:
        pairs = [
            (left, (jnp.concatenate(rights),) if rights[0].shape[0] < tok else rights) for left, rights in pairs
        ]
        parts = [chunks_of(left, right, orders) for left, rights in pairs for right in rights]
        return tuple(jnp.concatenate(side, 2) for side in zip(*parts))
    out = jax.ShapeDtypeStruct((size // 2, chunk, columns), BF)
    flat = [item for left, rights in pairs for item in (left, *rights)]
    return pl.pallas_call(
        functools.partial(weight_kernel, orders, [len(rights) for _, rights in pairs]),
        in_specs=[SM] + [VM] * len(flat),
        out_shape=(out, out),
        scratch_shapes=[pltpu.VMEM((size, chunk, tok), BF) for _ in pairs],
        compiler_params=params(),
        cost_estimate=cost(2.2),
        name="weight_grad",
    )(index, *flat)


def norm2_kernel(
    result_ref, part_ref, upper_ref, lower_ref, middle_ref, gain_ref,
    grad_middle_ref, low_ref, gain_sum_ref, shift_sum_ref, bias_sum_ref,
):
    other = jnp.concatenate([upper_ref[...], lower_ref[...]], 0)
    grad = part_ref[...].astype(F32) + other.astype(F32)
    normal, inverse = norm_stats(middle_ref[...])
    gain_sum_ref[...] = jnp.sum(grad * normal, 0, keepdims=True)
    shift_sum_ref[...] = jnp.sum(grad, 0, keepdims=True)
    middle = result_ref[...].astype(F32) + norm_back(grad, normal, inverse, line(gain_ref))
    grad_middle_ref[...] = middle
    bias_sum_ref[...] = jnp.sum(middle, 0, keepdims=True)
    low_ref[...] = middle.astype(BF)


def make_norm2(result, part, other, middle, gain):
    tok, width = middle.shape
    small = jax.ShapeDtypeStruct((1, width), F32)
    return pl.pallas_call(
        norm2_kernel,
        in_specs=[VM] * 6,
        out_shape=(
            jax.ShapeDtypeStruct((tok, width), F32), jax.ShapeDtypeStruct((tok, width), BF), small, small, small
        ),
        compiler_params=params(),
        cost_estimate=cost(2.4),
        name="norm2",
    )(result, part, *other, middle, gain)


def back_kernel(
    cells_ref, low_ref, x_ref, wo_ref, q_ref, k_ref, v_ref, lse_ref, w_ref, gq_ref, gk_ref, gv_ref, normed_ref, sums_ref,
):
    tok = q_ref.shape[0]
    cells = jnp.broadcast_to(cells_ref[...], (128, tok)).T
    lane = lax.broadcasted_iota(jnp.int32, (tok, 128), 1)
    gm = dot_nt(low_ref[...], wo_ref[...]).astype(BF)
    for pair in range(q_ref.shape[1] // 128):
        cut = slice(pair * 128, pair * 128 + 128)
        out = pair_back(
            cells, q_ref[:, cut], k_ref[:, cut], v_ref[:, cut], gm[:, cut], lse_ref[2 * pair : 2 * pair + 2], lane
        )
        for ref, value in zip((gq_ref, gk_ref, gv_ref), out):
            ref[:, cut] = value
    total = dot_nt(gq_ref[...], w_ref[0]) + dot_nt(gk_ref[...], w_ref[1]) + dot_nt(gv_ref[...], w_ref[2])
    normal, _ = norm_stats(x_ref[...].astype(F32))
    sums_ref[0:1] = jnp.sum(total * normal, 0, keepdims=True)
    sums_ref[1:2] = jnp.sum(total, 0, keepdims=True)
    normed_ref[...] = total.astype(BF)


def make_back(cell_ids, low, tokens, w_out, q, k, v, lse, w_qkv):
    tok, local = q.shape
    width = low.shape[1]
    one = jax.ShapeDtypeStruct((tok, local), BF)
    return pl.pallas_call(
        back_kernel,
        in_specs=[VM] * 9,
        out_shape=(
            one, one, one, jax.ShapeDtypeStruct((tok, width), BF), jax.ShapeDtypeStruct((2, width), F32)
        ),
        compiler_params=params(),
        cost_estimate=cost(6.4),
        name="back",
    )(cell_ids, low, tokens, w_out, q, k, v, lse, w_qkv)


def last_kernel(x_ref, part_ref, other_ref, middle_ref, gain_ref, out_hbm, out_ref, sems):
    half = x_ref.shape[0] // 2
    cuts = [pl.ds(place * half, half) for place in range(2)]
    out = []
    for place, cut in enumerate(cuts):
        grad = part_ref[cut].astype(F32) + other_ref[cut].astype(F32)
        normal, inverse = norm_stats(x_ref[cut].astype(F32))
        grad = norm_back(grad, normal, inverse, line(gain_ref))
        out_ref[cut] = middle_ref[cut] + grad
        out += fetch([(out_ref.at[cut], out_hbm.at[cut])], sems.at[pl.ds(place, 1)])
    for copy in out:
        copy.wait()


def make_last(tokens, part, other, grad_middle, gain):
    tok, width = tokens.shape
    return pl.pallas_call(
        last_kernel,
        in_specs=[VM] * 5,
        out_specs=HBM,
        out_shape=pltpu.HBM((tok, width), F32),
        scratch_shapes=[pltpu.VMEM((tok, width), F32), pltpu.SemaphoreType.DMA((2,))],
        compiler_params=params(),
        cost_estimate=cost(2.3),
        name="last",
    )(tokens, part, other, grad_middle, gain)


def output_kernel(orders, place_ref, range_hbm, offset_hbm, bias_hbm, middle_hbm, *refs):
    own, other = refs[:4], refs[4:8]
    wp_ref, out_ref, keep_ref, send_ref, range_ref, offset_ref, bias_ref, middle_ref, hits, sems = refs[8:]
    copies = fetch(
        ((range_hbm, range_ref), (offset_hbm, offset_ref), (bias_hbm, bias_ref), (middle_hbm, middle_ref)), sems
    )
    half, rows, width = keep_ref.shape
    tok = range_ref.shape[1]
    for copy in copies[:2]:
        copy.wait()
    index = slot_of(place_ref, orders, range_ref[...]) * rows + offset_ref[...]
    gene = lax.broadcasted_iota(jnp.int32, (rows, tok), 0)
    batch = hits.shape[0] // rows

    def find(first):
        for spot in range(batch):
            hits[spot * rows : (spot + 1) * rows, :] = jnp.where(
                gene + (first + spot) * rows == index, 1.0, 0.0
            ).astype(BF)

    find(0)
    for copy in copies[2:]:
        copy.wait()
    feed = jnp.concatenate([left[...].astype(F32) + right[...].astype(F32) for left, right in zip(own, other)], 0)
    low = (middle_ref[...] + feed + line(bias_ref)).astype(BF)
    out_ref[...] = low
    sent = dot(low, wp_ref[...]).astype(BF)
    for first in range(0, 2 * half, batch):
        if first:
            find(first)
        ref = keep_ref if first < half else send_ref
        at = first % half
        ref[at : at + batch] = dot(hits[...], sent).astype(BF).reshape((batch, rows, width))


def make_output(place, gene_range, gene_offset, bias, middle, own, other, w_proj, orders, genes):
    tok, width = middle.shape
    proj = w_proj.shape[1]
    owners = 1 << len(orders[0])
    rows = -(-genes // 16) * 16
    half = jax.ShapeDtypeStruct((owners // 2, rows, proj), BF)
    return pl.pallas_call(
        functools.partial(output_kernel, orders),
        in_specs=[SM] + [HBM] * 4 + [VM] * 9,
        out_shape=(jax.ShapeDtypeStruct((tok, width), BF), half, half),
        scratch_shapes=[
            pltpu.VMEM((1, tok), jnp.int32),
            pltpu.VMEM((1, tok), jnp.int32),
            pltpu.VMEM((width,), F32),
            pltpu.VMEM((tok, width), F32),
            pltpu.VMEM((min(owners // 2, 8) * rows, tok), BF),
            pltpu.SemaphoreType.DMA((4,)),
        ],
        compiler_params=params(20 if owners <= 16 else 48),
        cost_estimate=cost(2.8, SLOW),
        name="output",
    )(place, near(gene_range), near(gene_offset), near(bias), near(middle), *own, *other, w_proj)


def fold_kernel(keep_ref, far_ref, new_keep_ref, send_ref):
    total = keep_ref[...].astype(F32) + far_ref[...].astype(F32)
    half = total.shape[0] // 2
    new_keep_ref[...] = total[:half].astype(BF)
    send_ref[...] = total[half:].astype(BF)


def last_fold_kernel(keep_ref, far_ref, out_hbm, out_ref, sems):
    out_ref[...] = (keep_ref[...].astype(F32) + far_ref[...].astype(F32))[0]
    for copy in fetch(((out_ref, out_hbm),), sems):
        copy.wait()


def fold(keep, far):
    slots, rows, columns = keep.shape
    if slots == 1:
        return pl.pallas_call(
            last_fold_kernel,
            in_specs=[VM, VM],
            out_specs=HBM,
            out_shape=pltpu.HBM((rows, columns), F32),
            scratch_shapes=[pltpu.VMEM((rows, columns), F32), pltpu.SemaphoreType.DMA((1,))],
            compiler_params=params(16),
            cost_estimate=cost(0.4),
            name="last_fold",
        )(keep, far)
    return pl.pallas_call(
        fold_kernel,
        in_specs=[VM, VM],
        out_shape=(jax.ShapeDtypeStruct((slots // 2, rows, columns), BF),) * 2,
        compiler_params=params(16 if slots <= 8 else 48),
        cost_estimate=cost(0.4),
        name="fold",
    )(keep, far)


def parted(value):
    high = value.astype(BF).astype(F32)
    return jnp.concatenate([high, value - high], 0).astype(BF)


def tail_kernel(orders, groups, vectors, place_ref, own_ref, other_ref, *refs):
    keep_ref, small_ref, send_ref, rest_ref = refs[-4 - len(groups) : -len(groups)]
    size, chunk, tok = refs[-1].shape
    half = size // 2 * chunk
    quarter = send_ref.shape[0]
    at = place = 0
    for count, chosen in zip(groups, refs[-len(groups) :]):
        turned = refs[place][...].astype(F32).T.astype(BF).reshape(chosen.shape)
        for owner in range(size):
            chosen[slot_of(place_ref, orders, owner)] = turned[owner]
        rights = [ref[...] for ref in refs[place + 1 : place + 1 + count]]
        if rights[0].shape[0] < tok:
            rights = [jnp.concatenate(rights, 0)]
        for right in rights:
            cut = slice(at, at + right.shape[1])
            out = (size // 2, chunk, right.shape[1])
            keep_ref[:, :, cut] = dot(chosen[: size // 2].reshape(half, tok), right).astype(BF).reshape(out)
            sent = dot(chosen[size // 2 :].reshape(half, tok), right).astype(BF)
            send_ref[:, cut] = sent[:quarter]
            rest_ref[: half - quarter, cut] = sent[quarter:]
            at += right.shape[1]
        place += 1 + count
    sums = own_ref[...] + other_ref[...]
    vector = sums.shape[1]
    per_row = small_ref.shape[1] // vector
    pieces = [sums[0:1], sums[1:2]]
    for ref in refs[place : place + vectors]:
        pieces += [ref[:, start : start + vector] for start in range(0, ref.shape[1], vector)]
    small_ref[...] = jnp.zeros_like(small_ref)
    for spot, piece in enumerate(pieces):
        row, column = spot // per_row, spot % per_row * vector
        small_ref[row : row + 1, column : column + vector] = piece
    rest_ref[half - quarter :, :] = parted(small_ref[...])


def make_tail(index, pairs, own, other, sums, orders):
    tok, width = pairs[0][0].shape
    columns = sum(right.shape[1] * right.shape[0] for _, rights in pairs for right in rights) // tok
    size = 1 << len(orders[0])
    chunk = width // size
    flat = [item for left, rights in pairs for item in (left, *rights)]
    return pl.pallas_call(
        functools.partial(tail_kernel, orders, [len(rights) for _, rights in pairs], len(sums)),
        in_specs=[SM] + [VM] * (2 + len(flat) + len(sums)),
        out_shape=(
            jax.ShapeDtypeStruct((size // 2, chunk, columns), BF),
            jax.ShapeDtypeStruct((8, columns), F32),
            jax.ShapeDtypeStruct((size // 4 * chunk, columns), BF),
            jax.ShapeDtypeStruct((size // 4 * chunk + 16, columns), BF),
        ),
        scratch_shapes=[pltpu.VMEM((size, chunk, tok), BF) for _ in pairs],
        compiler_params=params(),
        cost_estimate=cost(2.9),
        name="tail_grad",
    )(index, own, other, *flat, *sums)


def late_sums(keep_ref, small_ref, far_refs):
    slots, chunk, columns = keep_ref.shape
    count = slots * chunk
    far = jnp.concatenate([ref[...] for ref in far_refs], 0)
    total = keep_ref[...].astype(F32) + far[:count].astype(F32).reshape(keep_ref.shape)
    extra = far[count:].astype(F32)
    return total, small_ref[...] + extra[:8] + extra[8:]


def late_fold_kernel(keep_ref, small_ref, *refs):
    far_refs, (new_keep_ref, new_small_ref, send_ref) = refs[:-3], refs[-3:]
    total, small = late_sums(keep_ref, small_ref, far_refs)
    half, chunk, columns = new_keep_ref.shape
    new_keep_ref[...] = total[:half].astype(BF)
    new_small_ref[...] = small
    send_ref[: half * chunk, :] = total[half:].reshape(half * chunk, columns).astype(BF)
    send_ref[half * chunk :, :] = parted(small)


def late_fold(keep, small, far):
    slots, chunk, columns = keep.shape
    half = slots // 2
    return pl.pallas_call(
        late_fold_kernel,
        in_specs=[VM, VM] + [VM] * len(far),
        out_shape=(
            jax.ShapeDtypeStruct((half, chunk, columns), BF),
            jax.ShapeDtypeStruct(small.shape, F32),
            jax.ShapeDtypeStruct((half * chunk + 16, columns), BF),
        ),
        compiler_params=params(),
        cost_estimate=cost(0.4),
        name="late_fold",
    )(keep, small, *far)


def finish_kernel(keep_ref, small_ref, far_ref, qkv_hbm, *refs):
    sums, (qkv_ref, sems) = refs[:-2], refs[-2:]
    total, small = late_sums(keep_ref, small_ref, (far_ref,))
    total = total[0]
    local = qkv_ref.shape[2]
    for j in range(3):
        qkv_ref[j] = total[:, j * local : (j + 1) * local]
    copies = fetch(((qkv_ref, qkv_hbm),), sems)
    vector = sums[0].shape[0]
    per_row = small.shape[1] // vector
    spot = 0
    for ref in sums:
        for start in range(0, ref.shape[0], vector):
            row, column = spot // per_row, spot % per_row * vector
            ref[start : start + vector] = small[row, column : column + vector]
            spot += 1
    for copy in copies:
        copy.wait()


def finish(keep, small, far, local, lengths):
    chunk = keep.shape[1]
    return pl.pallas_call(
        finish_kernel,
        in_specs=[VM] * 3,
        out_specs=[HBM] + [VM] * len(lengths),
        out_shape=(
            pltpu.HBM((3, chunk, local), F32),
            *(jax.ShapeDtypeStruct((length,), F32) for length in lengths),
        ),
        scratch_shapes=[pltpu.VMEM((3, chunk, local), F32), pltpu.SemaphoreType.DMA((1,))],
        compiler_params=params(),
        cost_estimate=cost(0.75),
        name="finish",
    )(keep, small, far)


def halves_kernel(keep_ref, far_ref, wout_hbm, proj_hbm, wout_ref, proj_ref, sems):
    total = (keep_ref[...].astype(F32) + far_ref[...].astype(F32))[0]
    local = wout_ref.shape[1]
    wout_ref[...] = total[:, :local]
    proj_ref[...] = total[:, local:]
    copies = fetch(((wout_ref, wout_hbm), (proj_ref, proj_hbm)), sems)
    for copy in copies:
        copy.wait()


def make_halves(keep, far, local, proj):
    chunk = keep.shape[1]
    return pl.pallas_call(
        halves_kernel,
        in_specs=[VM] * 2,
        out_specs=[HBM] * 2,
        out_shape=(pltpu.HBM((chunk, local), F32), pltpu.HBM((chunk, proj), F32)),
        scratch_shapes=[
            pltpu.VMEM((chunk, local), F32),
            pltpu.VMEM((chunk, proj), F32),
            pltpu.SemaphoreType.DMA((2,)),
        ],
        compiler_params=params(),
        cost_estimate=cost(0.4),
        name="halves",
    )(keep, far)


def dense_kernel(keep_ref, far_ref, zero_ref, divisor_ref, out_ref):
    genes = out_ref.shape[0]
    total = (keep_ref[...].astype(F32) + far_ref[...].astype(F32))[0]
    out_ref[...] = (zero_ref[...].astype(F32) + total[:genes]) / divisor_ref[...]


def make_dense(keep, far, zero_embed, divisor):
    return pl.pallas_call(
        dense_kernel,
        in_specs=[VM] * 4,
        out_shape=jax.ShapeDtypeStruct(zero_embed.shape, F32),
        compiler_params=params(),
        cost_estimate=cost(0.7),
        name="dense",
    )(keep, far, zero_embed, divisor)
ORDERS = {
    "dense": ("xzwy", "zxwy"),
    "down": ("yxwz", "xyzw"),
    "up": ("xzyw", "yxzw"),
    "A": ("wyxz", "zyxw"),
    "B": ("yxwz", "zywx"),
}
ADDS = {
    "output": [],
    "sent": [],
    "down": [],
    "feed_back": ["dense"],
    "up": [],
    "norm2": [],
    "A": [],
    "back": [],
    "B": ["swap", "down", "up", "dense", "dense", "A", "B", "down", "up", "B", "A", "down", "dense", "A", "last", "up", "down", "A", "B", "up"],
}


def dp_swap(value, bits):
    size = lax.axis_size("dp")
    pairs = [(2 * i + core, 2 * (i ^ (1 << bits[core])) + core) for i in range(size) for core in range(2)]
    return lax.ppermute(value, ("dp", "mp"), pairs)


def mp_swap(value):
    return lax.ppermute(value, "mp", [(0, 1), (1, 0)])


def slot_offsets(order):
    bits = len(order)
    return [
        sum(((s >> (bits - 1 - place)) & 1) << bit for place, bit in enumerate(order))
        for s in range(1 << bits)
    ]


def chunks_of(left, right, orders):
    offsets = [slot_offsets(order) for order in orders]
    size = len(offsets[0])
    grad = lax.dot_general(left, right, (((0,), (0,)), ((), ())), preferred_element_type=F32)
    chosen = jnp.asarray(offsets, jnp.int32)[lax.axis_index("mp")] ^ lax.axis_index("dp")
    slots = jnp.take(grad.astype(BF).reshape(size, -1, grad.shape[1]), chosen, axis=0)
    return slots[: size // 2], slots[size // 2 :]


def tie(value, *others):
    return lax.optimization_barrier((value,) + others)[0]


class Scatter:
    def __init__(self, orders):
        self.orders = orders
        self.step = 0

    def exchange(self, value):
        self.flight = dp_swap(value, [order[self.step] for order in self.orders])

    def send(self, keep, send):
        self.keep = keep
        self.exchange(send)

    @property
    def waiting(self):
        return self.step == len(self.orders[0]) - 1

    def add(self, token):
        out = fold(tie(self.keep, token), self.flight)
        self.step += 1
        if self.step == len(self.orders[0]):
            self.result = out
            return out
        self.send(*out)
        return out[0]


class LateScatter(Scatter):
    def send(self, keep, small, *pieces):
        self.keep, self.small = keep, small
        bits = [order[self.step] for order in self.orders]
        self.flight = [dp_swap(piece, bits) for piece in pieces]

    def add(self, token):
        self.step += 1
        self.send(*late_fold(tie(self.keep, token), self.small, self.flight))
        return self.keep


class Total:
    def __init__(self, bits):
        self.bits = list(range(bits))

    def send(self, value):
        self.result = value
        if self.bits:
            bit = self.bits.pop()
            self.flight = dp_swap(value, [bit, bit])

    def add(self, token):
        self.send(tie(self.result, token) + self.flight)
        return self.result


def scatter_plan(bits):
    if bits == 4:
        orders, adds = ORDERS, ADDS
        return {name: [["xyzw".index(axis) for axis in one] for one in pair] for name, pair in orders.items()}, adds
    one = list(range(bits))
    adds = {name: [] for name in ADDS}
    adds["B"] = ["swap", "last"] + [name for _ in one for name in list(ORDERS) + ["small"]]
    return {name: [one, one[1:-1] + [0, bits - 1]] for name in ORDERS}, adds


def per_device(
    tokens,
    cell_ids,
    gene_range,
    gene_offset,
    gain1,
    shift1,
    w_qkv,
    w_out,
    out_bias,
    gain2,
    shift2,
    w_up,
    up_bias,
    w_down,
    down_bias,
    w_proj,
    zero_embed,
    dense_cot,
):
    owners = lax.axis_size("dp")
    bits = owners.bit_length() - 1
    divisor = None
    place = jnp.stack([lax.axis_index("dp"), lax.axis_index("mp")])
    genes = zero_embed.shape[0]
    orders, adds = scatter_plan(bits)
    parts = {name: Scatter(pair) for name, pair in orders.items()}
    riding = tokens.shape[1] // owners % 16 == 0
    if riding:
        parts["B"] = LateScatter(orders["B"])
    else:
        parts["small"] = Total(bits)
    gene_range, gene_offset = gene_range.reshape(1, -1), gene_offset.reshape(1, -1)

    finals = {}
    local = w_out.shape[0]

    def service(event, token):
        for name in adds[event]:
            if name == "swap":
                finals["other"] = mp_swap(tie(finals["part"], token))
                continue
            if name == "last":
                token = finals["tokens"] = make_last(tokens, tie(finals["part"], token), finals["other"], grad_middle, gain1)
                continue
            part = parts[name]
            if name == "A" and part.waiting:
                part.result = make_halves(tie(part.keep, token), part.flight, local, w_proj.shape[1])
                token = part.result[0]
            elif name == "dense" and part.waiting:
                part.result = make_dense(tie(part.keep, token), part.flight, zero_embed, divisor)
                token = part.result
            else:
                token = part.add(token)
        return token

    spread = list(range(bits))[::-1]
    gather = [spread, spread[:1] + spread[-1:] + spread[1:-1]]
    payload, tokens, w_near = make_payload(gene_range, gene_offset, dense_cot, tokens, w_qkv, owners)
    payload = payload[None]
    steps = [[order[step] for order in gather] for step in range(bits)]
    far = dp_swap(payload, steps[0])
    out_other = mp_swap(w_out)
    proj_other = mp_swap(w_proj)
    normed1, q, k, v = make_qkv(tokens, gain1, shift1, w_near)
    *mixed, lse, q, k, v, normed1 = make_attend(cell_ids, q, k, v, normed1)
    mixed_other = [mp_swap(half) for half in mixed]
    held = join(payload, tie(far, lse))
    for step in range(1, bits - 2):
        far = dp_swap(held, steps[step])
        if step < bits - 3:
            held = join(held, far)
    middle, normed2 = make_middle(
        tie(tokens, held), mixed, mixed_other, w_out, out_other, out_bias, gain2, shift2
    )
    turned2 = make_turned(place, normed2, orders["up"])
    held = join(held, tie(far, turned2))
    far = dp_swap(held, steps[-2])
    far_first = dp_swap(held, steps[-1])
    *feed_part, act, slope, middle = make_feed(tie(normed2, held), middle, w_up, up_bias, w_down)
    feed_other = [mp_swap(half) for half in feed_part]
    far, far_first = lax.optimization_barrier((far, far_first, act))[:2]
    far_second = dp_swap(far, steps[-1])
    dense_part = parts["dense"]
    block_out, dense_keep, dense_send = make_output(
        place, gene_range, gene_offset, down_bias, middle, feed_part, feed_other, w_proj, dense_part.orders, genes
    )
    dense_part.send(dense_keep, dense_send)
    token = service("output", block_out)
    grad_sent, grad_zero, divisor = make_sent(
        place, gene_range, gene_offset, (held, far, far_first, tie(far_second, token)), genes, gather
    )
    sent_other = mp_swap(grad_sent)
    token = service("sent", grad_sent)
    grad_result, grad_down_bias, down = make_result(
        place, tie(grad_sent, token), sent_other, w_proj, proj_other, act, parts["down"].orders
    )
    parts["down"].send(*down)
    token = service("down", down[0])
    grad_hidden, part2, *halves, grad_up_bias = make_feed_back(tie(grad_result, token), slope, w_down, w_up)
    other2 = [mp_swap(half) for half in halves]
    token = service("feed_back", part2)
    up = make_turned_weight(place, turned2, tie(grad_hidden, token), orders["up"])
    parts["up"].send(*up)
    token = service("up", up[0])
    grad_middle, low, grad_gain2, grad_shift2, grad_out_bias = make_norm2(
        grad_result, tie(part2, token), other2, middle, gain2
    )
    token = service("norm2", low)
    parts["A"].send(*make_weight(place, [(tie(low, token), mixed), (block_out, (grad_sent,))], orders["A"]))
    token = service("A", parts["A"].keep)
    gq, gk, gv, part1, sums1 = make_back(cell_ids, tie(low, token), tokens, w_out, q, k, v, lse, w_qkv)
    sums_other = mp_swap(sums1)
    finals["part"] = part1
    token = service("back", gq)
    sums = [grad_out_bias, grad_gain2, grad_shift2, grad_down_bias, grad_up_bias]
    pairs = [(normed1, (tie(gq, token), gk, gv))]
    last = parts["B"]
    lengths = [item.shape[-1] for item in (sums1, sums1, *sums)]
    if riding:
        last.send(*make_tail(place, pairs, sums1, sums_other, sums, orders["B"]))
        token = service("B", last.keep)
        share_qkv, *small_sums = finish(tie(last.keep, token), last.small, last.flight[0], local, lengths)
    else:
        last.send(*make_weight(place, pairs, orders["B"]))
        sums1 = sums1 + sums_other
        parts["small"].send(jnp.concatenate([sums1[:1], sums1[1:]] + sums, 1))
        token = service("B", last.keep)
        share_qkv = jnp.stack([last.result[:, j * local : (j + 1) * local] for j in range(3)])
        small_sums, at = [], 0
        for length in lengths:
            small_sums.append(parts["small"].result[0, at : at + length])
            at += length
    share_wout, share_proj = parts["A"].result
    small_sums = small_sums[:5] + [small_sums[6], small_sums[5]]
    share_up, share_down, dense = parts["up"].result, parts["down"].result, dense_part.result
    return (
        block_out,
        dense,
        finals["tokens"],
        grad_zero,
        share_qkv,
        share_wout.T,
        share_up,
        share_down.T,
        share_proj,
    ) + tuple(small_sums)


def solution(mesh):
    in_specs = (
        P("dp", None),
        P("dp", None),
        P("dp", None),
        P("dp"),
        P(),
        P(),
        P(None, None, "mp"),
        P("mp", None),
        P(),
        P(),
        P(),
        P(None, "mp"),
        P("mp"),
        P("mp", None),
        P(),
        P(None, "mp"),
        P("dp", "mp"),
        P("dp", "mp"),
    )
    out_specs = (
        P("dp", None),
        P("dp", "mp"),
        P("dp", None),
        P("dp", "mp"),
        P(None, "dp", "mp"),
        P("mp", "dp"),
        P("dp", "mp"),
        P("mp", "dp"),
        P("dp", "mp"),
        P(),
        P(),
        P(),
        P(),
        P(),
        P("mp"),
        P(),
    )
    return jax.shard_map(
        per_device, mesh=mesh, in_specs=in_specs, out_specs=out_specs, check_vma=False
    )
```

```python
import functools
import jax
import jax.numpy as jnp
from jax import lax
from jax.experimental import pallas as pl
from jax.experimental.pallas import tpu as pltpu
from jax.sharding import PartitionSpec as P

HEAD_DIM = 64
EPSILON = 1e-05
BIG = 1e30
BF = jnp.bfloat16
F32 = jnp.float32
MIB = 1 << 20
SLOW, FAST = 1e8, 1e8

NT = (((1,), (1,)), ((), ()))


def dot(left, right):
    return jnp.dot(left, right, preferred_element_type=F32)


def dot_nt(left, right):
    return lax.dot_general(left, right, NT, preferred_element_type=F32)


def whole(shape):
    return pl.BlockSpec(shape, lambda *_: (0,) * len(shape))


VM = pl.BlockSpec(memory_space=pltpu.VMEM)
SM = pl.BlockSpec(memory_space=pltpu.SMEM)


def pick(place_ref, offsets, slot):
    first, second = offsets[0][slot], offsets[1][slot]
    if first == second:
        return first
    return first + place_ref[1] * (second - first)


def slot_of(place_ref, orders, owner):
    other = place_ref[0] ^ owner
    slots = []
    for order in orders:
        bits = len(order)
        slots.append(sum(((other >> bit) & 1) << (bits - 1 - spot) for spot, bit in enumerate(order)))
    return jnp.where(place_ref[1] == 0, slots[0], slots[1])


def params(mib=20):
    return pltpu.CompilerParams(vmem_limit_bytes=mib * MIB)


def cost(micros, rate=FAST):
    return pl.CostEstimate(flops=int(micros * rate), bytes_accessed=1, transcendentals=0)


def near(item):
    return pltpu.with_memory_space_constraint(item, pltpu.HBM)


HBM = pl.BlockSpec(memory_space=pltpu.HBM)


def fetch(pairs, sems):
    copies = [
        pltpu.make_async_copy(source, target, sems.at[i]) for i, (source, target) in enumerate(pairs)
    ]
    for copy in copies:
        copy.start()
    return copies


def line(ref):
    return ref[...].reshape(1, -1)


def norm_stats(values):
    centered = values - jnp.mean(values, -1, keepdims=True)
    inverse = lax.rsqrt(jnp.mean(centered * centered, -1, keepdims=True) + EPSILON)
    return centered * inverse, inverse


def norm_back(grad, normal, inverse, gain):
    scaled = grad * gain
    return inverse * (
        scaled
        - jnp.mean(scaled, -1, keepdims=True)
        - normal * jnp.mean(scaled * normal, -1, keepdims=True)
    )


def gene_rows(genes, owners):
    owners_pad = -(-owners // 16) * 16
    return -(-genes // owners_pad) * owners_pad, owners_pad


def payload_kernel(
    owners_pad, range_hbm, offset_hbm, cot_hbm, x_hbm, w_hbm, out_ref, x_ref, w_ref, range_ref, offset_ref, cot_ref, sems,
):
    copies = fetch(
        (
            (range_hbm, range_ref),
            (offset_hbm, offset_ref),
            (cot_hbm, cot_ref),
            (x_hbm, x_ref),
            (w_hbm, w_ref),
        ),
        sems,
    )
    for copy in copies[:3]:
        copy.wait()
    genes, width = cot_ref.shape
    tok = range_ref.shape[1]
    rows = out_ref.shape[0] - owners_pad
    cot = cot_ref[...].astype(F32)
    if rows > genes:
        cot = jnp.concatenate([cot, jnp.zeros((rows - genes, width), F32)], 0)
    out_ref[:rows, :] = cot.astype(BF)
    owner_hits = jnp.where(
        lax.broadcasted_iota(jnp.int32, (owners_pad, tok), 0) == range_ref[...], 1.0, 0.0
    ).astype(BF)
    offset_hits = jnp.where(
        lax.broadcasted_iota(jnp.int32, (width, tok), 0) == offset_ref[...], 1.0, 0.0
    ).astype(BF)
    out_ref[rows:, :] = dot_nt(owner_hits, offset_hits).astype(BF)
    for copy in copies[3:]:
        copy.wait()


def make_payload(gene_range, gene_offset, cot, tokens, w_qkv, owners):
    genes, width = cot.shape
    tok = gene_offset.shape[1]
    rows, owners_pad = gene_rows(genes, owners)
    operands = (gene_range, gene_offset, cot, tokens, w_qkv)
    return pl.pallas_call(
        functools.partial(payload_kernel, owners_pad),
        in_specs=[HBM] * 5,
        out_specs=[VM] * 3,
        out_shape=(
            jax.ShapeDtypeStruct((rows + owners_pad, width), BF),
            jax.ShapeDtypeStruct(tokens.shape, BF),
            jax.ShapeDtypeStruct(w_qkv.shape, BF),
        ),
        scratch_shapes=[
            pltpu.VMEM((1, tok), jnp.int32),
            pltpu.VMEM((1, tok), jnp.int32),
            pltpu.VMEM((genes, width), BF),
            pltpu.SemaphoreType.DMA((5,)),
        ],
        compiler_params=params(),
        cost_estimate=cost(1.8, SLOW),
        name="payload",
    )(*map(near, operands))


def join_kernel(near_ref, far_ref, out_ref):
    half = near_ref.shape[0]
    out_ref[:half] = near_ref[...]
    out_ref[half:] = far_ref[...]


def join(near, far):
    return pl.pallas_call(
        join_kernel,
        in_specs=[VM, VM],
        out_shape=jax.ShapeDtypeStruct((2 * near.shape[0],) + near.shape[1:], near.dtype),
        compiler_params=params(16 if near.shape[0] < 8 else 32),
        cost_estimate=cost(0.4, SLOW),
        name="join",
    )(near, far)


def sent_kernel(genes, orders, count, place_ref, range_hbm, offset_hbm, *refs):
    range_ref, offset_ref, sems = refs[-3:]
    refs = refs[:-3]
    hist_refs, held_refs = refs[:count], refs[count : 2 * count]
    sent_ref, zero_ref, div_ref, total, by_gene, low = refs[2 * count :]
    batch, rows, width = held_refs[0].shape
    size, owners_pad, _ = hist_refs[0].shape
    step = pl.program_id(0)
    me = place_ref[0]
    tok = range_ref.shape[1]

    @pl.when(step == 0)
    def _():
        copies = fetch(((range_hbm, range_ref), (offset_hbm, offset_ref)), sems)
        counts = jnp.zeros((owners_pad, width), F32)
        for ref in hist_refs:
            for slot in range(size):
                counts += ref[slot].astype(F32)
        if owners_pad < 128:
            counts = jnp.concatenate([counts, jnp.zeros((128 - owners_pad, width), F32)], 0)
        by_gene[...] = 1.0 + counts.T[:rows]
        total[...] = jnp.zeros_like(total)
        for copy in copies:
            copy.wait()

    spread = by_gene[...]
    owner_lane = lax.broadcasted_iota(jnp.int32, spread.shape, 1)
    other = range_ref[...] ^ me
    slots = [
        sum(((other >> bit) & 1) << spot for spot, bit in enumerate(order)) for order in orders
    ]
    slots = jnp.where(place_ref[1] == 0, slots[0], slots[1])
    side = slots // size
    near = slots - side * size - step * batch
    index = jnp.where((near >= 0) & (near < batch), (side * batch + near) * rows + offset_ref[...], -1)
    columns = jnp.broadcast_to(index, (128, tok)).T
    for side, ref in enumerate(held_refs):
        for spot in range(batch):
            slot = side * size + step * batch + spot
            offset = jnp.int32(0)
            for core, order in enumerate(orders):
                one = sum(((slot >> i) & 1) << bit for i, bit in enumerate(order))
                offset = jnp.where(place_ref[1] == core, one, offset)
            divisor = jnp.sum(jnp.where(owner_lane == (me ^ offset), spread, 0.0), 1, keepdims=True)
            grad = ref[spot].astype(F32) * (1.0 / divisor)
            if spot == 0 and side == 0:

                @pl.when(step == 0)
                def _():
                    zero_ref[...] = grad[:genes]
                    div_ref[...] = jnp.broadcast_to(divisor[:genes], (genes, width))

            at = (side * batch + spot) * rows
            low[at : at + rows, :] = grad.astype(BF)
    lane = lax.broadcasted_iota(jnp.int32, (tok, 128), 1)
    hits = jnp.concatenate(
        [
            jnp.where(columns == lane + at, 1.0, 0.0).astype(BF)
            for at in range(0, count * batch * rows, 128)
        ],
        1,
    )
    total[...] += dot(hits, low[...])

    @pl.when(step == pl.num_programs(0) - 1)
    def _():
        sent_ref[...] = total[...].astype(BF)


def make_sent(place, gene_range, gene_offset, held, genes, orders):
    size, height, width = held[0].shape
    count = len(held)
    owners = count * size
    rows, owners_pad = gene_rows(genes, owners)
    batch = min(size, 4)
    tok = gene_offset.shape[1]
    hist = pl.BlockSpec((size, owners_pad, width), lambda i: (0, rows // owners_pad, 0))
    cots = pl.BlockSpec((batch, rows, width), lambda i: (i, 0, 0))
    return pl.pallas_call(
        functools.partial(sent_kernel, genes, orders, count),
        grid=(size // batch,),
        in_specs=[SM, HBM, HBM] + [hist] * count + [cots] * count,
        out_specs=(whole((tok, width)), whole((genes, width)), whole((genes, width))),
        out_shape=(
            jax.ShapeDtypeStruct((tok, width), BF),
            jax.ShapeDtypeStruct((genes, width), F32),
            jax.ShapeDtypeStruct((genes, width), F32),
        ),
        scratch_shapes=[
            pltpu.VMEM((tok, width), F32),
            pltpu.VMEM((rows, 128 * -(-owners // 128)), F32),
            pltpu.VMEM((count * batch * rows, width), BF),
            pltpu.VMEM((1, tok), jnp.int32),
            pltpu.VMEM((1, tok), jnp.int32),
            pltpu.SemaphoreType.DMA((2,)),
        ],
        compiler_params=params(20 if owners <= 16 else 48),
        cost_estimate=cost(2.5, SLOW),
        name="grad_sent",
    )(place, near(gene_range), near(gene_offset), *held, *held)


def qkv_kernel(x_ref, gain_ref, shift_ref, w_ref, normed_ref, q_ref, k_ref, v_ref):
    normal, _ = norm_stats(x_ref[...].astype(F32))
    normed = (normal * line(gain_ref) + line(shift_ref)).astype(BF)
    normed_ref[...] = normed
    for j, out in enumerate((q_ref, k_ref, v_ref)):
        out[...] = dot(normed, w_ref[j]).astype(BF)


def make_qkv(tokens, gain, shift, w_qkv):
    tok, width = tokens.shape
    local = w_qkv.shape[2]
    one = jax.ShapeDtypeStruct((tok, local), BF)
    return pl.pallas_call(
        qkv_kernel,
        in_specs=[VM] * 4,
        out_shape=(jax.ShapeDtypeStruct((tok, width), BF), one, one, one),
        compiler_params=params(),
        cost_estimate=cost(1.7, SLOW),
        name="qkv",
    )(tokens, gain, shift, w_qkv)


def masked_pair(q_pair, k_pair, cells, half, cell_count=8):
    lane = lax.broadcasted_iota(jnp.int32, q_pair.shape, 1)
    own = (lane // HEAD_DIM) == half
    place = lane % HEAD_DIM
    same = place == cells
    q_mask = jnp.where((place < cell_count) & jnp.logical_not(same), -BIG, 0.0)
    k_mask = jnp.where(same, 1.0, 0.0)
    scaled = q_pair.astype(F32) * (HEAD_DIM**-0.5)
    q_head = jnp.where(own, scaled, q_mask).astype(BF)
    k_head = jnp.where(own, k_pair.astype(F32), k_mask).astype(BF)
    return q_head, k_head


def attend_kernel(
    cells_ref, q_ref, k_ref, v_ref, normed_ref, upper_ref, lower_ref, lse_ref, q_far, k_far, v_far, normed_far, sems,
):
    copies = fetch(((q_ref, q_far), (k_ref, k_far), (v_ref, v_far), (normed_ref, normed_far)), sems)
    tok, local = q_ref.shape
    half_tok = tok // 2
    cells = jnp.broadcast_to(cells_ref[...], (128, tok)).T
    lane = lax.broadcasted_iota(jnp.int32, (tok, 128), 1)
    logs = jnp.zeros((tok, 128), F32)
    for pair in range(local // 128):
        cut = slice(pair * 128, pair * 128 + 128)
        q_pair, k_pair, v_pair = q_ref[:, cut], k_ref[:, cut], v_ref[:, cut]
        heads = []
        for half in range(2):
            q_head, k_head = masked_pair(q_pair, k_pair, cells, half)
            scores = dot_nt(q_head, k_head)
            top = jnp.max(scores, 1, keepdims=True)
            powers = jnp.exp(scores - top)
            total = jnp.sum(powers, 1, keepdims=True)
            probs = (powers * (1.0 / total)).astype(BF)
            logs = jnp.where(lane == 2 * pair + half, top + jnp.log(total), logs)
            heads.append(dot(probs, v_pair))
        mixed = jnp.where(lane < HEAD_DIM, heads[0], heads[1]).astype(BF)
        upper_ref[:, cut] = mixed[:half_tok]
        lower_ref[:, cut] = mixed[half_tok:]
    lse_ref[...] = logs.T[: lse_ref.shape[0]]
    for copy in copies:
        copy.wait()


def make_attend(cell_ids, q, k, v, normed):
    tok, local = q.shape
    heads = -(-local // HEAD_DIM // 8) * 8
    half = jax.ShapeDtypeStruct((tok // 2, local), BF)
    return pl.pallas_call(
        attend_kernel,
        in_specs=[VM] * 5,
        out_specs=[VM] * 3 + [HBM] * 4,
        out_shape=(
            half,
            half,
            jax.ShapeDtypeStruct((heads, tok), F32),
            *(pltpu.HBM(item.shape, BF) for item in (q, k, v, normed)),
        ),
        scratch_shapes=[pltpu.SemaphoreType.DMA((4,))],
        compiler_params=params(),
        cost_estimate=cost(2.9, SLOW),
        name="attend",
    )(cell_ids, q, k, v, normed)


def pair_back(cells, q_pair, k_pair, v_pair, gm_pair, lse, lane):
    factor = HEAD_DIM**-0.5
    k_turned = k_pair.astype(F32).T.astype(BF)
    gq_halves = []
    gk = gv = None
    for half in range(2):
        own = (lane // HEAD_DIM) == half
        q_head, k_head = masked_pair(q_pair, k_pair, cells, half)
        v_head = jnp.where(own, v_pair.astype(F32), 0.0).astype(BF)
        probs = jnp.exp(dot_nt(k_head, q_head) - lse[half : half + 1])
        part = dot(probs.astype(BF), gm_pair)
        gv = part if half == 0 else jnp.where(own, part, gv)
        grad_probs = dot_nt(v_head, gm_pair)
        spread = jnp.sum(probs * grad_probs, 0, keepdims=True)
        grad_scores = (probs * (grad_probs - spread)).astype(BF)
        part = dot(grad_scores, q_pair)
        gk = part if half == 0 else jnp.where(own, part, gk)
        gq_halves.append(dot(k_turned[half * HEAD_DIM : (half + 1) * HEAD_DIM], grad_scores))
    gq = (jnp.concatenate(gq_halves, 0).T * factor).astype(BF)
    return gq, (gk * factor).astype(BF), gv.astype(BF)


GELU_A = 0.7978845608028654
GELU_B = 0.044715


def middle_kernel(
    x_ref, own_upper_ref, own_lower_ref, upper_ref, lower_ref, wo_ref, wo_other_ref, bias_ref, gain_ref, shift_ref,
    middle_ref, normed_ref,
):
    own = jnp.concatenate([own_upper_ref[...], own_lower_ref[...]], 0)
    other = jnp.concatenate([upper_ref[...], lower_ref[...]], 0)
    attended = dot(own, wo_ref[...]) + dot(other, wo_other_ref[...])
    middle = x_ref[...].astype(F32) + attended + line(bias_ref)
    middle_ref[...] = middle
    normal, _ = norm_stats(middle)
    normed_ref[...] = (normal * line(gain_ref) + line(shift_ref)).astype(BF)


def make_middle(tokens, mixed, mixed_other, w_out, out_other, out_bias, gain, shift):
    tok, width = tokens.shape
    return pl.pallas_call(
        middle_kernel,
        in_specs=[VM] * 10,
        out_shape=(jax.ShapeDtypeStruct((tok, width), F32), jax.ShapeDtypeStruct((tok, width), BF)),
        compiler_params=params(),
        cost_estimate=cost(1.4, SLOW),
        name="middle",
    )(tokens, *mixed, *mixed_other, w_out, out_other, out_bias, gain, shift)


def feed_kernel(
    chunk, normed_ref, middle_ref, up_ref, up_bias_ref, down_ref,
    *refs,
):
    quarters, (act_far, slope_far, middle_far, act_ref, slope_ref, sems) = refs[:4], refs[4:]
    copies = fetch(((middle_ref, middle_far),), sems)
    normed = normed_ref[...]
    up_bias = line(up_bias_ref)
    units = up_ref.shape[1]
    for place, at in enumerate(range(0, units, chunk)):
        cut = slice(at, at + chunk)
        hidden = dot(normed, up_ref[:, cut]) + up_bias[:, cut]
        square = hidden * hidden
        curve = jnp.tanh(hidden * (GELU_A + (GELU_A * GELU_B) * square))
        half = 0.5 * hidden
        act_ref[:, cut] = (half + half * curve).astype(BF)
        slope = (0.5 + 0.5 * curve) + half * (1.0 - curve * curve) * (
            GELU_A + (3 * GELU_A * GELU_B) * square
        )
        slope_ref[:, cut] = slope.astype(BF)
        copies += fetch(
            ((act_ref.at[:, cut], act_far.at[:, cut]), (slope_ref.at[:, cut], slope_far.at[:, cut])),
            sems.at[pl.ds(1 + 2 * place, 2)],
        )
    feed = dot(act_ref[...], down_ref[...]).astype(BF)
    for place, ref in enumerate(quarters):
        ref[...] = feed[place * ref.shape[0] : (place + 1) * ref.shape[0]]
    for copy in copies:
        copy.wait()


def make_feed(normed, middle, w_up, up_bias, w_down, chunk=768):
    tok, width = normed.shape
    units = w_up.shape[1]
    return pl.pallas_call(
        functools.partial(feed_kernel, chunk),
        in_specs=[VM] * 5,
        out_specs=[VM] * 4 + [HBM] * 3,
        out_shape=(
            *(jax.ShapeDtypeStruct((tok // 4, width), BF) for _ in range(4)),
            pltpu.HBM((tok, units), BF),
            pltpu.HBM((tok, units), BF),
            pltpu.HBM((tok, width), F32),
        ),
        scratch_shapes=[
            pltpu.VMEM((tok, units), BF),
            pltpu.VMEM((tok, units), BF),
            pltpu.SemaphoreType.DMA((1 + 2 * units // chunk,)),
        ],
        compiler_params=params(24),
        cost_estimate=cost(4.1, SLOW),
        name="feed",
    )(normed, middle, w_up, up_bias, w_down)


def result_kernel(
    orders, place_ref, sent_ref, other_ref, wp_ref, wp_other_ref, act_ref,
    result_ref, bias_ref, keep_ref, send_ref, chosen,
):
    size, chunk, tok = chosen.shape
    half = size // 2 * chunk
    result = dot_nt(sent_ref[...], wp_ref[...]) + dot_nt(other_ref[...], wp_other_ref[...])
    low = result.astype(BF)
    result_ref[...] = low
    bias_ref[...] = jnp.sum(low.astype(F32), 0, keepdims=True)
    turned = low.astype(F32).T.astype(BF).reshape(chosen.shape)
    for owner in range(size):
        chosen[slot_of(place_ref, orders, owner)] = turned[owner]
    for at in range(0, act_ref.shape[1], 512):
        cut = slice(at, at + 512)
        right = act_ref[:, cut]
        out = (size // 2, chunk, right.shape[1])
        keep_ref[:, :, cut] = dot(chosen[: size // 2].reshape(half, tok), right).astype(BF).reshape(out)
        send_ref[:, :, cut] = dot(chosen[size // 2 :].reshape(half, tok), right).astype(BF).reshape(out)


def plain_result_kernel(sent_ref, other_ref, wp_ref, wp_other_ref, result_ref, bias_ref):
    result = dot_nt(sent_ref[...], wp_ref[...]) + dot_nt(other_ref[...], wp_other_ref[...])
    low = result.astype(BF)
    result_ref[...] = low
    bias_ref[...] = jnp.sum(low.astype(F32), 0, keepdims=True)


def make_result(index, sent, sent_other, w_proj, proj_other, act, orders):
    tok = sent.shape[0]
    width = w_proj.shape[0]
    units = act.shape[1]
    size = 1 << len(orders[0])
    chunk = width // size
    outs = (jax.ShapeDtypeStruct((tok, width), BF), jax.ShapeDtypeStruct((1, width), F32))
    if chunk % 16:
        result, bias = pl.pallas_call(
            plain_result_kernel, in_specs=[VM] * 4, out_shape=outs, compiler_params=params(), name="result"
        )(sent, sent_other, w_proj, proj_other)
        return result, bias, make_weight(index, [(result, (act,))], orders)
    half = jax.ShapeDtypeStruct((size // 2, chunk, units), BF)
    result, bias, keep, send = pl.pallas_call(
        functools.partial(result_kernel, orders),
        in_specs=[SM] + [VM] * 5,
        out_shape=(*outs, half, half),
        scratch_shapes=[pltpu.VMEM((size, chunk, tok), BF)],
        compiler_params=params(),
        cost_estimate=cost(3.7, SLOW),
        name="result",
    )(index, sent, sent_other, w_proj, proj_other, act)
    return result, bias, (keep, send)


def feed_back_kernel(
    chunk, result_ref, slope_ref, down_ref, up_ref, hidden_ref, normed_ref, upper_ref, lower_ref, up_bias_ref
):
    low = result_ref[...]
    for at in range(0, up_ref.shape[1], chunk):
        cut = slice(at, at + chunk)
        grad = (dot_nt(low, down_ref[cut]) * slope_ref[:, cut].astype(F32)).astype(BF)
        hidden_ref[:, cut] = grad
        up_bias_ref[:, cut] = jnp.sum(grad.astype(F32), 0, keepdims=True)
    normed = dot_nt(hidden_ref[...], up_ref[...]).astype(BF)
    normed_ref[...] = normed
    half = upper_ref.shape[0]
    upper_ref[...] = normed[:half]
    lower_ref[...] = normed[half:]


def make_feed_back(result, slope, w_down, w_up, chunk=768):
    tok, width = result.shape
    units = w_up.shape[1]
    return pl.pallas_call(
        functools.partial(feed_back_kernel, chunk),
        in_specs=[VM] * 4,
        out_shape=(
            jax.ShapeDtypeStruct((tok, units), BF),
            jax.ShapeDtypeStruct((tok, width), BF),
            jax.ShapeDtypeStruct((tok // 2, width), BF),
            jax.ShapeDtypeStruct((tok // 2, width), BF),
            jax.ShapeDtypeStruct((1, units), F32),
        ),
        compiler_params=params(24),
        cost_estimate=cost(2.8),
        name="feed_back",
    )(result, slope, w_down, w_up)


def turn_kernel(orders, place_ref, left_ref, out_ref):
    turned = left_ref[...].astype(F32).T.astype(BF).reshape(out_ref.shape)
    for owner in range(out_ref.shape[0]):
        out_ref[slot_of(place_ref, orders, owner)] = turned[owner]


def make_turned(index, left, orders):
    tok, width = left.shape
    size = 1 << len(orders[0])
    if width // size % 16:
        return left
    return pl.pallas_call(
        functools.partial(turn_kernel, orders),
        in_specs=[SM, VM],
        out_shape=jax.ShapeDtypeStruct((size, width // size, tok), BF),
        compiler_params=params(),
        cost_estimate=cost(0.9, SLOW),
        name="turn",
    )(index, left)


def turned_kernel(chosen_ref, right_ref, keep_ref, send_ref):
    size, chunk, tok = chosen_ref.shape
    half = size // 2 * chunk
    for at in range(0, right_ref.shape[1], 512):
        cut = slice(at, at + 512)
        right = right_ref[:, cut]
        out = (size // 2, chunk, right.shape[1])
        keep_ref[:, :, cut] = dot(chosen_ref[: size // 2].reshape(half, tok), right).astype(BF).reshape(out)
        send_ref[:, :, cut] = dot(chosen_ref[size // 2 :].reshape(half, tok), right).astype(BF).reshape(out)


def make_turned_weight(index, left, right, orders):
    if left.ndim == 2:
        return make_weight(index, [(left, (right,))], orders)
    size, chunk, _ = left.shape
    out = jax.ShapeDtypeStruct((size // 2, chunk, right.shape[1]), BF)
    return pl.pallas_call(
        turned_kernel,
        in_specs=[VM, VM],
        out_shape=(out, out),
        compiler_params=params(),
        cost_estimate=cost(2.2),
        name="up_grad",
    )(left, right)


def weight_kernel(orders, groups, place_ref, *refs):
    ins = refs[: -2 - len(groups)]
    keep_ref, send_ref = refs[len(ins) : len(ins) + 2]
    size, chunk, tok = refs[-1].shape
    half = size // 2 * chunk
    at = place = 0
    for count, chosen in zip(groups, refs[len(ins) + 2 :]):
        turned = ins[place][...].astype(F32).T.astype(BF).reshape(chosen.shape)
        for owner in range(size):
            chosen[slot_of(place_ref, orders, owner)] = turned[owner]
        rights = [ref[...] for ref in ins[place + 1 : place + 1 + count]]
        if rights[0].shape[0] < tok:
            rights = [jnp.concatenate(rights, 0)]
        for right in rights:
            cut = slice(at, at + right.shape[1])
            out = (size // 2, chunk, right.shape[1])
            keep_ref[:, :, cut] = dot(chosen[: size // 2].reshape(half, tok), right).astype(BF).reshape(out)
            send_ref[:, :, cut] = dot(chosen[size // 2 :].reshape(half, tok), right).astype(BF).reshape(out)
            at += right.shape[1]
        place += 1 + count


def make_weight(index, pairs, orders):
    tok, width = pairs[0][0].shape
    columns = sum(right.shape[1] * right.shape[0] for _, rights in pairs for right in rights) // tok
    size = 1 << len(orders[0])
    chunk = width // size
    if chunk % 16:
        pairs = [
            (left, (jnp.concatenate(rights),) if rights[0].shape[0] < tok else rights) for left, rights in pairs
        ]
        parts = [chunks_of(left, right, orders) for left, rights in pairs for right in rights]
        return tuple(jnp.concatenate(side, 2) for side in zip(*parts))
    out = jax.ShapeDtypeStruct((size // 2, chunk, columns), BF)
    flat = [item for left, rights in pairs for item in (left, *rights)]
    return pl.pallas_call(
        functools.partial(weight_kernel, orders, [len(rights) for _, rights in pairs]),
        in_specs=[SM] + [VM] * len(flat),
        out_shape=(out, out),
        scratch_shapes=[pltpu.VMEM((size, chunk, tok), BF) for _ in pairs],
        compiler_params=params(),
        cost_estimate=cost(2.2),
        name="weight_grad",
    )(index, *flat)


def norm2_kernel(
    result_ref, part_ref, upper_ref, lower_ref, middle_ref, gain_ref,
    grad_middle_ref, low_ref, gain_sum_ref, shift_sum_ref, bias_sum_ref,
):
    other = jnp.concatenate([upper_ref[...], lower_ref[...]], 0)
    grad = part_ref[...].astype(F32) + other.astype(F32)
    normal, inverse = norm_stats(middle_ref[...])
    gain_sum_ref[...] = jnp.sum(grad * normal, 0, keepdims=True)
    shift_sum_ref[...] = jnp.sum(grad, 0, keepdims=True)
    middle = result_ref[...].astype(F32) + norm_back(grad, normal, inverse, line(gain_ref))
    grad_middle_ref[...] = middle
    bias_sum_ref[...] = jnp.sum(middle, 0, keepdims=True)
    low_ref[...] = middle.astype(BF)


def make_norm2(result, part, other, middle, gain):
    tok, width = middle.shape
    small = jax.ShapeDtypeStruct((1, width), F32)
    return pl.pallas_call(
        norm2_kernel,
        in_specs=[VM] * 6,
        out_shape=(
            jax.ShapeDtypeStruct((tok, width), F32), jax.ShapeDtypeStruct((tok, width), BF), small, small, small
        ),
        compiler_params=params(),
        cost_estimate=cost(2.4),
        name="norm2",
    )(result, part, *other, middle, gain)


def back_kernel(
    cells_ref, low_ref, x_ref, wo_ref, q_ref, k_ref, v_ref, lse_ref, w_ref, gq_ref, gk_ref, gv_ref, normed_ref, sums_ref,
):
    tok = q_ref.shape[0]
    cells = jnp.broadcast_to(cells_ref[...], (128, tok)).T
    lane = lax.broadcasted_iota(jnp.int32, (tok, 128), 1)
    gm = dot_nt(low_ref[...], wo_ref[...]).astype(BF)
    for pair in range(q_ref.shape[1] // 128):
        cut = slice(pair * 128, pair * 128 + 128)
        out = pair_back(
            cells, q_ref[:, cut], k_ref[:, cut], v_ref[:, cut], gm[:, cut], lse_ref[2 * pair : 2 * pair + 2], lane
        )
        for ref, value in zip((gq_ref, gk_ref, gv_ref), out):
            ref[:, cut] = value
    total = dot_nt(gq_ref[...], w_ref[0]) + dot_nt(gk_ref[...], w_ref[1]) + dot_nt(gv_ref[...], w_ref[2])
    normal, _ = norm_stats(x_ref[...].astype(F32))
    sums_ref[0:1] = jnp.sum(total * normal, 0, keepdims=True)
    sums_ref[1:2] = jnp.sum(total, 0, keepdims=True)
    normed_ref[...] = total.astype(BF)


def make_back(cell_ids, low, tokens, w_out, q, k, v, lse, w_qkv):
    tok, local = q.shape
    width = low.shape[1]
    one = jax.ShapeDtypeStruct((tok, local), BF)
    return pl.pallas_call(
        back_kernel,
        in_specs=[VM] * 9,
        out_shape=(
            one, one, one, jax.ShapeDtypeStruct((tok, width), BF), jax.ShapeDtypeStruct((2, width), F32)
        ),
        compiler_params=params(),
        cost_estimate=cost(6.4),
        name="back",
    )(cell_ids, low, tokens, w_out, q, k, v, lse, w_qkv)


def last_kernel(x_ref, part_ref, other_ref, middle_ref, gain_ref, out_hbm, out_ref, sems):
    half = x_ref.shape[0] // 2
    cuts = [pl.ds(place * half, half) for place in range(2)]
    out = []
    for place, cut in enumerate(cuts):
        grad = part_ref[cut].astype(F32) + other_ref[cut].astype(F32)
        normal, inverse = norm_stats(x_ref[cut].astype(F32))
        grad = norm_back(grad, normal, inverse, line(gain_ref))
        out_ref[cut] = middle_ref[cut] + grad
        out += fetch([(out_ref.at[cut], out_hbm.at[cut])], sems.at[pl.ds(place, 1)])
    for copy in out:
        copy.wait()


def make_last(tokens, part, other, grad_middle, gain):
    tok, width = tokens.shape
    return pl.pallas_call(
        last_kernel,
        in_specs=[VM] * 5,
        out_specs=HBM,
        out_shape=pltpu.HBM((tok, width), F32),
        scratch_shapes=[pltpu.VMEM((tok, width), F32), pltpu.SemaphoreType.DMA((2,))],
        compiler_params=params(),
        cost_estimate=cost(2.3),
        name="last",
    )(tokens, part, other, grad_middle, gain)


def output_kernel(orders, place_ref, range_hbm, offset_hbm, bias_hbm, middle_hbm, *refs):
    own, other = refs[:4], refs[4:8]
    wp_ref, out_ref, keep_ref, send_ref, range_ref, offset_ref, bias_ref, middle_ref, hits, sems = refs[8:]
    copies = fetch(
        ((range_hbm, range_ref), (offset_hbm, offset_ref), (bias_hbm, bias_ref), (middle_hbm, middle_ref)), sems
    )
    half, rows, width = keep_ref.shape
    tok = range_ref.shape[1]
    for copy in copies[:2]:
        copy.wait()
    index = slot_of(place_ref, orders, range_ref[...]) * rows + offset_ref[...]
    gene = lax.broadcasted_iota(jnp.int32, (rows, tok), 0)
    batch = hits.shape[0] // rows

    def find(first):
        for spot in range(batch):
            hits[spot * rows : (spot + 1) * rows, :] = jnp.where(
                gene + (first + spot) * rows == index, 1.0, 0.0
            ).astype(BF)

    find(0)
    for copy in copies[2:]:
        copy.wait()
    feed = jnp.concatenate([left[...].astype(F32) + right[...].astype(F32) for left, right in zip(own, other)], 0)
    low = (middle_ref[...] + feed + line(bias_ref)).astype(BF)
    out_ref[...] = low
    sent = dot(low, wp_ref[...]).astype(BF)
    for first in range(0, 2 * half, batch):
        if first:
            find(first)
        ref = keep_ref if first < half else send_ref
        at = first % half
        ref[at : at + batch] = dot(hits[...], sent).astype(BF).reshape((batch, rows, width))


def make_output(place, gene_range, gene_offset, bias, middle, own, other, w_proj, orders, genes):
    tok, width = middle.shape
    proj = w_proj.shape[1]
    owners = 1 << len(orders[0])
    rows = -(-genes // 16) * 16
    half = jax.ShapeDtypeStruct((owners // 2, rows, proj), BF)
    return pl.pallas_call(
        functools.partial(output_kernel, orders),
        in_specs=[SM] + [HBM] * 4 + [VM] * 9,
        out_shape=(jax.ShapeDtypeStruct((tok, width), BF), half, half),
        scratch_shapes=[
            pltpu.VMEM((1, tok), jnp.int32),
            pltpu.VMEM((1, tok), jnp.int32),
            pltpu.VMEM((width,), F32),
            pltpu.VMEM((tok, width), F32),
            pltpu.VMEM((min(owners // 2, 8) * rows, tok), BF),
            pltpu.SemaphoreType.DMA((4,)),
        ],
        compiler_params=params(20 if owners <= 16 else 48),
        cost_estimate=cost(2.8, SLOW),
        name="output",
    )(place, near(gene_range), near(gene_offset), near(bias), near(middle), *own, *other, w_proj)


def fold_kernel(keep_ref, far_ref, new_keep_ref, send_ref):
    total = keep_ref[...].astype(F32) + far_ref[...].astype(F32)
    half = total.shape[0] // 2
    new_keep_ref[...] = total[:half].astype(BF)
    send_ref[...] = total[half:].astype(BF)


def last_fold_kernel(keep_ref, far_ref, out_hbm, out_ref, sems):
    out_ref[...] = (keep_ref[...].astype(F32) + far_ref[...].astype(F32))[0]
    for copy in fetch(((out_ref, out_hbm),), sems):
        copy.wait()


def fold(keep, far):
    slots, rows, columns = keep.shape
    if slots == 1:
        return pl.pallas_call(
            last_fold_kernel,
            in_specs=[VM, VM],
            out_specs=HBM,
            out_shape=pltpu.HBM((rows, columns), F32),
            scratch_shapes=[pltpu.VMEM((rows, columns), F32), pltpu.SemaphoreType.DMA((1,))],
            compiler_params=params(16),
            cost_estimate=cost(0.4),
            name="last_fold",
        )(keep, far)
    return pl.pallas_call(
        fold_kernel,
        in_specs=[VM, VM],
        out_shape=(jax.ShapeDtypeStruct((slots // 2, rows, columns), BF),) * 2,
        compiler_params=params(16 if slots <= 8 else 48),
        cost_estimate=cost(0.4),
        name="fold",
    )(keep, far)


def parted(value):
    high = value.astype(BF).astype(F32)
    return jnp.concatenate([high, value - high], 0).astype(BF)


def tail_kernel(orders, groups, vectors, place_ref, own_ref, other_ref, *refs):
    keep_ref, small_ref, send_ref, rest_ref = refs[-4 - len(groups) : -len(groups)]
    size, chunk, tok = refs[-1].shape
    half = size // 2 * chunk
    quarter = send_ref.shape[0]
    at = place = 0
    for count, chosen in zip(groups, refs[-len(groups) :]):
        if len(refs[place].shape) == 3:
            chosen = refs[place]
        else:
            turned = refs[place][...].astype(F32).T.astype(BF).reshape(chosen.shape)
            for owner in range(size):
                chosen[slot_of(place_ref, orders, owner)] = turned[owner]
        rights = [ref[...] for ref in refs[place + 1 : place + 1 + count]]
        if rights[0].shape[0] < tok:
            rights = [jnp.concatenate(rights, 0)]
        for right in rights:
            cut = slice(at, at + right.shape[1])
            out = (size // 2, chunk, right.shape[1])
            keep_ref[:, :, cut] = dot(chosen[: size // 2].reshape(half, tok), right).astype(BF).reshape(out)
            sent = dot(chosen[size // 2 :].reshape(half, tok), right).astype(BF)
            send_ref[:, cut] = sent[:quarter]
            rest_ref[: half - quarter, cut] = sent[quarter:]
            at += right.shape[1]
        place += 1 + count
    sums = own_ref[...] + other_ref[...]
    vector = sums.shape[1]
    per_row = small_ref.shape[1] // vector
    pieces = [sums[0:1], sums[1:2]]
    for ref in refs[place : place + vectors]:
        pieces += [ref[:, start : start + vector] for start in range(0, ref.shape[1], vector)]
    small_ref[...] = jnp.zeros_like(small_ref)
    for spot, piece in enumerate(pieces):
        row, column = spot // per_row, spot % per_row * vector
        small_ref[row : row + 1, column : column + vector] = piece
    rest_ref[half - quarter :, :] = parted(small_ref[...])


def make_tail(index, pairs, own, other, sums, orders):
    tok, width = pairs[0][1][0].shape[0], own.shape[1]
    columns = sum(right.shape[1] * right.shape[0] for _, rights in pairs for right in rights) // tok
    size = 1 << len(orders[0])
    chunk = width // size
    flat = [item for left, rights in pairs for item in (left, *rights)]
    return pl.pallas_call(
        functools.partial(tail_kernel, orders, [len(rights) for _, rights in pairs], len(sums)),
        in_specs=[SM] + [VM] * (2 + len(flat) + len(sums)),
        out_shape=(
            jax.ShapeDtypeStruct((size // 2, chunk, columns), BF),
            jax.ShapeDtypeStruct((8, columns), F32),
            jax.ShapeDtypeStruct((size // 4 * chunk, columns), BF),
            jax.ShapeDtypeStruct((size // 4 * chunk + 16, columns), BF),
        ),
        scratch_shapes=[pltpu.VMEM((size, chunk, tok), BF) for _ in pairs],
        compiler_params=params(),
        cost_estimate=cost(2.9),
        name="tail_grad",
    )(index, own, other, *flat, *sums)


def late_sums(keep_ref, small_ref, far_refs):
    slots, chunk, columns = keep_ref.shape
    count = slots * chunk
    far = jnp.concatenate([ref[...] for ref in far_refs], 0)
    total = keep_ref[...].astype(F32) + far[:count].astype(F32).reshape(keep_ref.shape)
    extra = far[count:].astype(F32)
    return total, small_ref[...] + extra[:8] + extra[8:]


def late_fold_kernel(keep_ref, small_ref, *refs):
    far_refs, (new_keep_ref, new_small_ref, send_ref) = refs[:-3], refs[-3:]
    total, small = late_sums(keep_ref, small_ref, far_refs)
    half, chunk, columns = new_keep_ref.shape
    new_keep_ref[...] = total[:half].astype(BF)
    new_small_ref[...] = small
    send_ref[: half * chunk, :] = total[half:].reshape(half * chunk, columns).astype(BF)
    send_ref[half * chunk :, :] = parted(small)


def late_fold(keep, small, far):
    slots, chunk, columns = keep.shape
    half = slots // 2
    return pl.pallas_call(
        late_fold_kernel,
        in_specs=[VM, VM] + [VM] * len(far),
        out_shape=(
            jax.ShapeDtypeStruct((half, chunk, columns), BF),
            jax.ShapeDtypeStruct(small.shape, F32),
            jax.ShapeDtypeStruct((half * chunk + 16, columns), BF),
        ),
        compiler_params=params(),
        cost_estimate=cost(0.4),
        name="late_fold",
    )(keep, small, *far)


def finish_kernel(keep_ref, small_ref, far_ref, qkv_hbm, *refs):
    sums, (qkv_ref, sems) = refs[:-2], refs[-2:]
    total, small = late_sums(keep_ref, small_ref, (far_ref,))
    total = total[0]
    local = qkv_ref.shape[2]
    for j in range(3):
        qkv_ref[j] = total[:, j * local : (j + 1) * local]
    copies = fetch(((qkv_ref, qkv_hbm),), sems)
    vector = sums[0].shape[0]
    per_row = small.shape[1] // vector
    spot = 0
    for ref in sums:
        for start in range(0, ref.shape[0], vector):
            row, column = spot // per_row, spot % per_row * vector
            ref[start : start + vector] = small[row, column : column + vector]
            spot += 1
    for copy in copies:
        copy.wait()


def finish(keep, small, far, local, lengths):
    chunk = keep.shape[1]
    return pl.pallas_call(
        finish_kernel,
        in_specs=[VM] * 3,
        out_specs=[HBM] + [VM] * len(lengths),
        out_shape=(
            pltpu.HBM((3, chunk, local), F32),
            *(jax.ShapeDtypeStruct((length,), F32) for length in lengths),
        ),
        scratch_shapes=[pltpu.VMEM((3, chunk, local), F32), pltpu.SemaphoreType.DMA((1,))],
        compiler_params=params(),
        cost_estimate=cost(0.75),
        name="finish",
    )(keep, small, far)


def halves_kernel(keep_ref, far_ref, wout_hbm, proj_hbm, wout_ref, proj_ref, sems):
    total = (keep_ref[...].astype(F32) + far_ref[...].astype(F32))[0]
    local = wout_ref.shape[1]
    wout_ref[...] = total[:, :local]
    proj_ref[...] = total[:, local:]
    copies = fetch(((wout_ref, wout_hbm), (proj_ref, proj_hbm)), sems)
    for copy in copies:
        copy.wait()


def make_halves(keep, far, local, proj):
    chunk = keep.shape[1]
    return pl.pallas_call(
        halves_kernel,
        in_specs=[VM] * 2,
        out_specs=[HBM] * 2,
        out_shape=(pltpu.HBM((chunk, local), F32), pltpu.HBM((chunk, proj), F32)),
        scratch_shapes=[
            pltpu.VMEM((chunk, local), F32),
            pltpu.VMEM((chunk, proj), F32),
            pltpu.SemaphoreType.DMA((2,)),
        ],
        compiler_params=params(),
        cost_estimate=cost(0.4),
        name="halves",
    )(keep, far)


def dense_kernel(keep_ref, far_ref, zero_ref, divisor_ref, out_ref):
    genes = out_ref.shape[0]
    total = (keep_ref[...].astype(F32) + far_ref[...].astype(F32))[0]
    out_ref[...] = (zero_ref[...].astype(F32) + total[:genes]) / divisor_ref[...]


def make_dense(keep, far, zero_embed, divisor):
    return pl.pallas_call(
        dense_kernel,
        in_specs=[VM] * 4,
        out_shape=jax.ShapeDtypeStruct(zero_embed.shape, F32),
        compiler_params=params(),
        cost_estimate=cost(0.7),
        name="dense",
    )(keep, far, zero_embed, divisor)
ORDERS = {
    "dense": ("xzwy", "zxwy"),
    "down": ("yxwz", "xyzw"),
    "up": ("xzyw", "yxzw"),
    "A": ("wyxz", "zyxw"),
    "B": ("yxwz", "zywx"),
}
ADDS = {
    "output": [],
    "sent": [],
    "down": [],
    "feed_back": ["dense"],
    "up": [],
    "norm2": [],
    "A": [],
    "back": [],
    "B": ["swap", "down", "up", "dense", "dense", "A", "B", "down", "up", "B", "A", "down", "dense", "A", "last", "up", "down", "A", "B", "up"],
}


def dp_swap(value, bits):
    size = lax.axis_size("dp")
    pairs = [(2 * i + core, 2 * (i ^ (1 << bits[core])) + core) for i in range(size) for core in range(2)]
    return lax.ppermute(value, ("dp", "mp"), pairs)


def mp_swap(value):
    return lax.ppermute(value, "mp", [(0, 1), (1, 0)])


def slot_offsets(order):
    bits = len(order)
    return [
        sum(((s >> (bits - 1 - place)) & 1) << bit for place, bit in enumerate(order))
        for s in range(1 << bits)
    ]


def chunks_of(left, right, orders):
    offsets = [slot_offsets(order) for order in orders]
    size = len(offsets[0])
    grad = lax.dot_general(left, right, (((0,), (0,)), ((), ())), preferred_element_type=F32)
    chosen = jnp.asarray(offsets, jnp.int32)[lax.axis_index("mp")] ^ lax.axis_index("dp")
    slots = jnp.take(grad.astype(BF).reshape(size, -1, grad.shape[1]), chosen, axis=0)
    return slots[: size // 2], slots[size // 2 :]


def tie(value, *others):
    return lax.optimization_barrier((value,) + others)[0]


class Scatter:
    def __init__(self, orders):
        self.orders = orders
        self.step = 0

    def exchange(self, value):
        self.flight = dp_swap(value, [order[self.step] for order in self.orders])

    def send(self, keep, send):
        self.keep = keep
        self.exchange(send)

    @property
    def waiting(self):
        return self.step == len(self.orders[0]) - 1

    def add(self, token):
        out = fold(tie(self.keep, token), self.flight)
        self.step += 1
        if self.step == len(self.orders[0]):
            self.result = out
            return out
        self.send(*out)
        return out[0]


class LateScatter(Scatter):
    def send(self, keep, small, *pieces):
        self.keep, self.small = keep, small
        bits = [order[self.step] for order in self.orders]
        self.flight = [dp_swap(piece, bits) for piece in pieces]

    def add(self, token):
        self.step += 1
        self.send(*late_fold(tie(self.keep, token), self.small, self.flight))
        return self.keep


class Total:
    def __init__(self, bits):
        self.bits = list(range(bits))

    def send(self, value):
        self.result = value
        if self.bits:
            bit = self.bits.pop()
            self.flight = dp_swap(value, [bit, bit])

    def add(self, token):
        self.send(tie(self.result, token) + self.flight)
        return self.result


def scatter_plan(bits):
    if bits == 4:
        orders, adds = ORDERS, ADDS
        return {name: [["xyzw".index(axis) for axis in one] for one in pair] for name, pair in orders.items()}, adds
    one = list(range(bits))
    adds = {name: [] for name in ADDS}
    adds["B"] = ["swap", "last"] + [name for _ in one for name in list(ORDERS) + ["small"]]
    return {name: [one, one[1:-1] + [0, bits - 1]] for name in ORDERS}, adds


def per_device(
    tokens,
    cell_ids,
    gene_range,
    gene_offset,
    gain1,
    shift1,
    w_qkv,
    w_out,
    out_bias,
    gain2,
    shift2,
    w_up,
    up_bias,
    w_down,
    down_bias,
    w_proj,
    zero_embed,
    dense_cot,
):
    owners = lax.axis_size("dp")
    bits = owners.bit_length() - 1
    divisor = None
    place = jnp.stack([lax.axis_index("dp"), lax.axis_index("mp")])
    genes = zero_embed.shape[0]
    orders, adds = scatter_plan(bits)
    parts = {name: Scatter(pair) for name, pair in orders.items()}
    riding = tokens.shape[1] // owners % 16 == 0
    if riding:
        parts["B"] = LateScatter(orders["B"])
    else:
        parts["small"] = Total(bits)
    gene_range, gene_offset = gene_range.reshape(1, -1), gene_offset.reshape(1, -1)

    finals = {}
    local = w_out.shape[0]

    def service(event, token):
        for name in adds[event]:
            if name == "swap":
                finals["other"] = mp_swap(tie(finals["part"], token))
                continue
            if name == "last":
                token = finals["tokens"] = make_last(tokens, tie(finals["part"], token), finals["other"], grad_middle, gain1)
                continue
            part = parts[name]
            if name == "A" and part.waiting:
                part.result = make_halves(tie(part.keep, token), part.flight, local, w_proj.shape[1])
                token = part.result[0]
            elif name == "dense" and part.waiting:
                part.result = make_dense(tie(part.keep, token), part.flight, zero_embed, divisor)
                token = part.result
            else:
                token = part.add(token)
        return token

    spread = list(range(bits))[::-1]
    gather = [spread, spread[:1] + spread[-1:] + spread[1:-1]]
    payload, tokens, w_near = make_payload(gene_range, gene_offset, dense_cot, tokens, w_qkv, owners)
    payload = payload[None]
    steps = [[order[step] for order in gather] for step in range(bits)]
    far = dp_swap(payload, steps[0])
    out_other = mp_swap(w_out)
    proj_other = mp_swap(w_proj)
    normed1, q, k, v = make_qkv(tokens, gain1, shift1, w_near)
    *mixed, lse, q, k, v, normed1 = make_attend(cell_ids, q, k, v, normed1)
    mixed_other = [mp_swap(half) for half in mixed]
    held = join(payload, tie(far, lse))
    for step in range(1, bits - 2):
        far = dp_swap(held, steps[step])
        if step < bits - 3:
            held = join(held, far)
    middle, normed2 = make_middle(
        tie(tokens, held), mixed, mixed_other, w_out, out_other, out_bias, gain2, shift2
    )
    turned2 = make_turned(place, normed2, orders["up"])
    turned1 = make_turned(place, normed1, orders["B"])
    held = join(held, tie(far, turned2, turned1))
    far = dp_swap(held, steps[-2])
    far_first = dp_swap(held, steps[-1])
    *feed_part, act, slope, middle = make_feed(tie(normed2, held), middle, w_up, up_bias, w_down)
    feed_other = [mp_swap(half) for half in feed_part]
    far, far_first = lax.optimization_barrier((far, far_first, act))[:2]
    far_second = dp_swap(far, steps[-1])
    dense_part = parts["dense"]
    block_out, dense_keep, dense_send = make_output(
        place, gene_range, gene_offset, down_bias, middle, feed_part, feed_other, w_proj, dense_part.orders, genes
    )
    dense_part.send(dense_keep, dense_send)
    token = service("output", block_out)
    grad_sent, grad_zero, divisor = make_sent(
        place, gene_range, gene_offset, (held, far, far_first, tie(far_second, token)), genes, gather
    )
    sent_other = mp_swap(grad_sent)
    token = service("sent", grad_sent)
    grad_result, grad_down_bias, down = make_result(
        place, tie(grad_sent, token), sent_other, w_proj, proj_other, act, parts["down"].orders
    )
    parts["down"].send(*down)
    token = service("down", down[0])
    grad_hidden, part2, *halves, grad_up_bias = make_feed_back(tie(grad_result, token), slope, w_down, w_up)
    other2 = [mp_swap(half) for half in halves]
    token = service("feed_back", part2)
    up = make_turned_weight(place, turned2, tie(grad_hidden, token), orders["up"])
    parts["up"].send(*up)
    token = service("up", up[0])
    grad_middle, low, grad_gain2, grad_shift2, grad_out_bias = make_norm2(
        grad_result, tie(part2, token), other2, middle, gain2
    )
    token = service("norm2", low)
    parts["A"].send(*make_weight(place, [(tie(low, token), mixed), (block_out, (grad_sent,))], orders["A"]))
    token = service("A", parts["A"].keep)
    gq, gk, gv, part1, sums1 = make_back(cell_ids, tie(low, token), tokens, w_out, q, k, v, lse, w_qkv)
    sums_other = mp_swap(sums1)
    finals["part"] = part1
    token = service("back", gq)
    sums = [grad_out_bias, grad_gain2, grad_shift2, grad_down_bias, grad_up_bias]
    pairs = [(turned1, (tie(gq, token), gk, gv))]
    last = parts["B"]
    lengths = [item.shape[-1] for item in (sums1, sums1, *sums)]
    if riding:
        last.send(*make_tail(place, pairs, sums1, sums_other, sums, orders["B"]))
        token = service("B", last.keep)
        share_qkv, *small_sums = finish(tie(last.keep, token), last.small, last.flight[0], local, lengths)
    else:
        last.send(*make_weight(place, pairs, orders["B"]))
        sums1 = sums1 + sums_other
        parts["small"].send(jnp.concatenate([sums1[:1], sums1[1:]] + sums, 1))
        token = service("B", last.keep)
        share_qkv = jnp.stack([last.result[:, j * local : (j + 1) * local] for j in range(3)])
        small_sums, at = [], 0
        for length in lengths:
            small_sums.append(parts["small"].result[0, at : at + length])
            at += length
    share_wout, share_proj = parts["A"].result
    small_sums = small_sums[:5] + [small_sums[6], small_sums[5]]
    share_up, share_down, dense = parts["up"].result, parts["down"].result, dense_part.result
    return (
        block_out,
        dense,
        finals["tokens"],
        grad_zero,
        share_qkv,
        share_wout.T,
        share_up,
        share_down.T,
        share_proj,
    ) + tuple(small_sums)


def solution(mesh):
    in_specs = (
        P("dp", None),
        P("dp", None),
        P("dp", None),
        P("dp"),
        P(),
        P(),
        P(None, None, "mp"),
        P("mp", None),
        P(),
        P(),
        P(),
        P(None, "mp"),
        P("mp"),
        P("mp", None),
        P(),
        P(None, "mp"),
        P("dp", "mp"),
        P("dp", "mp"),
    )
    out_specs = (
        P("dp", None),
        P("dp", "mp"),
        P("dp", None),
        P("dp", "mp"),
        P(None, "dp", "mp"),
        P("mp", "dp"),
        P("dp", "mp"),
        P("mp", "dp"),
        P("dp", "mp"),
        P(),
        P(),
        P(),
        P(),
        P(),
        P("mp"),
        P(),
    )
    return jax.shard_map(
        per_device, mesh=mesh, in_specs=in_specs, out_specs=out_specs, check_vma=False
    )
```
